128 devices in a mesh: tm: 4 (over z_lo, core), py: 4 (over y), pz: 8 (over z_hi, x).
Axes of the slice: x: 4, y: 4, z: 4 (z_hi: 2, z_lo: 2; z = z_hi * 2 + z_lo), core: 2. Of those that a mesh axis runs over, the one named last changes fastest.
Arguments:
- fine_state: float32 [4, 3, 2, 16, 32, 3, 1, 1024], P('tm', None, None, None, ('py', 'pz')), may hold values from -12 to 12
- fine_terms: float32 [4, 3, 2, 16, 32, 3, 1, 1024], P('tm', None, None, None, ('py', 'pz')), may hold values from -12 to 12
Outputs:
- fine_nodes: float32 [4, 2, 2, 16, 32, 3, 1, 1024], P('tm', None, None, None, ('py', 'pz'))
- fine_term: float32 [4, 2, 16, 32, 3, 1, 1024], P('tm', None, None, ('py', 'pz'))
- coarse_nodes: float32 [4, 2, 2, 8, 32, 3, 1, 512], P('tm', None, None, None, ('py', 'pz'))
The draws below stay inside these ranges and needn't reach their ends.
All inputs are finite; a program needn't handle non-finite values.
Results may differ from the reference program's by a relative error of at most 0.0003.
Values sent between devices are 32-bit elements; how exact they have to be, the bound alone decides.
A program may use at most 192 MiB of HBM per device.

```python
import math
import jax
import jax.numpy as jnp
from jax import lax

EDGE = 1024
MEMBERS = 1
NODES = 3
STEPS = 4
GROUP = 32
KXH = 16


def signed_modes(count):
    positions = jnp.arange(count)
    return jnp.where(positions < count // 2, positions, positions - count).astype(jnp.float32)


def solenoidal(raw, boost):
    mode_x = jnp.arange(KXH * GROUP).astype(jnp.float32).reshape(KXH, GROUP)
    wave_x = (2.0 * math.pi / EDGE * mode_x)[:, :, None, None]
    wave_y = 2.0 * math.pi / EDGE * signed_modes(EDGE)
    wave_sq = wave_x * wave_x + wave_y * wave_y
    wave_safe = jnp.where(wave_sq > 0, wave_sq, 1.0)
    lifted = raw * (1.0 + boost * jnp.exp(-40.0 * wave_sq))[None, None, None, :, :, None]
    comp_x = lifted[:, :, :, :, :, 0]
    comp_y = lifted[:, :, :, :, :, 1]
    comp_z = lifted[:, :, :, :, :, 2]
    along = (wave_x * comp_x + wave_y * comp_y) / wave_safe
    return jnp.stack([comp_x - wave_x * along, comp_y - wave_y * along, comp_z], axis=5)


def draw_fine_state(key, part):
    key = jax.random.fold_in(key, 11)
    dimensions = (STEPS, NODES, 2, KXH, GROUP, 3, MEMBERS, EDGE)
    raw = jax.random.truncated_normal(key, -4.0, 4.0, dimensions, jnp.float32)
    return solenoidal(raw, 0.0)


def draw_fine_terms(key, part):
    key = jax.random.fold_in(key, 12)
    dimensions = (STEPS, NODES, 2, KXH, GROUP, 3, MEMBERS, EDGE)
    raw = jax.random.truncated_normal(key, -4.0, 4.0, dimensions, jnp.float32)
    return solenoidal(raw, 0.0)


def setup_inputs(seed: int = 0) -> dict:
    streams_of = jax.random.split(jax.random.key(seed), 3)
    return {
        "fine_state": draw_fine_state(jax.random.fold_in(streams_of[2], 71), 0),
        "fine_terms": draw_fine_terms(jax.random.fold_in(streams_of[2], 71), 0),
    }


VISCOSITY = 0.5
TIME_STEP = 0.2
WEIGHTS = ((5.0 / 24.0, 1.0 / 3.0, -1.0 / 24.0), (-1.0 / 24.0, 1.0 / 3.0, 5.0 / 24.0))


def signed(count):
    positions = jnp.arange(count)
    return jnp.where(positions < count // 2, positions, positions - count).astype(jnp.float32)


def level_of(extent):
    mode_x = jnp.arange(extent // 2).astype(jnp.float32)
    mode_y = signed(extent)
    wave_x = (2.0 * math.pi / EDGE * mode_x)[:, None, None]
    wave_y = (2.0 * math.pi / EDGE * mode_y)[None, None, :]
    wave_sq = wave_x * wave_x + wave_y * wave_y
    kept = (jnp.abs(mode_x)[:, None, None] <= extent // 3) & (jnp.abs(mode_y)[None, None, :] <= extent // 3)
    anchor = (mode_x[:, None, None] == 0) & (mode_y[None, None, :] == 0)
    dealias = jnp.where(kept & ~anchor, 1.0, 0.0).astype(jnp.float32)
    wave_safe = jnp.where(anchor, jnp.float32(1.0), wave_sq).astype(jnp.float32)
    return {"wave_x": wave_x, "wave_y": wave_y, "wave_sq": wave_sq, "dealias": dealias, "wave_safe": wave_safe, "extent": extent}


def to_space(spectrum, extent):
    mixed = jnp.fft.ifft(spectrum, axis=-1, norm="ortho")
    mixed = jnp.moveaxis(mixed, 1, -1)
    mixed = jnp.pad(mixed, [(0, 0), (0, 0), (0, 0), (0, 1)])
    return jnp.fft.irfft(mixed, n=extent, axis=-1, norm="ortho")


def to_spectrum(physical, extent):
    spectral = jnp.fft.rfft(physical, axis=-1, norm="ortho")[..., : extent // 2]
    spectral = jnp.moveaxis(spectral, -1, 1)
    return jnp.fft.fft(spectral, axis=-1, norm="ortho")


def nonlinear(spectrum, level_data):
    wave_x, wave_y = level_data["wave_x"], level_data["wave_y"]
    comp_x, comp_y, comp_z = spectrum[0], spectrum[1], spectrum[2]
    vorticity = 1j * jnp.stack([wave_y * comp_z, -wave_x * comp_z, wave_x * comp_y - wave_y * comp_x])
    physical = to_space(jnp.concatenate([spectrum, vorticity]), level_data["extent"])
    velocity, spin = physical[:3], physical[3:]
    crossed = jnp.stack([velocity[1] * spin[2] - velocity[2] * spin[1], velocity[2] * spin[0] - velocity[0] * spin[2], velocity[0] * spin[1] - velocity[1] * spin[0]])
    spectral = to_spectrum(crossed, level_data["extent"]) * level_data["dealias"]
    along_k = wave_x * spectral[0] + wave_y * spectral[1]
    ratio = along_k / level_data["wave_safe"]
    return jnp.stack([spectral[0] - wave_x * ratio, spectral[1] - wave_y * ratio, spectral[2]])


def restrict(values):
    extent = values.shape[-1]
    quarter = extent // 4
    lower_x = values[..., : values.shape[-3] // 2, :, :]
    return 0.5 * jnp.concatenate([lower_x[..., :quarter], lower_x[..., extent - quarter:]], axis=-1)


def interpolate(values):
    quarter = values.shape[-1] // 2
    middle = jnp.zeros(values.shape[:-1] + (2 * quarter,), values.dtype)
    widened = jnp.concatenate([values[..., :quarter], middle, values[..., quarter:]], axis=-1)
    padding = [(0, 0)] * (widened.ndim - 3) + [(0, values.shape[-3]), (0, 0), (0, 0)]
    return 2.0 * jnp.pad(widened, padding)


def node_sweep(old, old_terms, start_value, start_term, wave_sq, evaluate):
    half_step = 0.5 * TIME_STEP
    divisor = 1.0 + half_step * VISCOSITY * wave_sq
    slopes = [old_terms[node] - VISCOSITY * wave_sq * old[node] for node in range(3)]
    section_one = start_value + half_step * (VISCOSITY * wave_sq * old[1] + start_term - old_terms[0])
    section_one = section_one + TIME_STEP * (WEIGHTS[0][0] * slopes[0] + WEIGHTS[0][1] * slopes[1] + WEIGHTS[0][2] * slopes[2])
    node_one = section_one / divisor
    term_one = evaluate(node_one)
    section_two = node_one + half_step * (VISCOSITY * wave_sq * old[2] + term_one - old_terms[1])
    section_two = section_two + TIME_STEP * (WEIGHTS[1][0] * slopes[0] + WEIGHTS[1][1] * slopes[1] + WEIGHTS[1][2] * slopes[2])
    return node_one, term_one, section_two / divisor


def to_complex(packed):
    shape_in = packed.shape
    real_part = packed[:, :, 0].reshape(shape_in[0], shape_in[1], shape_in[3] * shape_in[4], shape_in[5], shape_in[6], shape_in[7])
    imag_part = packed[:, :, 1].reshape(shape_in[0], shape_in[1], shape_in[3] * shape_in[4], shape_in[5], shape_in[6], shape_in[7])
    return lax.complex(jnp.moveaxis(real_part, 2, 3), jnp.moveaxis(imag_part, 2, 3))


def packed_form(values):
    real_part = jnp.moveaxis(jnp.real(values), -3, -4)
    imag_part = jnp.moveaxis(jnp.imag(values), -3, -4)
    shape_out = real_part.shape[:-4] + (real_part.shape[-4] // GROUP, GROUP) + real_part.shape[-3:]
    return jnp.stack([real_part.reshape(shape_out), imag_part.reshape(shape_out)], axis=-6)


def reference(fine_state, fine_terms):
    states = to_complex(fine_state)
    terms = to_complex(fine_terms)
    fine_level = level_of(EDGE)
    coarse_level = level_of(EDGE // 2)

    def fine_eval(values):
        return nonlinear(values, fine_level)

    def coarse_eval(values):
        return nonlinear(values, coarse_level)

    begin = restrict(states[0, 0])
    fine_list, term_list, coarse_list = [], [], []
    for time_rank in range(STEPS):
        old = [states[time_rank, node] for node in range(3)]
        old_terms = [terms[time_rank, node] for node in range(3)]
        coarse_old = [restrict(entry_value) for entry_value in old]
        coarse_terms = [restrict(entry_value) for entry_value in old_terms]
        coarse_one, unused, coarse_two = node_sweep(coarse_old, coarse_terms, begin, coarse_eval(begin), coarse_level["wave_sq"], coarse_eval)
        coarse_new = [begin, coarse_one, coarse_two]
        corrected = [old[node] + interpolate(coarse_new[node] - coarse_old[node]) for node in range(3)]
        if time_rank == 0:
            start_value, start_term = old[0], old_terms[0]
        else:
            start_value, start_term = states[time_rank - 1, 2], terms[time_rank - 1, 2]
        fine_one, term_one, fine_two = node_sweep(corrected, old_terms, start_value, start_term, fine_level["wave_sq"], fine_eval)
        fine_list.append(jnp.stack([fine_one, fine_two]))
        term_list.append(term_one)
        coarse_list.append(jnp.stack([coarse_one, coarse_two]))
        begin = coarse_two
    return (packed_form(jnp.stack(fine_list)), packed_form(jnp.stack(term_list)), packed_form(jnp.stack(coarse_list)))
```

```python
import math

import jax
import jax.numpy as jnp
import ml_dtypes
import numpy as np
from jax import lax
from jax.experimental import pallas as pl
from jax.experimental.pallas import tpu as pltpu
from jax.sharding import PartitionSpec as P

EDGE = 1024
VISCOSITY = 0.5
TIME_STEP = 0.2
HALF_STEP = 0.5 * TIME_STEP
WEIGHTS = ((5.0 / 24.0, 1.0 / 3.0, -1.0 / 24.0), (-1.0 / 24.0, 1.0 / 3.0, 5.0 / 24.0))
UNIT = 2.0 * math.pi / EDGE
GROUP = 32
ROWS = 256
LANES = 128
F32 = jnp.float32
BF16 = jnp.bfloat16
MESH = pl.DeviceIdType.MESH
TERM_ONE = [TIME_STEP * w for w in WEIGHTS[0]]
TERM_ONE[0] -= HALF_STEP
TERM_TWO = [TIME_STEP * w for w in WEIGHTS[1]]
TERM_TWO[1] -= HALF_STEP
STATE_ONE = [-TIME_STEP * w for w in WEIGHTS[0]]
STATE_ONE[1] += HALF_STEP
STATE_TWO = [-TIME_STEP * w for w in WEIGHTS[1]]
STATE_TWO[2] += HALF_STEP


def halves(table):
    high = table.astype(ml_dtypes.bfloat16)
    low = (table - high.astype(np.float64)).astype(ml_dtypes.bfloat16)
    return high, low


def lane_circle(extent):
    inner = extent // GROUP
    modes = inner // 2
    pairs = 64 // modes
    fore = np.zeros((2, pairs, modes, 2, pairs, inner))
    back = np.zeros((2, pairs, inner, 2, pairs, modes))
    phase = 2.0 * math.pi * np.outer(np.arange(modes), np.arange(inner)) / inner
    kept = (np.arange(modes) * GROUP <= extent // 3)[None, :]
    for pair in range(pairs):
        cosine, sine = 2.0 / extent * np.cos(phase), 2.0 / extent * np.sin(phase)
        fore[0, pair, :, 0, pair] = cosine
        fore[1, pair, :, 0, pair] = -sine
        fore[0, pair, :, 1, pair] = sine
        fore[1, pair, :, 1, pair] = cosine
        target = pair
        sources = [(pair, pair)]
        if extent < EDGE:
            slot, rest = divmod(pair, 2)
            sources = [(((1, 2, 0, 1)[slot]) * 2 + rest, pair)]
        for source, target in sources:
            cosine = 1.0 / extent * np.cos(phase).T * kept
            sine = 1.0 / extent * np.sin(phase).T * kept
            back[0, source, :, 0, target] = cosine
            back[1, source, :, 0, target] = sine
            back[0, source, :, 1, target] = -sine
            back[1, source, :, 1, target] = cosine
    fore = fore.reshape(128, 256)
    back = back.reshape(256, 128)
    return fore, back


def constant_tables():
    index = np.arange(ROWS)
    phase = 2.0 * math.pi * np.outer(index, index) / ROWS
    along_y = np.concatenate([np.cos(phase), np.sin(phase)], axis=1)
    small = 2.0 * math.pi * np.outer(np.arange(GROUP), np.arange(GROUP)) / GROUP
    eye = np.eye(8)
    along_x = np.concatenate([np.kron(np.cos(small), eye), -np.kron(np.sin(small), eye)], axis=1)
    along_y_high, along_y_low = halves(along_y)
    along_x_high, along_x_low = halves(along_x)
    out = [along_y_high, along_y_low, along_x_high, along_x_low]
    out += [np.ascontiguousarray(along_x_high.T), np.ascontiguousarray(along_x_low.T)]
    lane = np.arange(LANES)
    for extent in (EDGE // 2, EDGE):
        fore, back = lane_circle(extent)
        fore_high, fore_low = halves(fore)
        back_high, back_low = halves(back)
        out += [np.concatenate([fore_high, fore_high], axis=0), fore_low]
        out += [np.concatenate([back_high, back_low], axis=1)]
        inner = extent // GROUP
        turn = 2.0 * math.pi * np.outer(index // 8, lane % inner) / extent
        out += [np.cos(turn).astype(np.float32), np.sin(turn).astype(np.float32)]
        if extent < EDGE:
            offset = (lane % 16) // 8
        else:
            offset = np.array([0, 2, 1, 3])[(lane % 64) // 16]
        turn = 2.0 * math.pi * np.outer(index, offset) / extent
        out += [np.cos(turn).astype(np.float32), np.sin(turn).astype(np.float32)]
    return out


def split(value):
    high = value.astype(BF16)
    return high, (value - high.astype(F32)).astype(BF16)


def dot(left, right):
    return jnp.dot(left, right, preferred_element_type=F32)


def roll(value, shift):
    return pltpu.roll(value, shift % LANES, axis=1)


def lanes_like(value):
    return lax.broadcasted_iota(jnp.int32, value.shape, 1)


def swap(value, distance):
    bit = (lanes_like(value) // distance) % 2
    return jnp.where(bit == 1, roll(value, distance), roll(value, -distance))


def butterfly(value, distance):
    bit = (lanes_like(value) // distance) % 2
    return jnp.where(bit == 1, -value, value) + swap(value, distance)


def turned(value):
    other = roll(value, 64)
    return jnp.where(lanes_like(value) < 64, -other, other)


def tile(index):
    return pl.ds(index * LANES, LANES)


def chunks(size):
    return [pl.ds(start, size) for start in range(0, ROWS, size)]


def iterate(
    state_ref, terms_ref,
    y_high, y_low, x_high, x_low, xt_high, xt_low,
    fore_high_c, fore_low_c, back_c, turn_xc_c, turn_xs_c, turn_yc_c, turn_ys_c,
    fore_high_f, fore_low_f, back_f, turn_xc_f, turn_xs_f, turn_yc_f, turn_ys_f,
    nodes_out, term_out, coarse_out,
    rhs_high, rhs_low, grid_buf, cross_high, cross_low,
    fore_send, fore_recv, back_send, back_recv, hand_send, hand_recv,
    fine_send, fine_recv, fine_back_send, fine_back_recv, start_send, start_recv,
    right_one, right_two, mix_one, mix_two,
    curl_one, curl_two, keep_same, keep_cross, damp_c, cos_c, sin_c,
    pre_one, pre_two, old_one, old_two, begin, node_c,
    ky_f, damp_f, stiff_f, cos_f, sin_f, same_x, same_y, cross_f, mask_f,
    right_one_f, right_two_f, node_f,
    fore_sent, fore_got, back_sent, back_got, hand_sems, fine_sems, start_sems,
):
    rank = lax.axis_index("tm")
    place = lax.axis_index("py") * 8 + lax.axis_index("pz")

    def device(time_rank, position):
        return (time_rank, position // 8, position % 8)

    barrier = pltpu.get_barrier_semaphore()

    @pl.when(rank > 0)
    def _():
        def greet_back(step, carry):
            pl.semaphore_signal(
                barrier, inc=1, device_id=device(rank - 1, (place + step) % GROUP), device_id_type=MESH
            )
            return carry

        lax.fori_loop(0, GROUP, greet_back, 0)

    def greet(step, carry):
        pl.semaphore_signal(
            barrier, inc=1, device_id=device(rank, (place + step) % GROUP), device_id_type=MESH
        )
        return carry

    lax.fori_loop(1, GROUP, greet, 0)

    def block(position):
        return pl.ds(pl.multiple_of(position * 8, 8), 8)

    def post(source, target, sent, got, time_rank, first):
        def one(step, carry):
            position = (place + step) % GROUP
            pltpu.make_async_remote_copy(
                src_ref=source.at[block(position)],
                dst_ref=target.at[block(place)],
                send_sem=sent,
                recv_sem=got,
                device_id=device(time_rank, position),
                device_id_type=MESH,
            ).start()
            return carry

        if first == 1:
            pltpu.make_async_copy(source.at[block(place)], target.at[block(place)], got).start()
        lax.fori_loop(first, GROUP, one, 0)

    def receive(target, got):
        pltpu.make_async_copy(target, target, got).wait()

    def drain(source, sent, first):
        part = source.at[pl.ds(0, (GROUP - first) * 8)]
        pltpu.make_async_copy(part, part, sent).wait()

    place_f32 = place.astype(F32)
    row = lax.broadcasted_iota(jnp.int32, (ROWS, LANES), 0)
    lane = lax.broadcasted_iota(jnp.int32, (ROWS, LANES), 1)

    def wave_tables(extent, mode_x, mode_y):
        wave_x, wave_y = UNIT * mode_x, UNIT * mode_y
        wave_sq = wave_x * wave_x + wave_y * wave_y
        anchor = (mode_x == 0) & (mode_y == 0)
        kept = (mode_x <= extent // 3) & (jnp.abs(mode_y) <= extent // 3) & ~anchor
        mask = jnp.where(kept, 1.0, 0.0).astype(F32)
        inverse = mask / jnp.where(anchor, 1.0, wave_sq)
        damp = 1.0 / (1.0 + HALF_STEP * VISCOSITY * wave_sq)
        return wave_x, wave_y, wave_sq, mask, inverse, damp

    slot = (lane % 64) // 16
    mode_x = (lane % 8).astype(F32) * GROUP + place_f32
    mode_y = (row - 256 * ((lane % 16) // 8)).astype(F32)
    wave_x, wave_y, wave_sq, mask, inverse, damp = wave_tables(EDGE // 2, mode_x, mode_y)
    curl_one[...] = jnp.where(slot == 1, -wave_x, jnp.where(slot == 2, wave_x, wave_y))
    curl_two[...] = jnp.where(slot == 2, -wave_y, 0.0)
    same = jnp.where(slot == 2, mask, jnp.where(slot == 1, wave_x * wave_x, wave_y * wave_y) * inverse)
    keep_same[...] = same * (HALF_STEP * damp)
    keep_cross[...] = jnp.where(slot == 2, 0.0, -wave_x * wave_y * inverse) * (HALF_STEP * damp)
    damp_c[...] = damp
    weight = jnp.where(mode_x == 0, 0.5, 1.0)
    cos_c[...] = turn_yc_c[...] * weight
    sin_c[...] = turn_ys_c[...] * weight

    def coarse_tile(ref, base, scale, target):
        for half in range(2):
            pieces = []
            for part in range(2):
                for component in (0, 1, 2, 0):
                    for quarter in (0, 3):
                        start = base + part * 384 + component * 8 + 2 * quarter + half
                        pieces.append(ref[pl.ds(start, 8, stride=24), :])
            target[pl.ds(half * 128, 128), :] = scale * jnp.concatenate(pieces, axis=0).T

    def fine_tile(ref, component, target):
        for half in range(2):
            pieces = []
            for part in range(2):
                for quarter in range(4):
                    start = part * 384 + component * 8 + 2 * quarter + half
                    pieces.append(ref[pl.ds(start, 16, stride=24), :])
            target[pl.ds(half * 128, 128), tile(component)] = jnp.concatenate(pieces, axis=0).T

    def y_product(count, target):
        for start in range(0, count * LANES, 256):
            width = min(256, count * LANES - start)
            part = pl.ds(start, width)
            high, low = rhs_high[:, part], rhs_low[:, part]
            target[:, part] = dot(y_high[...], high) + dot(y_high[...], low) + dot(y_low[...], high)

    def stack(rows, index, first, second):
        high, low = split(first)
        rhs_high[rows, tile(index)] = high
        rhs_low[rows, tile(index)] = low
        high, low = split(second)
        lower = pl.ds(rows.start + ROWS, rows.size)
        rhs_high[lower, tile(index)] = high
        rhs_low[lower, tile(index)] = low

    def spread_coarse(source, target):
        for rows in chunks(64):
            velocity = source[rows, :]
            rotated = turned(velocity)
            back_two, back_one, ahead = roll(rotated, -32), roll(rotated, -16), roll(rotated, 16)
            position = (lanes_like(velocity) % 64) // 16
            chosen = jnp.where(position == 0, back_two, jnp.where(position == 1, back_one, ahead))
            vorticity = curl_one[rows, :] * chosen + curl_two[rows, :] * back_one
            for index, field in enumerate((velocity, vorticity)):
                mixed = butterfly(field, 8)
                mixed_turned = turned(mixed)
                cosine, sine = cos_c[rows, :], sin_c[rows, :]
                stack(
                    rows,
                    index,
                    mixed * cosine + mixed_turned * sine,
                    mixed_turned * cosine - mixed * sine,
                )
        y_product(2, target)

    def grid_stage(source, count, target, fore_high, fore_low, back, cosine_ref, sine_ref):
        cosine, sine = cosine_ref[...], sine_ref[...]
        every = pl.ds(0, ROWS)
        for index in range(count):
            high, low = split(source[:, tile(index)])
            inner = dot(jnp.concatenate([high, low], axis=1), fore_high[...]) + dot(high, fore_low[...])
            real, imag = inner[:, :LANES], inner[:, LANES:]
            stack(every, index, real * cosine - imag * sine, real * sine + imag * cosine)
        for start in range(0, count * LANES, 256):
            part = pl.ds(start, 256)
            high, low = rhs_high[:, part], rhs_low[:, part]
            grid_buf[:, part] = dot(x_high[...], high) + dot(x_high[...], low) + dot(x_low[...], high)
        if count == 2:
            speed, spin = grid_buf[:, tile(0)], grid_buf[:, tile(1)]
            crossed = [speed * roll(spin, -32) - roll(speed, -32) * spin]
        else:
            fields = [grid_buf[:, tile(index)] for index in range(6)]
            crossed = [
                fields[1] * fields[5] - fields[2] * fields[4],
                fields[2] * fields[3] - fields[0] * fields[5],
                fields[0] * fields[4] - fields[1] * fields[3],
            ]
        for index, value in enumerate(crossed):
            high, low = split(value)
            both = dot(xt_high[...], jnp.concatenate([high, low], axis=1))
            outer = both[:, :LANES] + both[:, LANES:] + dot(xt_low[...], high)
            real, imag = outer[:ROWS], outer[ROWS:]
            ready = jnp.concatenate([real * cosine + imag * sine, imag * cosine - real * sine], axis=1)
            high, low = split(ready)
            both = dot(high, back[...])
            target[:, tile(index)] = both[:, :LANES] + both[:, LANES:] + dot(low, back[:, :LANES])

    def gather_y(source, count):
        for index in range(count):
            for rows in chunks(128):
                value = source[rows, tile(index)]
                stack(rows, index, value, -turned(value))
        y_product(count, grid_buf)

    def finish_coarse(start_ref, right_ref, target):
        gather_y(back_recv.at[0] if start_ref is begin else back_recv.at[1], 1)
        for rows in chunks(128):
            value = grid_buf[rows, tile(0)]
            value = value * turn_yc_c[rows, :] - turned(value) * turn_ys_c[rows, :]
            value = butterfly(value, 8)
            position = (lanes_like(value) % 64) // 16
            partner = jnp.where(
                position == 0, roll(value, -16), jnp.where(position == 1, roll(value, 16), roll(value, 32))
            )
            term = keep_same[rows, :] * value + keep_cross[rows, :] * partner
            target[rows, :] = damp_c[rows, :] * start_ref[rows, :] + right_ref[rows, :] + term

    coarse_tile(state_ref, 0, 0.5, begin)

    @pl.when(rank == 0)
    def _():
        spread_coarse(begin, fore_send.at[0])

    @pl.when(rank < 3)
    def _():
        pl.semaphore_wait(barrier, 2 * GROUP - 1)

    @pl.when(rank == 3)
    def _():
        pl.semaphore_wait(barrier, GROUP - 1)

    @pl.when(rank == 0)
    def _():
        post(fore_send.at[0], fore_recv.at[0], fore_sent.at[0], fore_got.at[0], rank, 1)

    def combine(a, carry):
        wave_x = UNIT * (a.astype(F32) * GROUP + place_f32)
        sub = lax.broadcasted_iota(jnp.int32, (8, LANES), 0)
        mode = sub * 128 + lax.broadcasted_iota(jnp.int32, (8, LANES), 1)
        wave_y = UNIT * jnp.where(mode < EDGE // 2, mode, mode - EDGE).astype(F32)
        stiff = VISCOSITY * (wave_x * wave_x + wave_y * wave_y)
        for part in range(2):
            for component in range(3):
                base = pl.multiple_of(a * 24 + (part * 384 + component * 8), 8)
                rows = pl.ds(base, 8)
                states = [state_ref[pl.ds(base + node * 768, 8), :] for node in range(3)]
                terms = [terms_ref[pl.ds(base + node * 768, 8), :] for node in range(3)]
                one = sum(w * s for w, s in zip(STATE_ONE, states))
                two = sum(w * s for w, s in zip(STATE_TWO, states))
                mix_one[rows, :] = one
                mix_two[rows, :] = two
                right_one[rows, :] = sum(w * t for w, t in zip(TERM_ONE, terms)) + stiff * one
                right_two[rows, :] = sum(w * t for w, t in zip(TERM_TWO, terms)) + stiff * two
                start_send[rows, :] = states[2] + HALF_STEP * terms[2]
        return carry

    lax.fori_loop(0, 16, combine, 0, unroll=2)

    @pl.when(rank < 3)
    def _():
        pltpu.make_async_remote_copy(
            src_ref=start_send,
            dst_ref=start_recv,
            send_sem=start_sems.at[0],
            recv_sem=start_sems.at[1],
            device_id=device(rank + 1, place),
            device_id_type=MESH,
        ).start()

    coarse_tile(right_one, 0, 0.5, pre_one)
    pre_one[...] = pre_one[...] * damp_c[...]

    coarse_tables = (fore_high_c, fore_low_c, back_c, turn_xc_c, turn_xs_c)
    receive(fore_recv.at[0], fore_got.at[0])
    grid_stage(fore_recv.at[0], 2, back_send.at[0], *coarse_tables)
    post(back_send.at[0], back_recv.at[0], back_sent.at[0], back_got.at[0], rank, 1)

    @pl.when(rank > 0)
    def _():
        pltpu.make_async_copy(hand_recv, hand_recv, hand_sems.at[1]).wait()
        begin[...] = hand_recv[...]

    coarse_tile(right_two, 0, 0.5, pre_two)
    pre_two[...] = pre_two[...] * damp_c[...]
    receive(back_recv.at[0], back_got.at[0])
    finish_coarse(begin, pre_one, node_c)
    spread_coarse(node_c, fore_send.at[1])
    post(fore_send.at[1], fore_recv.at[1], fore_sent.at[1], fore_got.at[1], rank, 1)

    coarse_tile(mix_one, 0, 0.5, old_one)
    coarse_tile(mix_two, 0, 0.5, old_two)
    receive(fore_recv.at[1], fore_got.at[1])
    grid_stage(fore_recv.at[1], 2, back_send.at[1], *coarse_tables)
    post(back_send.at[1], back_recv.at[1], back_sent.at[1], back_got.at[1], rank, 1)

    quarter = (lane % 64) // 16
    mode_x = (lane % 16).astype(F32) * GROUP + place_f32
    mode_y = (row + 256 * quarter - jnp.where(quarter >= 2, EDGE, 0)).astype(F32)
    wave_x, wave_y, wave_sq, mask, inverse, damp = wave_tables(EDGE, mode_x, mode_y)
    ky_f[...] = wave_y
    damp_f[...] = damp
    stiff_f[...] = (2.0 * VISCOSITY) * wave_sq
    same_x[...] = wave_y * wave_y * inverse
    same_y[...] = wave_x * wave_x * inverse
    cross_f[...] = -wave_x * wave_y * inverse
    mask_f[...] = mask
    weight = jnp.where(mode_x == 0, 0.5, 1.0)
    cos_f[...] = turn_yc_f[...] * weight
    sin_f[...] = turn_ys_f[...] * weight

    receive(back_recv.at[1], back_got.at[1])
    finish_coarse(node_c, pre_two, hand_send)

    @pl.when(rank < 3)
    def _():
        spread_coarse(hand_send, fore_send.at[2])
        post(fore_send.at[2], fore_recv.at[0], fore_sent.at[2], fore_got.at[0], rank + 1, 0)
        pltpu.make_async_remote_copy(
            src_ref=hand_send,
            dst_ref=hand_recv,
            send_sem=hand_sems.at[0],
            recv_sem=hand_sems.at[1],
            device_id=device(rank + 1, place),
            device_id_type=MESH,
        ).start()

    @pl.when(rank == 0)
    def _():
        first = pl.ds(0, 768)
        right_one[...] = right_one[...] + state_ref[first, :] + HALF_STEP * terms_ref[first, :]

    @pl.when(rank > 0)
    def _():
        pltpu.make_async_copy(start_recv, start_recv, start_sems.at[1]).wait()
        right_one[...] = right_one[...] + start_recv[...]

    for component in range(3):
        fine_tile(right_one, component, right_one_f)
        fine_tile(right_two, component, right_two_f)

    for rows in chunks(64):
        news = [begin[rows, :], node_c[rows, :], hand_send[rows, :]]
        change_one = sum(w * n for w, n in zip(STATE_ONE, news)) - old_one[rows, :]
        change_two = sum(w * n for w, n in zip(STATE_TWO, news)) - old_two[rows, :]
        inner = lanes_like(change_one) % 64
        stiff, damping = stiff_f[rows, :], damp_f[rows, :]
        fields = []
        for component in range(3):

            def placed(change):
                low = jnp.where(inner < 8, roll(change, -16 * component), 0.0)
                high = roll(change, 40 - 16 * component)
                return jnp.where((inner >= 48) & (inner < 56), high, low)

            value = right_one_f[rows, tile(component)] + stiff * placed(change_one)
            value = value * damping
            node_f[rows, tile(component)] = value
            right_two_f[rows, tile(component)] = right_two_f[rows, tile(component)] + stiff * placed(change_two)
            fields.append(value)
        rotated = [turned(value) for value in fields]
        ky = ky_f[rows, :]
        kx = UNIT * ((lanes_like(ky) % 16).astype(F32) * GROUP + place_f32)
        fields += [ky * rotated[2], -kx * rotated[2], kx * rotated[1] - ky * rotated[0]]
        position = (lanes_like(ky) % 64) // 16
        cosine, sine = cos_f[rows, :], sin_f[rows, :]
        for index, field in enumerate(fields):
            mixed = butterfly(field, 32)
            mixed = jnp.where(position == 3, turned(mixed), mixed)
            mixed = butterfly(mixed, 16)
            mixed_turned = turned(mixed)
            stack(
                rows, index, mixed * cosine + mixed_turned * sine, mixed_turned * cosine - mixed * sine
            )
    y_product(6, fine_send)
    post(fine_send, fine_recv, fine_sems.at[0], fine_sems.at[1], rank, 1)

    def give_back(source, component, target, base):
        for half in range(2):
            block_t = source[pl.ds(half * 128, 128), tile(component)].T
            for part in range(2):
                for quarter in range(4):
                    start = base + part * 384 + component * 8 + 2 * quarter + half
                    first = (part * 4 + quarter) * 16
                    target[pl.ds(start, 16, stride=24), :] = block_t[first : first + 16]

    def give_back_coarse(source, base):
        for half in range(2):
            block_t = source[pl.ds(half * 128, 128), :].T
            for part in range(2):
                for component in range(3):
                    for quarter in range(2):
                        start = base + part * 96 + component * 4 + 2 * quarter + half
                        first = part * 64 + component * 16 + quarter * 8
                        coarse_out[pl.ds(start, 8, stride=12), :] = block_t[first : first + 8]

    give_back_coarse(node_c, 0)
    give_back_coarse(hand_send, 192)
    receive(fine_recv, fine_sems.at[1])
    grid_stage(
        fine_recv, 6, fine_back_send, fore_high_f, fore_low_f, back_f, turn_xc_f, turn_xs_f
    )
    post(fine_back_send, fine_back_recv, fine_sems.at[2], fine_sems.at[3], rank, 1)
    for component in range(3):
        give_back(node_f, component, nodes_out, 0)
    receive(fine_back_recv, fine_sems.at[3])
    gather_y(fine_back_recv, 3)
    for rows in chunks(64):
        cosine, sine = turn_yc_f[rows, :], turn_ys_f[rows, :]
        modes = []
        for component in range(3):
            value = grid_buf[rows, tile(component)]
            value = value * cosine - turned(value) * sine
            value = butterfly(value, 16)
            position = (lanes_like(value) % 64) // 16
            value = jnp.where(position == 3, -turned(value), value)
            modes.append(butterfly(value, 32))
        cross = cross_f[rows, :]
        results = [
            same_x[rows, :] * modes[0] + cross * modes[1],
            same_y[rows, :] * modes[1] + cross * modes[0],
            mask_f[rows, :] * modes[2],
        ]
        for component, value in enumerate(results):
            part = tile(component)
            right_one_f[rows, part] = value
            total = node_f[rows, part] + HALF_STEP * value + right_two_f[rows, part]
            node_f[rows, part] = total * damp_f[rows, :]
    for component in range(3):
        give_back(right_one_f, component, term_out, 0)
        give_back(node_f, component, nodes_out, 768)

    @pl.when(rank == 0)
    def _():
        drain(fore_send.at[0], fore_sent.at[0], 1)

    drain(fore_send.at[1], fore_sent.at[1], 1)
    for index in range(2):
        drain(back_send.at[index], back_sent.at[index], 1)
    drain(fine_send, fine_sems.at[0], 1)
    drain(fine_back_send, fine_sems.at[2], 1)

    @pl.when(rank < 3)
    def _():
        drain(fore_send.at[2], fore_sent.at[2], 0)
        pltpu.make_async_copy(hand_send, hand_send, hand_sems.at[0]).wait()
        pltpu.make_async_copy(start_send, start_send, start_sems.at[0]).wait()


def shards(fine_state, fine_terms):
    tables = [jnp.asarray(table) for table in constant_tables()]
    full, natural, wide = (ROWS, LANES), (768, LANES), (ROWS, 3 * LANES)
    dma = pltpu.SemaphoreType.DMA
    scratch = [
        pltpu.VMEM((2 * ROWS, 6 * LANES), BF16),
        pltpu.VMEM((2 * ROWS, 6 * LANES), BF16),
        pltpu.VMEM((ROWS, 6 * LANES), F32),
        pltpu.VMEM(wide, BF16),
        pltpu.VMEM(wide, BF16),
        pltpu.VMEM((3, ROWS, 2 * LANES), F32),
        pltpu.VMEM((2, ROWS, 2 * LANES), F32),
        pltpu.VMEM((2, ROWS, LANES), F32),
        pltpu.VMEM((2, ROWS, LANES), F32),
        pltpu.VMEM(full, F32),
        pltpu.VMEM(full, F32),
        pltpu.VMEM((ROWS, 6 * LANES), F32),
        pltpu.VMEM((ROWS, 6 * LANES), F32),
        pltpu.VMEM(wide, F32),
        pltpu.VMEM(wide, F32),
    ]
    scratch += [pltpu.VMEM(natural, F32)] * 6
    scratch += [pltpu.VMEM(full, F32)] * (7 + 6 + 9)
    scratch += [pltpu.VMEM(wide, F32)] * 3
    scratch += [dma((3,)), dma((2,)), dma((2,)), dma((2,)), dma((2,)), dma((4,)), dma((2,))]
    outs = pl.pallas_call(
        iterate,
        out_shape=(
            jax.ShapeDtypeStruct((1536, LANES), F32),
            jax.ShapeDtypeStruct((768, LANES), F32),
            jax.ShapeDtypeStruct((384, LANES), F32),
        ),
        in_specs=[pl.BlockSpec(memory_space=pltpu.VMEM)] * (2 + len(tables)),
        out_specs=[pl.BlockSpec(memory_space=pltpu.VMEM)] * 3,
        scratch_shapes=scratch,
        compiler_params=pltpu.CompilerParams(
            collective_id=0, has_side_effects=True, vmem_limit_bytes=44 * 1024 * 1024
        ),
        name="iterate",
    )(fine_state.reshape(2304, LANES), fine_terms.reshape(2304, LANES), *tables)
    return (
        outs[0].reshape(1, 2, 2, 16, 1, 3, 1, 1024),
        outs[1].reshape(1, 2, 16, 1, 3, 1, 1024),
        outs[2].reshape(1, 2, 2, 8, 1, 3, 1, 512),
    )


def solution(mesh):
    split_over = P("tm", None, None, None, ("py", "pz"), None, None, None)
    return jax.shard_map(
        shards,
        mesh=mesh,
        in_specs=(split_over, split_over),
        out_specs=(
            split_over,
            P("tm", None, None, ("py", "pz"), None, None, None),
            split_over,
        ),
        check_vma=False,
    )
```

```python
import math

import jax
import jax.numpy as jnp
import ml_dtypes
import numpy as np
from jax import lax
from jax.experimental import pallas as pl
from jax.experimental.pallas import tpu as pltpu
from jax.sharding import PartitionSpec as P

EDGE = 1024
VISCOSITY = 0.5
TIME_STEP = 0.2
HALF_STEP = 0.5 * TIME_STEP
WEIGHTS = ((5.0 / 24.0, 1.0 / 3.0, -1.0 / 24.0), (-1.0 / 24.0, 1.0 / 3.0, 5.0 / 24.0))
UNIT = 2.0 * math.pi / EDGE
GROUP = 32
ROWS = 256
LANES = 128
F32 = jnp.float32
BF16 = jnp.bfloat16
MESH = pl.DeviceIdType.MESH
TERM_ONE = [TIME_STEP * w for w in WEIGHTS[0]]
TERM_ONE[0] -= HALF_STEP
TERM_TWO = [TIME_STEP * w for w in WEIGHTS[1]]
TERM_TWO[1] -= HALF_STEP
STATE_ONE = [-TIME_STEP * w for w in WEIGHTS[0]]
STATE_ONE[1] += HALF_STEP
STATE_TWO = [-TIME_STEP * w for w in WEIGHTS[1]]
STATE_TWO[2] += HALF_STEP


def halves(table):
    high = table.astype(ml_dtypes.bfloat16)
    low = (table - high.astype(np.float64)).astype(ml_dtypes.bfloat16)
    return high, low


def lane_circle(extent):
    inner = extent // GROUP
    modes = inner // 2
    pairs = 64 // modes
    fore = np.zeros((2, pairs, modes, 2, pairs, inner))
    back = np.zeros((2, pairs, inner, 2, pairs, modes))
    phase = 2.0 * math.pi * np.outer(np.arange(modes), np.arange(inner)) / inner
    kept = (np.arange(modes) * GROUP <= extent // 3)[None, :]
    for pair in range(pairs):
        cosine, sine = 2.0 / extent * np.cos(phase), 2.0 / extent * np.sin(phase)
        fore[0, pair, :, 0, pair] = cosine
        fore[1, pair, :, 0, pair] = -sine
        fore[0, pair, :, 1, pair] = sine
        fore[1, pair, :, 1, pair] = cosine
        target = pair
        sources = [(pair, pair)]
        if extent < EDGE:
            slot, rest = divmod(pair, 2)
            sources = [(((1, 2, 0, 1)[slot]) * 2 + rest, pair)]
        for source, target in sources:
            cosine = 1.0 / extent * np.cos(phase).T * kept
            sine = 1.0 / extent * np.sin(phase).T * kept
            back[0, source, :, 0, target] = cosine
            back[1, source, :, 0, target] = sine
            back[0, source, :, 1, target] = -sine
            back[1, source, :, 1, target] = cosine
    fore = fore.reshape(128, 256)
    back = back.reshape(256, 128)
    return fore, back


def constant_tables():
    index = np.arange(ROWS)
    phase = 2.0 * math.pi * np.outer(index, index) / ROWS
    along_y = np.concatenate([np.cos(phase), np.sin(phase)], axis=1)
    small = 2.0 * math.pi * np.outer(np.arange(GROUP), np.arange(GROUP)) / GROUP
    eye = np.eye(8)
    along_x = np.concatenate([np.kron(np.cos(small), eye), -np.kron(np.sin(small), eye)], axis=1)
    matrices = list(halves(along_y)) + list(halves(along_x))
    matrices.append(np.concatenate(halves(along_x.T), axis=1))
    lane = np.arange(LANES)
    turns, inner_parts = [], []
    for extent in (EDGE // 2, EDGE):
        fore, back = lane_circle(extent)
        fore_high, fore_low = halves(fore)
        back_high, back_low = halves(back)
        inner_parts.append(
            np.concatenate([fore_high, fore_high, fore_low, np.concatenate([back_high, back_low], axis=1)], axis=0)
        )
        inner = extent // GROUP
        turn = 2.0 * math.pi * np.outer(index // 8, lane % inner) / extent
        turns += [np.cos(turn), np.sin(turn)]
        if extent < EDGE:
            offset = (lane % 16) // 8
        else:
            offset = np.array([0, 2, 1, 3])[(lane % 64) // 16]
        turn = 2.0 * math.pi * np.outer(index, offset) / extent
        turns += [np.cos(turn), np.sin(turn)]
    matrices.append(np.concatenate(inner_parts, axis=1))
    return np.concatenate(matrices, axis=0), np.concatenate(turns, axis=0).astype(np.float32)


def split(value):
    high = value.astype(BF16)
    return high, (value - high.astype(F32)).astype(BF16)


def dot(left, right):
    return jnp.dot(left, right, preferred_element_type=F32)


def roll(value, shift):
    return pltpu.roll(value, shift % LANES, axis=1)


def lanes_like(value):
    return lax.broadcasted_iota(jnp.int32, value.shape, 1)


def swap(value, distance):
    bit = (lanes_like(value) // distance) % 2
    return jnp.where(bit == 1, roll(value, distance), roll(value, -distance))


def butterfly(value, distance):
    bit = (lanes_like(value) // distance) % 2
    return jnp.where(bit == 1, -value, value) + swap(value, distance)


def turned(value):
    other = roll(value, 64)
    return jnp.where(lanes_like(value) < 64, -other, other)


def tile(index):
    return pl.ds(index * LANES, LANES)


def chunks(size):
    return [pl.ds(start, size) for start in range(0, ROWS, size)]


def iterate(
    state_hbm, terms_hbm, matrices_hbm, turns_hbm,
    nodes_out, term_out, coarse_out,
    rhs_high, rhs_low, grid_buf, cross_high, cross_low,
    fore_send, fore_recv, back_send, back_recv, hand_send, hand_recv,
    fine_send, fine_recv, fine_back_send, fine_back_recv, start_send, start_recv,
    right_one, right_two, mix_one, mix_two,
    curl_one, curl_two, keep_same, keep_cross, damp_c, cos_c, sin_c,
    pre_one, pre_two, old_one, old_two, begin, node_c,
    ky_f, damp_f, stiff_f, cos_f, sin_f, same_x, same_y, cross_f, mask_f,
    right_one_f, right_two_f, node_f,
    state_ref, terms_ref, matrices, turns,
    fore_sent, fore_got, back_sent, back_got, hand_sems, fine_sems, start_sems, load_sems,
):
    loads = []
    for source, target, start, size in (
        (state_hbm, state_ref, 0, 768),
        (matrices_hbm, matrices, 0, 512),
        (turns_hbm, turns, 0, 1024),
        (state_hbm, state_ref, 768, 1536),
        (terms_hbm, terms_ref, 0, 2304),
        (matrices_hbm, matrices, 512, 1664),
        (turns_hbm, turns, 1024, 1024),
    ):
        rows = pl.ds(start, size)
        loads.append(pltpu.make_async_copy(source.at[rows], target.at[rows], load_sems.at[len(loads)]))
        loads[-1].start()

    def matrix(start, size, first=0, width=512):
        return matrices.at[pl.ds(start, size), pl.ds(first, width)]

    y_high, y_low = matrix(0, 256), matrix(256, 256)
    x_high, x_low = matrix(512, 256), matrix(768, 256)
    xt_high, xt_low = matrix(1024, 512, 0, 256), matrix(1024, 512, 256, 256)
    fore_high_c, fore_low_c, back_c = (matrix(*rows, 0, 256) for rows in ((1536, 256), (1792, 128), (1920, 256)))
    fore_high_f, fore_low_f, back_f = (matrix(*rows, 256, 256) for rows in ((1536, 256), (1792, 128), (1920, 256)))
    turn_xc_c, turn_xs_c, turn_yc_c, turn_ys_c, turn_xc_f, turn_xs_f, turn_yc_f, turn_ys_f = (
        turns.at[pl.ds(start, ROWS), :] for start in range(0, 8 * ROWS, ROWS)
    )
    rank = lax.axis_index("tm")
    place = lax.axis_index("py") * 8 + lax.axis_index("pz")

    def device(time_rank, position):
        return (time_rank, position // 8, position % 8)

    barrier = pltpu.get_barrier_semaphore()

    @pl.when(rank > 0)
    def _():
        def greet_back(step, carry):
            pl.semaphore_signal(
                barrier, inc=1, device_id=device(rank - 1, (place + step) % GROUP), device_id_type=MESH
            )
            return carry

        lax.fori_loop(0, GROUP, greet_back, 0)

    def greet(step, carry):
        pl.semaphore_signal(
            barrier, inc=1, device_id=device(rank, (place + step) % GROUP), device_id_type=MESH
        )
        return carry

    lax.fori_loop(1, GROUP, greet, 0)

    def block(position):
        return pl.ds(pl.multiple_of(position * 8, 8), 8)

    def post(source, target, sent, got, time_rank, first):
        def one(step, carry):
            position = (place + step) % GROUP
            pltpu.make_async_remote_copy(
                src_ref=source.at[block(position)],
                dst_ref=target.at[block(place)],
                send_sem=sent,
                recv_sem=got,
                device_id=device(time_rank, position),
                device_id_type=MESH,
            ).start()
            return carry

        if first == 1:
            pltpu.make_async_copy(source.at[block(place)], target.at[block(place)], got).start()
        lax.fori_loop(first, GROUP, one, 0)

    def receive(target, got):
        pltpu.make_async_copy(target, target, got).wait()

    def drain(source, sent, first):
        part = source.at[pl.ds(0, (GROUP - first) * 8)]
        pltpu.make_async_copy(part, part, sent).wait()

    place_f32 = place.astype(F32)
    row = lax.broadcasted_iota(jnp.int32, (ROWS, LANES), 0)
    lane = lax.broadcasted_iota(jnp.int32, (ROWS, LANES), 1)

    def wave_tables(extent, mode_x, mode_y):
        wave_x, wave_y = UNIT * mode_x, UNIT * mode_y
        wave_sq = wave_x * wave_x + wave_y * wave_y
        anchor = (mode_x == 0) & (mode_y == 0)
        kept = (mode_x <= extent // 3) & (jnp.abs(mode_y) <= extent // 3) & ~anchor
        mask = jnp.where(kept, 1.0, 0.0).astype(F32)
        inverse = mask / jnp.where(anchor, 1.0, wave_sq)
        damp = 1.0 / (1.0 + HALF_STEP * VISCOSITY * wave_sq)
        return wave_x, wave_y, wave_sq, mask, inverse, damp

    loads[2].wait()
    slot = (lane % 64) // 16
    mode_x = (lane % 8).astype(F32) * GROUP + place_f32
    mode_y = (row - 256 * ((lane % 16) // 8)).astype(F32)
    wave_x, wave_y, wave_sq, mask, inverse, damp = wave_tables(EDGE // 2, mode_x, mode_y)
    curl_one[...] = jnp.where(slot == 1, -wave_x, jnp.where(slot == 2, wave_x, wave_y))
    curl_two[...] = jnp.where(slot == 2, -wave_y, 0.0)
    same = jnp.where(slot == 2, mask, jnp.where(slot == 1, wave_x * wave_x, wave_y * wave_y) * inverse)
    keep_same[...] = same * (HALF_STEP * damp)
    keep_cross[...] = jnp.where(slot == 2, 0.0, -wave_x * wave_y * inverse) * (HALF_STEP * damp)
    damp_c[...] = damp
    weight = jnp.where(mode_x == 0, 0.5, 1.0)
    cos_c[...] = turn_yc_c[...] * weight
    sin_c[...] = turn_ys_c[...] * weight

    def coarse_tile(ref, base, scale, target):
        for half in range(2):
            pieces = []
            for part in range(2):
                for component in (0, 1, 2, 0):
                    for quarter in (0, 3):
                        start = base + part * 384 + component * 8 + 2 * quarter + half
                        pieces.append(ref[pl.ds(start, 8, stride=24), :])
            target[pl.ds(half * 128, 128), :] = scale * jnp.concatenate(pieces, axis=0).T

    def fine_tile(ref, component, target):
        for half in range(2):
            pieces = []
            for part in range(2):
                for quarter in range(4):
                    start = part * 384 + component * 8 + 2 * quarter + half
                    pieces.append(ref[pl.ds(start, 16, stride=24), :])
            target[pl.ds(half * 128, 128), tile(component)] = jnp.concatenate(pieces, axis=0).T

    def y_product(count, target):
        for start in range(0, count * LANES, 256):
            width = min(256, count * LANES - start)
            part = pl.ds(start, width)
            high, low = rhs_high[:, part], rhs_low[:, part]
            target[:, part] = dot(y_high[...], high) + dot(y_high[...], low) + dot(y_low[...], high)

    def stack(rows, index, first, second):
        high, low = split(first)
        rhs_high[rows, tile(index)] = high
        rhs_low[rows, tile(index)] = low
        high, low = split(second)
        lower = pl.ds(rows.start + ROWS, rows.size)
        rhs_high[lower, tile(index)] = high
        rhs_low[lower, tile(index)] = low

    def spread_coarse(source, target):
        for rows in chunks(64):
            velocity = source[rows, :]
            rotated = turned(velocity)
            back_two, back_one, ahead = roll(rotated, -32), roll(rotated, -16), roll(rotated, 16)
            position = (lanes_like(velocity) % 64) // 16
            chosen = jnp.where(position == 0, back_two, jnp.where(position == 1, back_one, ahead))
            vorticity = curl_one[rows, :] * chosen + curl_two[rows, :] * back_one
            for index, field in enumerate((velocity, vorticity)):
                mixed = butterfly(field, 8)
                mixed_turned = turned(mixed)
                cosine, sine = cos_c[rows, :], sin_c[rows, :]
                stack(
                    rows,
                    index,
                    mixed * cosine + mixed_turned * sine,
                    mixed_turned * cosine - mixed * sine,
                )
        y_product(2, target)

    def grid_stage(source, count, target, fore_high, fore_low, back, cosine_ref, sine_ref):
        cosine, sine = cosine_ref[...], sine_ref[...]
        every = pl.ds(0, ROWS)
        for index in range(count):
            high, low = split(source[:, tile(index)])
            inner = dot(jnp.concatenate([high, low], axis=1), fore_high[...]) + dot(high, fore_low[...])
            real, imag = inner[:, :LANES], inner[:, LANES:]
            stack(every, index, real * cosine - imag * sine, real * sine + imag * cosine)
        for start in range(0, count * LANES, 256):
            part = pl.ds(start, 256)
            high, low = rhs_high[:, part], rhs_low[:, part]
            grid_buf[:, part] = dot(x_high[...], high) + dot(x_high[...], low) + dot(x_low[...], high)
        if count == 2:
            speed, spin = grid_buf[:, tile(0)], grid_buf[:, tile(1)]
            crossed = [speed * roll(spin, -32) - roll(speed, -32) * spin]
        else:
            fields = [grid_buf[:, tile(index)] for index in range(6)]
            crossed = [
                fields[1] * fields[5] - fields[2] * fields[4],
                fields[2] * fields[3] - fields[0] * fields[5],
                fields[0] * fields[4] - fields[1] * fields[3],
            ]
        for index, value in enumerate(crossed):
            high, low = split(value)
            both = dot(xt_high[...], jnp.concatenate([high, low], axis=1))
            outer = both[:, :LANES] + both[:, LANES:] + dot(xt_low[...], high)
            real, imag = outer[:ROWS], outer[ROWS:]
            ready = jnp.concatenate([real * cosine + imag * sine, imag * cosine - real * sine], axis=1)
            high, low = split(ready)
            both = dot(high, back[...])
            target[:, tile(index)] = both[:, :LANES] + both[:, LANES:] + dot(low, back[:, :LANES])

    def gather_y(source, count):
        for index in range(count):
            for rows in chunks(128):
                value = source[rows, tile(index)]
                stack(rows, index, value, -turned(value))
        y_product(count, grid_buf)

    def finish_coarse(start_ref, right_ref, target):
        gather_y(back_recv.at[0] if start_ref is begin else back_recv.at[1], 1)
        for rows in chunks(128):
            value = grid_buf[rows, tile(0)]
            value = value * turn_yc_c[rows, :] - turned(value) * turn_ys_c[rows, :]
            value = butterfly(value, 8)
            position = (lanes_like(value) % 64) // 16
            partner = jnp.where(
                position == 0, roll(value, -16), jnp.where(position == 1, roll(value, 16), roll(value, 32))
            )
            term = keep_same[rows, :] * value + keep_cross[rows, :] * partner
            target[rows, :] = damp_c[rows, :] * start_ref[rows, :] + right_ref[rows, :] + term

    loads[0].wait()
    coarse_tile(state_ref, 0, 0.5, begin)
    loads[1].wait()

    @pl.when(rank == 0)
    def _():
        spread_coarse(begin, fore_send.at[0])

    @pl.when(rank < 3)
    def _():
        pl.semaphore_wait(barrier, 2 * GROUP - 1)

    @pl.when(rank == 3)
    def _():
        pl.semaphore_wait(barrier, GROUP - 1)

    @pl.when(rank == 0)
    def _():
        post(fore_send.at[0], fore_recv.at[0], fore_sent.at[0], fore_got.at[0], rank, 1)

    def combine(a, carry):
        wave_x = UNIT * (a.astype(F32) * GROUP + place_f32)
        sub = lax.broadcasted_iota(jnp.int32, (8, LANES), 0)
        mode = sub * 128 + lax.broadcasted_iota(jnp.int32, (8, LANES), 1)
        wave_y = UNIT * jnp.where(mode < EDGE // 2, mode, mode - EDGE).astype(F32)
        stiff = VISCOSITY * (wave_x * wave_x + wave_y * wave_y)
        for part in range(2):
            for component in range(3):
                base = pl.multiple_of(a * 24 + (part * 384 + component * 8), 8)
                rows = pl.ds(base, 8)
                states = [state_ref[pl.ds(base + node * 768, 8), :] for node in range(3)]
                terms = [terms_ref[pl.ds(base + node * 768, 8), :] for node in range(3)]
                one = sum(w * s for w, s in zip(STATE_ONE, states))
                two = sum(w * s for w, s in zip(STATE_TWO, states))
                mix_one[rows, :] = one
                mix_two[rows, :] = two
                right_one[rows, :] = sum(w * t for w, t in zip(TERM_ONE, terms)) + stiff * one
                right_two[rows, :] = sum(w * t for w, t in zip(TERM_TWO, terms)) + stiff * two
                start_send[rows, :] = states[2] + HALF_STEP * terms[2]
        return carry

    for index in (3, 4, 5, 6):
        loads[index].wait()
    lax.fori_loop(0, 16, combine, 0, unroll=2)

    @pl.when(rank < 3)
    def _():
        pltpu.make_async_remote_copy(
            src_ref=start_send,
            dst_ref=start_recv,
            send_sem=start_sems.at[0],
            recv_sem=start_sems.at[1],
            device_id=device(rank + 1, place),
            device_id_type=MESH,
        ).start()

    coarse_tile(right_one, 0, 0.5, pre_one)
    pre_one[...] = pre_one[...] * damp_c[...]

    coarse_tables = (fore_high_c, fore_low_c, back_c, turn_xc_c, turn_xs_c)
    receive(fore_recv.at[0], fore_got.at[0])
    grid_stage(fore_recv.at[0], 2, back_send.at[0], *coarse_tables)
    post(back_send.at[0], back_recv.at[0], back_sent.at[0], back_got.at[0], rank, 1)

    @pl.when(rank > 0)
    def _():
        pltpu.make_async_copy(hand_recv, hand_recv, hand_sems.at[1]).wait()
        begin[...] = hand_recv[...]

    coarse_tile(right_two, 0, 0.5, pre_two)
    pre_two[...] = pre_two[...] * damp_c[...]
    receive(back_recv.at[0], back_got.at[0])
    finish_coarse(begin, pre_one, node_c)
    spread_coarse(node_c, fore_send.at[1])
    post(fore_send.at[1], fore_recv.at[1], fore_sent.at[1], fore_got.at[1], rank, 1)

    coarse_tile(mix_one, 0, 0.5, old_one)
    coarse_tile(mix_two, 0, 0.5, old_two)
    receive(fore_recv.at[1], fore_got.at[1])
    grid_stage(fore_recv.at[1], 2, back_send.at[1], *coarse_tables)
    post(back_send.at[1], back_recv.at[1], back_sent.at[1], back_got.at[1], rank, 1)

    quarter = (lane % 64) // 16
    mode_x = (lane % 16).astype(F32) * GROUP + place_f32
    mode_y = (row + 256 * quarter - jnp.where(quarter >= 2, EDGE, 0)).astype(F32)
    wave_x, wave_y, wave_sq, mask, inverse, damp = wave_tables(EDGE, mode_x, mode_y)
    ky_f[...] = wave_y
    damp_f[...] = damp
    stiff_f[...] = (2.0 * VISCOSITY) * wave_sq
    same_x[...] = wave_y * wave_y * inverse
    same_y[...] = wave_x * wave_x * inverse
    cross_f[...] = -wave_x * wave_y * inverse
    mask_f[...] = mask
    weight = jnp.where(mode_x == 0, 0.5, 1.0)
    cos_f[...] = turn_yc_f[...] * weight
    sin_f[...] = turn_ys_f[...] * weight

    receive(back_recv.at[1], back_got.at[1])
    finish_coarse(node_c, pre_two, hand_send)

    @pl.when(rank < 3)
    def _():
        spread_coarse(hand_send, fore_send.at[2])
        post(fore_send.at[2], fore_recv.at[0], fore_sent.at[2], fore_got.at[0], rank + 1, 0)
        pltpu.make_async_remote_copy(
            src_ref=hand_send,
            dst_ref=hand_recv,
            send_sem=hand_sems.at[0],
            recv_sem=hand_sems.at[1],
            device_id=device(rank + 1, place),
            device_id_type=MESH,
        ).start()

    @pl.when(rank == 0)
    def _():
        first = pl.ds(0, 768)
        right_one[...] = right_one[...] + state_ref[first, :] + HALF_STEP * terms_ref[first, :]

    @pl.when(rank > 0)
    def _():
        pltpu.make_async_copy(start_recv, start_recv, start_sems.at[1]).wait()
        right_one[...] = right_one[...] + start_recv[...]

    for component in range(3):
        fine_tile(right_one, component, right_one_f)
        fine_tile(right_two, component, right_two_f)

    def spread_fine():
        for rows in chunks(64):
            news = [begin[rows, :], node_c[rows, :], hand_send[rows, :]]
            change_one = sum(w * n for w, n in zip(STATE_ONE, news)) - old_one[rows, :]
            change_two = sum(w * n for w, n in zip(STATE_TWO, news)) - old_two[rows, :]
            inner = lanes_like(change_one) % 64
            stiff, damping = stiff_f[rows, :], damp_f[rows, :]
            fields = []
            for component in range(3):

                def placed(change):
                    low = jnp.where(inner < 8, roll(change, -16 * component), 0.0)
                    high = roll(change, 40 - 16 * component)
                    return jnp.where((inner >= 48) & (inner < 56), high, low)

                value = right_one_f[rows, tile(component)] + stiff * placed(change_one)
                value = value * damping
                node_f[rows, tile(component)] = value
                right_two_f[rows, tile(component)] = right_two_f[rows, tile(component)] + stiff * placed(change_two)
                fields.append(value)
            rotated = [turned(value) for value in fields]
            ky = ky_f[rows, :]
            kx = UNIT * ((lanes_like(ky) % 16).astype(F32) * GROUP + place_f32)
            fields += [ky * rotated[2], -kx * rotated[2], kx * rotated[1] - ky * rotated[0]]
            position = (lanes_like(ky) % 64) // 16
            cosine, sine = cos_f[rows, :], sin_f[rows, :]
            for index, field in enumerate(fields):
                mixed = butterfly(field, 32)
                mixed = jnp.where(position == 3, turned(mixed), mixed)
                mixed = butterfly(mixed, 16)
                mixed_turned = turned(mixed)
                stack(
                    rows, index, mixed * cosine + mixed_turned * sine, mixed_turned * cosine - mixed * sine
                )

    spread_fine()
    y_product(6, fine_send)
    post(fine_send, fine_recv, fine_sems.at[0], fine_sems.at[1], rank, 1)

    def give_back(source, component, target, base):
        for half in range(2):
            block_t = source[pl.ds(half * 128, 128), tile(component)].T
            for part in range(2):
                for quarter in range(4):
                    start = base + part * 384 + component * 8 + 2 * quarter + half
                    first = (part * 4 + quarter) * 16
                    target[pl.ds(start, 16, stride=24), :] = block_t[first : first + 16]

    def give_back_coarse(source, base):
        for half in range(2):
            block_t = source[pl.ds(half * 128, 128), :].T
            for part in range(2):
                for component in range(3):
                    for quarter in range(2):
                        start = base + part * 96 + component * 4 + 2 * quarter + half
                        first = part * 64 + component * 16 + quarter * 8
                        coarse_out[pl.ds(start, 8, stride=12), :] = block_t[first : first + 8]

    give_back_coarse(node_c, 0)
    give_back_coarse(hand_send, 192)
    receive(fine_recv, fine_sems.at[1])
    grid_stage(
        fine_recv, 6, fine_back_send, fore_high_f, fore_low_f, back_f, turn_xc_f, turn_xs_f
    )
    post(fine_back_send, fine_back_recv, fine_sems.at[2], fine_sems.at[3], rank, 1)
    for component in range(3):
        give_back(node_f, component, nodes_out, 0)
    receive(fine_back_recv, fine_sems.at[3])
    gather_y(fine_back_recv, 3)
    def finish_fine():
        for rows in chunks(64):
            cosine, sine = turn_yc_f[rows, :], turn_ys_f[rows, :]
            modes = []
            for component in range(3):
                value = grid_buf[rows, tile(component)]
                value = value * cosine - turned(value) * sine
                value = butterfly(value, 16)
                position = (lanes_like(value) % 64) // 16
                value = jnp.where(position == 3, -turned(value), value)
                modes.append(butterfly(value, 32))
            cross = cross_f[rows, :]
            results = [
                same_x[rows, :] * modes[0] + cross * modes[1],
                same_y[rows, :] * modes[1] + cross * modes[0],
                mask_f[rows, :] * modes[2],
            ]
            for component, value in enumerate(results):
                part = tile(component)
                right_one_f[rows, part] = value
                total = node_f[rows, part] + HALF_STEP * value + right_two_f[rows, part]
                node_f[rows, part] = total * damp_f[rows, :]

    finish_fine()
    for component in range(3):
        give_back(right_one_f, component, term_out, 0)
        give_back(node_f, component, nodes_out, 768)

    @pl.when(rank == 0)
    def _():
        drain(fore_send.at[0], fore_sent.at[0], 1)

    drain(fore_send.at[1], fore_sent.at[1], 1)
    for index in range(2):
        drain(back_send.at[index], back_sent.at[index], 1)
    drain(fine_send, fine_sems.at[0], 1)
    drain(fine_back_send, fine_sems.at[2], 1)

    @pl.when(rank < 3)
    def _():
        drain(fore_send.at[2], fore_sent.at[2], 0)
        pltpu.make_async_copy(hand_send, hand_send, hand_sems.at[0]).wait()
        pltpu.make_async_copy(start_send, start_send, start_sems.at[0]).wait()


def shards(fine_state, fine_terms):
    matrices, turns = constant_tables()
    full, natural, wide = (ROWS, LANES), (768, LANES), (ROWS, 3 * LANES)
    dma = pltpu.SemaphoreType.DMA
    scratch = [
        pltpu.VMEM((2 * ROWS, 6 * LANES), BF16),
        pltpu.VMEM((2 * ROWS, 6 * LANES), BF16),
        pltpu.VMEM((ROWS, 6 * LANES), F32),
        pltpu.VMEM(wide, BF16),
        pltpu.VMEM(wide, BF16),
        pltpu.VMEM((3, ROWS, 2 * LANES), F32),
        pltpu.VMEM((2, ROWS, 2 * LANES), F32),
        pltpu.VMEM((2, ROWS, LANES), F32),
        pltpu.VMEM((2, ROWS, LANES), F32),
        pltpu.VMEM(full, F32),
        pltpu.VMEM(full, F32),
        pltpu.VMEM((ROWS, 6 * LANES), F32),
        pltpu.VMEM((ROWS, 6 * LANES), F32),
        pltpu.VMEM(wide, F32),
        pltpu.VMEM(wide, F32),
    ]
    scratch += [pltpu.VMEM(natural, F32)] * 6
    scratch += [pltpu.VMEM(full, F32)] * (7 + 6 + 9)
    scratch += [pltpu.VMEM(wide, F32)] * 3
    scratch += [pltpu.VMEM((2304, LANES), F32)] * 2
    scratch += [pltpu.VMEM(matrices.shape, BF16), pltpu.VMEM(turns.shape, F32)]
    scratch += [dma((count,)) for count in (3, 2, 2, 2, 2, 4, 2, 7)]
    outs = pl.pallas_call(
        iterate,
        out_shape=(
            jax.ShapeDtypeStruct((1536, LANES), F32),
            jax.ShapeDtypeStruct((768, LANES), F32),
            jax.ShapeDtypeStruct((384, LANES), F32),
        ),
        in_specs=[pl.BlockSpec(memory_space=pltpu.HBM)] * 4,
        out_specs=[pl.BlockSpec(memory_space=pltpu.VMEM)] * 3,
        scratch_shapes=scratch,
        compiler_params=pltpu.CompilerParams(
            collective_id=0, has_side_effects=True, vmem_limit_bytes=62 * 1024 * 1024
        ),
        name="iterate",
    )(fine_state.reshape(2304, LANES), fine_terms.reshape(2304, LANES), jnp.asarray(matrices), jnp.asarray(turns))
    return (
        outs[0].reshape(1, 2, 2, 16, 1, 3, 1, 1024),
        outs[1].reshape(1, 2, 16, 1, 3, 1, 1024),
        outs[2].reshape(1, 2, 2, 8, 1, 3, 1, 512),
    )


def solution(mesh):
    split_over = P("tm", None, None, None, ("py", "pz"), None, None, None)
    return jax.shard_map(
        shards,
        mesh=mesh,
        in_specs=(split_over, split_over),
        out_specs=(
            split_over,
            P("tm", None, None, ("py", "pz"), None, None, None),
            split_over,
        ),
        check_vma=False,
    )
```

```python
import math

import jax
import jax.numpy as jnp
import ml_dtypes
import numpy as np
from jax import lax
from jax.experimental import pallas as pl
from jax.experimental.pallas import tpu as pltpu
from jax.sharding import PartitionSpec as P

EDGE = 1024
VISCOSITY = 0.5
TIME_STEP = 0.2
HALF_STEP = 0.5 * TIME_STEP
WEIGHTS = ((5.0 / 24.0, 1.0 / 3.0, -1.0 / 24.0), (-1.0 / 24.0, 1.0 / 3.0, 5.0 / 24.0))
UNIT = 2.0 * math.pi / EDGE
GROUP = 32
ROWS = 256
LANES = 128
F32 = jnp.float32
BF16 = jnp.bfloat16
MESH = pl.DeviceIdType.MESH
TERM_ONE = [TIME_STEP * w for w in WEIGHTS[0]]
TERM_ONE[0] -= HALF_STEP
TERM_TWO = [TIME_STEP * w for w in WEIGHTS[1]]
TERM_TWO[1] -= HALF_STEP
STATE_ONE = [-TIME_STEP * w for w in WEIGHTS[0]]
STATE_ONE[1] += HALF_STEP
STATE_TWO = [-TIME_STEP * w for w in WEIGHTS[1]]
STATE_TWO[2] += HALF_STEP


HOPS = (0, 1, 2, 1)
OFFSETS = sorted(
    ((y, z, x) for y in range(4) for z in range(2) for x in range(4)),
    key=lambda step: -(HOPS[step[0]] + 2 * step[1] + HOPS[step[2]]),
)


def halves(table):
    high = table.astype(ml_dtypes.bfloat16)
    low = (table - high.astype(np.float64)).astype(ml_dtypes.bfloat16)
    return high, low


def lane_circle(extent):
    inner = extent // GROUP
    modes = inner // 2
    pairs = 64 // modes
    fore = np.zeros((2, pairs, modes, 2, pairs, inner))
    back = np.zeros((2, pairs, inner, 2, pairs, modes))
    phase = 2.0 * math.pi * np.outer(np.arange(modes), np.arange(inner)) / inner
    kept = (np.arange(modes) * GROUP <= extent // 3)[None, :]
    for pair in range(pairs):
        cosine, sine = 2.0 / extent * np.cos(phase), 2.0 / extent * np.sin(phase)
        fore[0, pair, :, 0, pair] = cosine
        fore[1, pair, :, 0, pair] = -sine
        fore[0, pair, :, 1, pair] = sine
        fore[1, pair, :, 1, pair] = cosine
        target = pair
        sources = [(pair, pair)]
        if extent < EDGE:
            slot, rest = divmod(pair, 2)
            sources = [(((1, 2, 0, 1)[slot]) * 2 + rest, pair)]
        for source, target in sources:
            cosine = 1.0 / extent * np.cos(phase).T * kept
            sine = 1.0 / extent * np.sin(phase).T * kept
            back[0, source, :, 0, target] = cosine
            back[1, source, :, 0, target] = sine
            back[0, source, :, 1, target] = -sine
            back[1, source, :, 1, target] = cosine
    fore = fore.reshape(128, 256)
    back = back.reshape(256, 128)
    return fore, back


def real_form(table):
    return np.block([[table.real, table.imag], [-table.imag, table.real]])


def doubled(table):
    return np.concatenate([table, table], axis=0)


def lane_maps():
    sign = np.array([[1.0, 1.0], [1.0, -1.0]])
    curl_y, curl_x, partner = np.zeros((4, 4)), np.zeros((4, 4)), np.zeros((4, 4))
    curl_y[2, 0] = curl_y[2, 3] = 1.0
    curl_y[0, 2] = -1.0
    curl_x[2, 1] = -1.0
    curl_x[1, 2] = 1.0
    partner[1, 0] = partner[1, 3] = partner[0, 1] = 1.0

    def coarse(slots):
        table = np.kron(np.kron(slots, sign), np.eye(8)).astype(complex)
        return real_form(table), real_form(1j * table)

    same = coarse(np.eye(4))
    spread_c = doubled(np.concatenate(same, axis=1))
    curl_c = np.concatenate([np.concatenate(coarse(slots), axis=1) for slots in (curl_y, curl_x)], axis=0)
    finish_c = doubled(np.concatenate([same[0], coarse(partner)[0]], axis=1))
    quarters, powers = np.arange(4), np.array([0, 2, 1, 3])
    table = np.kron(1j ** (np.outer(quarters, powers) % 4), np.eye(16))
    spread_f = doubled(np.concatenate([real_form(table), real_form(1j * table)], axis=1))
    finish_f = doubled(real_form(np.conj(table).T))
    place = np.zeros((3, 4, 2, 8, 4, 16))
    for component in range(3):
        for a in range(8):
            place[component, component, 0, a, 0, a] = 1.0
            place[component, component, 1, a, 3, a] = 1.0
    place_f = doubled(np.concatenate([real_form(table.reshape(64, 64).astype(complex)) for table in place], axis=1))
    return [
        np.concatenate(pair, axis=1).astype(ml_dtypes.bfloat16)
        for pair in ((spread_c, curl_c), (finish_c, spread_f), (place_f, finish_f))
    ]


def constant_tables():
    index = np.arange(ROWS)
    phase = 2.0 * math.pi * np.outer(index, index) / ROWS
    along_y = np.concatenate([np.cos(phase), np.sin(phase)], axis=1)
    small = 2.0 * math.pi * np.outer(np.arange(GROUP), np.arange(GROUP)) / GROUP
    eye = np.eye(8)
    along_x = np.concatenate([np.kron(np.cos(small), eye), -np.kron(np.sin(small), eye)], axis=1)
    maps = lane_maps()
    matrices = list(halves(along_y)) + [maps[0]] + list(halves(along_x))
    matrices.append(np.concatenate(halves(along_x.T), axis=1))
    lane = np.arange(LANES)
    turns, inner_parts = [], []
    for extent in (EDGE // 2, EDGE):
        fore, back = lane_circle(extent)
        fore_high, fore_low = halves(fore)
        back_high, back_low = halves(back)
        inner_parts.append(
            np.concatenate([fore_high, fore_high, fore_low, np.concatenate([back_high, back_low], axis=1)], axis=0)
        )
        inner = extent // GROUP
        turn = 2.0 * math.pi * np.outer(index // 8, lane % inner) / extent
        turns += [np.cos(turn), np.sin(turn)]
        if extent < EDGE:
            offset = (lane % 16) // 8
        else:
            offset = np.array([0, 2, 1, 3])[(lane % 64) // 16]
        turn = 2.0 * math.pi * np.outer(index, offset) / extent
        turns += [np.cos(turn), np.sin(turn)]
    matrices.append(np.concatenate(inner_parts, axis=1))
    matrices += maps[1:]
    return np.concatenate(matrices, axis=0), np.concatenate(turns, axis=0).astype(np.float32)


def split(value):
    high = value.astype(BF16)
    return high, (value - high.astype(F32)).astype(BF16)


def dot(left, right):
    return jnp.dot(left, right, preferred_element_type=F32)


def roll(value, shift):
    return pltpu.roll(value, shift % LANES, axis=1)


def lanes_like(value):
    return lax.broadcasted_iota(jnp.int32, value.shape, 1)


def turned(value):
    other = roll(value, 64)
    return jnp.where(lanes_like(value) < 64, -other, other)


def tile(index):
    return pl.ds(index * LANES, LANES)


def chunks(size):
    return [pl.ds(start, size) for start in range(0, ROWS, size)]


def iterate(
    state_hbm, terms_hbm, matrices_hbm, turns_hbm,
    nodes_out, term_out, coarse_out,
    rhs_high, rhs_low, grid_buf,
    fore_send, fore_recv, back_send, back_recv, hand_send, hand_recv,
    fine_send, fine_recv, fine_back_send, fine_back_recv, start_send, start_recv,
    right_one, right_two, mix_one, mix_two,
    curl_one, curl_two, keep_same, keep_cross, damp_c, cos_c, sin_c,
    pre_one, pre_two, old_one, old_two, begin, node_c,
    ky_f, damp_f, stiff_f, cos_f, sin_f, same_x, same_y, cross_f, mask_f,
    right_one_f, right_two_f, node_f,
    state_ref, terms_ref, matrices, turns,
    fore_sent, fore_got, back_sent, back_got, hand_sems, fine_sent, fine_got, fine_back_sent, fine_back_got, start_sems,
    load_sems,
):
    loads = []
    for source, target, start, size in (
        (state_hbm, state_ref, 0, 768),
        (matrices_hbm, matrices, 0, 768),
        (turns_hbm, turns, 0, 1024),
        (state_hbm, state_ref, 768, 1536),
        (terms_hbm, terms_ref, 0, 2304),
        (matrices_hbm, matrices, 768, 2176),
        (turns_hbm, turns, 1024, 1024),
    ):
        rows = pl.ds(start, size)
        loads.append(pltpu.make_async_copy(source.at[rows], target.at[rows], load_sems.at[len(loads)]))
        loads[-1].start()

    def matrix(start, size, first=0, width=512):
        return matrices.at[pl.ds(start, size), pl.ds(first, width)]

    y_high, y_low = matrix(0, 256), matrix(256, 256)
    spread_map, curl_map = matrix(512, 256, 0, 256), matrix(512, 256, 256, 256)
    x_high, x_low = matrix(768, 256), matrix(1024, 256)
    xt_high, xt_low = matrix(1280, 512, 0, 256), matrix(1280, 512, 256, 256)
    fore_high_c, fore_low_c, back_c = (matrix(*rows, 0, 256) for rows in ((1792, 256), (2048, 128), (2176, 256)))
    fore_high_f, fore_low_f, back_f = (matrix(*rows, 256, 256) for rows in ((1792, 256), (2048, 128), (2176, 256)))
    finish_map, spread_map_f = matrix(2432, 256, 0, 256), matrix(2432, 256, 256, 256)
    place_map, finish_map_f = matrix(2688, 256, 0, 384), matrix(2688, 256, 384, 128)
    turn_xc_c, turn_xs_c, turn_yc_c, turn_ys_c, turn_xc_f, turn_xs_f, turn_yc_f, turn_ys_f = (
        turns.at[pl.ds(start, ROWS), :] for start in range(0, 8 * ROWS, ROWS)
    )
    rank = lax.axis_index("tm")
    place = lax.axis_index("py") * 8 + lax.axis_index("pz")

    def device(time_rank, position):
        return (time_rank, position // 8, position % 8)

    barrier = pltpu.get_barrier_semaphore()

    @pl.when(rank > 0)
    def _():
        def greet_back(step, carry):
            pl.semaphore_signal(
                barrier, inc=1, device_id=device(rank - 1, (place + step) % GROUP), device_id_type=MESH
            )
            return carry

        lax.fori_loop(0, GROUP, greet_back, 0)

    def greet(step, carry):
        pl.semaphore_signal(
            barrier, inc=1, device_id=device(rank, (place + step) % GROUP), device_id_type=MESH
        )
        return carry

    lax.fori_loop(1, GROUP, greet, 0)

    def block(position):
        return pl.ds(pl.multiple_of(position * 8, 8), 8)

    at_y, at_z, at_x = lax.axis_index("py"), lax.axis_index("pz") // 4, lax.axis_index("pz") % 4
    spots_y = [(at_y + step) % 4 for step in range(4)]
    spots_z = [(at_z + step) % 2 for step in range(2)]
    spots_x = [(at_x + step) % 4 for step in range(4)]

    def post(source, target, sent, got, time_rank, first):
        for step_y, step_z, step_x in OFFSETS[: GROUP - first]:
            spot_y, spot_pz = spots_y[step_y], spots_z[step_z] * 4 + spots_x[step_x]
            pltpu.make_async_remote_copy(
                src_ref=source.at[block(spot_y * 8 + spot_pz)],
                dst_ref=target.at[block(place)],
                send_sem=sent,
                recv_sem=got,
                device_id=(time_rank, spot_y, spot_pz),
                device_id_type=MESH,
            ).start()
        if first == 1:
            pltpu.make_async_copy(source.at[block(place)], target.at[block(place)], got).start()

    def receive(target, got):
        pltpu.make_async_copy(target, target, got).wait()

    def drain(source, sent, first):
        part = source.at[pl.ds(0, (GROUP - first) * 8)]
        pltpu.make_async_copy(part, part, sent).wait()

    place_f32 = place.astype(F32)
    row = lax.broadcasted_iota(jnp.int32, (ROWS, LANES), 0)
    lane = lax.broadcasted_iota(jnp.int32, (ROWS, LANES), 1)

    def wave_tables(extent, mode_x, mode_y):
        wave_x, wave_y = UNIT * mode_x, UNIT * mode_y
        wave_sq = wave_x * wave_x + wave_y * wave_y
        anchor = (mode_x == 0) & (mode_y == 0)
        kept = (mode_x <= extent // 3) & (jnp.abs(mode_y) <= extent // 3) & ~anchor
        mask = jnp.where(kept, 1.0, 0.0).astype(F32)
        inverse = mask / jnp.where(anchor, 1.0, wave_sq)
        damp = 1.0 / (1.0 + HALF_STEP * VISCOSITY * wave_sq)
        return wave_x, wave_y, wave_sq, mask, inverse, damp

    loads[2].wait()
    slot = (lane % 64) // 16
    mode_x = (lane % 8).astype(F32) * GROUP + place_f32
    mode_y = (row - 256 * ((lane % 16) // 8)).astype(F32)
    wave_x, wave_y, wave_sq, mask, inverse, damp = wave_tables(EDGE // 2, mode_x, mode_y)
    curl_one[...] = wave_y
    curl_two[...] = wave_x
    same = jnp.where(slot == 2, mask, jnp.where(slot == 1, wave_x * wave_x, wave_y * wave_y) * inverse)
    keep_same[...] = same * (HALF_STEP * damp)
    keep_cross[...] = jnp.where(slot == 2, 0.0, -wave_x * wave_y * inverse) * (HALF_STEP * damp)
    damp_c[...] = damp
    weight = jnp.where(mode_x == 0, 0.5, 1.0)
    cos_c[...] = turn_yc_c[...] * weight
    sin_c[...] = turn_ys_c[...] * weight

    def coarse_tile(ref, base, scale, target):
        for half in range(2):
            pieces = []
            for part in range(2):
                for component in (0, 1, 2, 0):
                    for quarter in (0, 3):
                        start = base + part * 384 + component * 8 + 2 * quarter + half
                        pieces.append(ref[pl.ds(start, 8, stride=24), :])
            target[pl.ds(half * 128, 128), :] = scale * jnp.concatenate(pieces, axis=0).T

    def fine_tile(ref, component, target):
        for half in range(2):
            pieces = []
            for part in range(2):
                for quarter in range(4):
                    start = part * 384 + component * 8 + 2 * quarter + half
                    pieces.append(ref[pl.ds(start, 16, stride=24), :])
            target[pl.ds(half * 128, 128), tile(component)] = jnp.concatenate(pieces, axis=0).T

    def y_product(first, count, target):
        part = pl.ds(first * LANES, count * LANES)
        high, low = rhs_high[:, part], rhs_low[:, part]
        target[...] = dot(y_high[...], high) + dot(y_high[...], low) + dot(y_low[...], high)

    def pair(high, low):
        return jnp.concatenate([high, low], axis=1)

    def twisted(rows, index, value, value_turned, cosine, sine):
        stack(rows, index, value * cosine + value_turned * sine, value_turned * cosine - value * sine)

    def stack(rows, index, first, second):
        high, low = split(first)
        rhs_high[rows, tile(index)] = high
        rhs_low[rows, tile(index)] = low
        high, low = split(second)
        lower = pl.ds(rows.start + ROWS, rows.size)
        rhs_high[lower, tile(index)] = high
        rhs_low[lower, tile(index)] = low

    def spread_coarse(source, target):
        for rows in chunks(128):
            velocity = source[rows, :]
            high_y, low_y = split(velocity * curl_one[rows, :])
            high_x, low_x = split(velocity * curl_two[rows, :])
            mixed = dot(pair(*split(velocity)), spread_map[...])
            curled = dot(pair(high_y, high_x), curl_map[...]) + dot(pair(low_y, low_x), curl_map[...])
            cosine, sine = cos_c[rows, :], sin_c[rows, :]
            twisted(rows, 0, mixed[:, :LANES], mixed[:, LANES:], cosine, sine)
            twisted(rows, 1, curled[:, LANES:], -curled[:, :LANES], cosine, sine)
        y_product(0, 2, target)

    def to_grid(source, first, fore_high, fore_low, cosine, sine):
        every = pl.ds(0, ROWS)
        for index in range(2):
            high, low = split(source[:, tile(index)])
            inner = dot(pair(high, low), fore_high[...]) + dot(high, fore_low[...])
            real, imag = inner[:, :LANES], inner[:, LANES:]
            stack(every, first + index, real * cosine - imag * sine, real * sine + imag * cosine)
        part = pl.ds(first * LANES, 2 * LANES)
        high, low = rhs_high[:, part], rhs_low[:, part]
        grid_buf[:, part] = dot(x_high[...], high) + dot(x_high[...], low) + dot(x_low[...], high)

    def from_grid(value, target, back, cosine, sine):
        high, low = split(value)
        both = dot(xt_high[...], pair(high, low))
        outer = both[:, :LANES] + both[:, LANES:] + dot(xt_low[...], high)
        real, imag = outer[:ROWS], outer[ROWS:]
        high, low = split(pair(real * cosine + imag * sine, imag * cosine - real * sine))
        both = dot(high, back[...])
        target[...] = both[:, :LANES] + both[:, LANES:] + dot(low, back[:, :LANES])

    def grid_coarse(source, target):
        cosine, sine = turn_xc_c[...], turn_xs_c[...]
        to_grid(source, 0, fore_high_c, fore_low_c, cosine, sine)
        speed, spin = grid_buf[:, tile(0)], grid_buf[:, tile(1)]
        crossed = speed * roll(spin, -32) - roll(speed, -32) * spin
        from_grid(crossed, target, back_c, cosine, sine)

    def finish_coarse(source, start_ref, right_ref, target):
        for rows in chunks(128):
            value = source[rows, :]
            other = turned(value)
            stack(rows, 0, value, -other)
            stack(rows, 1, other, value)
        y_product(0, 2, grid_buf.at[:, pl.ds(0, 2 * LANES)])
        for rows in chunks(128):
            value = grid_buf[rows, tile(0)] * turn_yc_c[rows, :] - grid_buf[rows, tile(1)] * turn_ys_c[rows, :]
            modes = dot(pair(*split(value)), finish_map[...])
            term = keep_same[rows, :] * modes[:, :LANES] + keep_cross[rows, :] * modes[:, LANES:]
            target[rows, :] = damp_c[rows, :] * start_ref[rows, :] + right_ref[rows, :] + term

    loads[0].wait()
    coarse_tile(state_ref, 0, 0.5, begin)
    loads[1].wait()

    @pl.when(rank == 0)
    def _():
        spread_coarse(begin, fore_send.at[0])

    @pl.when(rank < 3)
    def _():
        pl.semaphore_wait(barrier, 2 * GROUP - 1)

    @pl.when(rank == 3)
    def _():
        pl.semaphore_wait(barrier, GROUP - 1)

    @pl.when(rank == 0)
    def _():
        post(fore_send.at[0], fore_recv.at[0], fore_sent.at[0], fore_got.at[0], rank, 1)

    def combine(a, carry):
        wave_x = UNIT * (a.astype(F32) * GROUP + place_f32)
        sub = lax.broadcasted_iota(jnp.int32, (8, LANES), 0)
        mode = sub * 128 + lax.broadcasted_iota(jnp.int32, (8, LANES), 1)
        wave_y = UNIT * jnp.where(mode < EDGE // 2, mode, mode - EDGE).astype(F32)
        stiff = VISCOSITY * (wave_x * wave_x + wave_y * wave_y)
        for part in range(2):
            for component in range(3):
                base = pl.multiple_of(a * 24 + (part * 384 + component * 8), 8)
                rows = pl.ds(base, 8)
                states = [state_ref[pl.ds(base + node * 768, 8), :] for node in range(3)]
                terms = [terms_ref[pl.ds(base + node * 768, 8), :] for node in range(3)]
                one = sum(w * s for w, s in zip(STATE_ONE, states))
                two = sum(w * s for w, s in zip(STATE_TWO, states))
                mix_one[rows, :] = one
                mix_two[rows, :] = two
                right_one[rows, :] = sum(w * t for w, t in zip(TERM_ONE, terms)) + stiff * one
                right_two[rows, :] = sum(w * t for w, t in zip(TERM_TWO, terms)) + stiff * two
                start_send[rows, :] = states[2] + HALF_STEP * terms[2]
        return carry

    for index in (3, 4, 5, 6):
        loads[index].wait()
    lax.fori_loop(0, 16, combine, 0, unroll=2)

    @pl.when(rank < 3)
    def _():
        pltpu.make_async_remote_copy(
            src_ref=start_send,
            dst_ref=start_recv,
            send_sem=start_sems.at[0],
            recv_sem=start_sems.at[1],
            device_id=device(rank + 1, place),
            device_id_type=MESH,
        ).start()

    coarse_tile(right_one, 0, 0.5, pre_one)
    pre_one[...] = pre_one[...] * damp_c[...]

    receive(fore_recv.at[0], fore_got.at[0])
    grid_coarse(fore_recv.at[0], back_send.at[0])
    post(back_send.at[0], back_recv.at[0], back_sent.at[0], back_got.at[0], rank, 1)

    @pl.when(rank > 0)
    def _():
        pltpu.make_async_copy(hand_recv, hand_recv, hand_sems.at[1]).wait()
        begin[...] = hand_recv[...]

    coarse_tile(right_two, 0, 0.5, pre_two)
    pre_two[...] = pre_two[...] * damp_c[...]
    receive(back_recv.at[0], back_got.at[0])
    finish_coarse(back_recv.at[0], begin, pre_one, node_c)
    spread_coarse(node_c, fore_send.at[1])
    post(fore_send.at[1], fore_recv.at[1], fore_sent.at[1], fore_got.at[1], rank, 1)

    coarse_tile(mix_one, 0, 0.5, old_one)
    coarse_tile(mix_two, 0, 0.5, old_two)
    receive(fore_recv.at[1], fore_got.at[1])
    grid_coarse(fore_recv.at[1], back_send.at[1])
    post(back_send.at[1], back_recv.at[1], back_sent.at[1], back_got.at[1], rank, 1)

    quarter = (lane % 64) // 16
    mode_x = (lane % 16).astype(F32) * GROUP + place_f32
    mode_y = (row + 256 * quarter - jnp.where(quarter >= 2, EDGE, 0)).astype(F32)
    wave_x, wave_y, wave_sq, mask, inverse, damp = wave_tables(EDGE, mode_x, mode_y)
    ky_f[...] = wave_y
    damp_f[...] = damp
    stiff_f[...] = (2.0 * VISCOSITY) * wave_sq
    same_x[...] = wave_y * wave_y * inverse
    same_y[...] = wave_x * wave_x * inverse
    cross_f[...] = -wave_x * wave_y * inverse
    mask_f[...] = mask
    weight = jnp.where(mode_x == 0, 0.5, 1.0)
    cos_f[...] = turn_yc_f[...] * weight
    sin_f[...] = turn_ys_f[...] * weight

    receive(back_recv.at[1], back_got.at[1])
    finish_coarse(back_recv.at[1], node_c, pre_two, hand_send)

    @pl.when(rank < 3)
    def _():
        spread_coarse(hand_send, fore_send.at[2])
        post(fore_send.at[2], fore_recv.at[0], fore_sent.at[2], fore_got.at[0], rank + 1, 0)
        pltpu.make_async_remote_copy(
            src_ref=hand_send,
            dst_ref=hand_recv,
            send_sem=hand_sems.at[0],
            recv_sem=hand_sems.at[1],
            device_id=device(rank + 1, place),
            device_id_type=MESH,
        ).start()

    @pl.when(rank == 0)
    def _():
        first = pl.ds(0, 768)
        right_one[...] = right_one[...] + state_ref[first, :] + HALF_STEP * terms_ref[first, :]

    @pl.when(rank > 0)
    def _():
        pltpu.make_async_copy(start_recv, start_recv, start_sems.at[1]).wait()
        right_one[...] = right_one[...] + start_recv[...]

    for component in range(3):
        fine_tile(right_one, component, right_one_f)
        fine_tile(right_two, component, right_two_f)

    def correct_fine():
        for rows in chunks(128):
            news = [begin[rows, :], node_c[rows, :], hand_send[rows, :]]
            change_one = sum(w * n for w, n in zip(STATE_ONE, news)) - old_one[rows, :]
            change_two = sum(w * n for w, n in zip(STATE_TWO, news)) - old_two[rows, :]
            placed_one = dot(pair(*split(change_one)), place_map[...])
            placed_two = dot(pair(*split(change_two)), place_map[...])
            stiff, damping = stiff_f[rows, :], damp_f[rows, :]
            for component in range(3):
                part = tile(component)
                lanes = slice(component * LANES, (component + 1) * LANES)
                node_f[rows, part] = (right_one_f[rows, part] + stiff * placed_one[:, lanes]) * damping
                right_two_f[rows, part] = right_two_f[rows, part] + stiff * placed_two[:, lanes]

    def fine_field(index, rows):
        x, y, z = (node_f.at[rows, tile(component)] for component in range(3))
        if index < 3:
            return (x, y, z)[index][...]
        ky = ky_f[rows, :]
        kx = UNIT * ((lanes_like(ky) % 16).astype(F32) * GROUP + place_f32)
        if index == 3:
            return ky * z[...]
        if index == 4:
            return -kx * z[...]
        return kx * y[...] - ky * x[...]

    def spread_fine(first):
        for rows in chunks(128):
            cosine, sine = cos_f[rows, :], sin_f[rows, :]
            for index in (first, first + 1):
                mixed = dot(pair(*split(fine_field(index, rows))), spread_map_f[...])
                if index < 3:
                    twisted(rows, index, mixed[:, :LANES], mixed[:, LANES:], cosine, sine)
                else:
                    twisted(rows, index, mixed[:, LANES:], -mixed[:, :LANES], cosine, sine)
        y_product(first, 2, fine_send.at[first // 2])

    correct_fine()
    for part in range(3):
        spread_fine(2 * part)
        post(fine_send.at[part], fine_recv.at[part], fine_sent.at[part], fine_got.at[part], rank, 1)

    def give_back(source, component, target, base):
        for half in range(2):
            block_t = source[pl.ds(half * 128, 128), tile(component)].T
            for part in range(2):
                for quarter in range(4):
                    start = base + part * 384 + component * 8 + 2 * quarter + half
                    first = (part * 4 + quarter) * 16
                    target[pl.ds(start, 16, stride=24), :] = block_t[first : first + 16]

    def give_back_coarse(source, base):
        for half in range(2):
            block_t = source[pl.ds(half * 128, 128), :].T
            for part in range(2):
                for component in range(3):
                    for quarter in range(2):
                        start = base + part * 96 + component * 4 + 2 * quarter + half
                        first = part * 64 + component * 16 + quarter * 8
                        coarse_out[pl.ds(start, 8, stride=12), :] = block_t[first : first + 8]

    give_back_coarse(node_c, 0)
    give_back_coarse(hand_send, 192)
    def cross_fine(component):
        second, third = (component + 1) % 3, (component + 2) % 3
        fields = [grid_buf[:, tile(index)] for index in (second, third, second + 3, third + 3)]
        return fields[0] * fields[3] - fields[1] * fields[2]

    for part in range(3):
        receive(fine_recv.at[part], fine_got.at[part])
        to_grid(fine_recv.at[part], 2 * part, fore_high_f, fore_low_f, turn_xc_f[...], turn_xs_f[...])
    for part in range(3):
        from_grid(cross_fine(part), fine_back_send.at[part], back_f, turn_xc_f[...], turn_xs_f[...])
        post(
            fine_back_send.at[part],
            fine_back_recv.at[part],
            fine_back_sent.at[part],
            fine_back_got.at[part],
            rank,
            1,
        )
    for component in range(3):
        give_back(node_f, component, nodes_out, 0)

    def gather_fine(component):
        for rows in chunks(128):
            value = fine_back_recv[component, rows, :]
            stack(rows, component, value, -turned(value))
        y_product(component, 1, grid_buf.at[:, tile(component)])
        for rows in chunks(128):
            value = grid_buf[rows, tile(component)]
            value = value * turn_yc_f[rows, :] - turned(value) * turn_ys_f[rows, :]
            right_one_f[rows, tile(component)] = dot(pair(*split(value)), finish_map_f[...])

    def finish_fine():
        for rows in chunks(64):
            modes = [right_one_f[rows, tile(component)] for component in range(3)]
            cross = cross_f[rows, :]
            results = [
                same_x[rows, :] * modes[0] + cross * modes[1],
                same_y[rows, :] * modes[1] + cross * modes[0],
                mask_f[rows, :] * modes[2],
            ]
            for component, value in enumerate(results):
                part = tile(component)
                right_one_f[rows, part] = value
                total = node_f[rows, part] + HALF_STEP * value + right_two_f[rows, part]
                node_f[rows, part] = total * damp_f[rows, :]

    for part in range(3):
        receive(fine_back_recv.at[part], fine_back_got.at[part])
        gather_fine(part)
    finish_fine()
    for component in range(3):
        give_back(right_one_f, component, term_out, 0)
        give_back(node_f, component, nodes_out, 768)

    @pl.when(rank == 0)
    def _():
        drain(fore_send.at[0], fore_sent.at[0], 1)

    drain(fore_send.at[1], fore_sent.at[1], 1)
    for index in range(2):
        drain(back_send.at[index], back_sent.at[index], 1)
    for part in range(3):
        drain(fine_send.at[part], fine_sent.at[part], 1)
        drain(fine_back_send.at[part], fine_back_sent.at[part], 1)

    @pl.when(rank < 3)
    def _():
        drain(fore_send.at[2], fore_sent.at[2], 0)
        pltpu.make_async_copy(hand_send, hand_send, hand_sems.at[0]).wait()
        pltpu.make_async_copy(start_send, start_send, start_sems.at[0]).wait()


def shards(fine_state, fine_terms):
    matrices, turns = constant_tables()
    full, natural, wide = (ROWS, LANES), (768, LANES), (ROWS, 3 * LANES)
    dma = pltpu.SemaphoreType.DMA
    scratch = [
        pltpu.VMEM((2 * ROWS, 6 * LANES), BF16),
        pltpu.VMEM((2 * ROWS, 6 * LANES), BF16),
        pltpu.VMEM((ROWS, 6 * LANES), F32),
        pltpu.VMEM((3, ROWS, 2 * LANES), F32),
        pltpu.VMEM((2, ROWS, 2 * LANES), F32),
        pltpu.VMEM((2, ROWS, LANES), F32),
        pltpu.VMEM((2, ROWS, LANES), F32),
        pltpu.VMEM(full, F32),
        pltpu.VMEM(full, F32),
        pltpu.VMEM((3, ROWS, 2 * LANES), F32),
        pltpu.VMEM((3, ROWS, 2 * LANES), F32),
        pltpu.VMEM((3, ROWS, LANES), F32),
        pltpu.VMEM((3, ROWS, LANES), F32),
    ]
    scratch += [pltpu.VMEM(natural, F32)] * 6
    scratch += [pltpu.VMEM(full, F32)] * (7 + 6 + 9)
    scratch += [pltpu.VMEM(wide, F32)] * 3
    scratch += [pltpu.VMEM((2304, LANES), F32)] * 2
    scratch += [pltpu.VMEM(matrices.shape, BF16), pltpu.VMEM(turns.shape, F32)]
    scratch += [dma((count,)) for count in (3, 2, 2, 2, 2, 3, 3, 3, 3, 2, 7)]
    outs = pl.pallas_call(
        iterate,
        out_shape=(
            jax.ShapeDtypeStruct((1536, LANES), F32),
            jax.ShapeDtypeStruct((768, LANES), F32),
            jax.ShapeDtypeStruct((384, LANES), F32),
        ),
        in_specs=[pl.BlockSpec(memory_space=pltpu.HBM)] * 4,
        out_specs=[pl.BlockSpec(memory_space=pltpu.VMEM)] * 3,
        scratch_shapes=scratch,
        compiler_params=pltpu.CompilerParams(
            collective_id=0, has_side_effects=True, vmem_limit_bytes=62 * 1024 * 1024
        ),
        name="iterate",
    )(fine_state.reshape(2304, LANES), fine_terms.reshape(2304, LANES), jnp.asarray(matrices), jnp.asarray(turns))
    return (
        outs[0].reshape(1, 2, 2, 16, 1, 3, 1, 1024),
        outs[1].reshape(1, 2, 16, 1, 3, 1, 1024),
        outs[2].reshape(1, 2, 2, 8, 1, 3, 1, 512),
    )


def solution(mesh):
    split_over = P("tm", None, None, None, ("py", "pz"), None, None, None)
    return jax.shard_map(
        shards,
        mesh=mesh,
        in_specs=(split_over, split_over),
        out_specs=(
            split_over,
            P("tm", None, None, ("py", "pz"), None, None, None),
            split_over,
        ),
        check_vma=False,
    )
```

```python
import math

import jax
import jax.numpy as jnp
import ml_dtypes
import numpy as np
from jax import lax
from jax.experimental import pallas as pl
from jax.experimental.pallas import tpu as pltpu
from jax.sharding import PartitionSpec as P

EDGE = 1024
VISCOSITY = 0.5
TIME_STEP = 0.2
HALF_STEP = 0.5 * TIME_STEP
WEIGHTS = ((5.0 / 24.0, 1.0 / 3.0, -1.0 / 24.0), (-1.0 / 24.0, 1.0 / 3.0, 5.0 / 24.0))
UNIT = 2.0 * math.pi / EDGE
GROUP = 32
ROWS = 256
LANES = 128
PIECES = 4
F32 = jnp.float32
BF16 = jnp.bfloat16
MESH = pl.DeviceIdType.MESH
TERM_ONE = [TIME_STEP * w for w in WEIGHTS[0]]
TERM_ONE[0] -= HALF_STEP
TERM_TWO = [TIME_STEP * w for w in WEIGHTS[1]]
TERM_TWO[1] -= HALF_STEP
STATE_ONE = [-TIME_STEP * w for w in WEIGHTS[0]]
STATE_ONE[1] += HALF_STEP
STATE_TWO = [-TIME_STEP * w for w in WEIGHTS[1]]
STATE_TWO[2] += HALF_STEP


HOPS = (0, 1, 2, 1)
DUTY, RANK = (
    sorted(
        ((y, z, x) for y in range(4) for z in range(2) for x in range(4)),
        key=lambda step: -(HOPS[step[0]] + apart * step[1] + HOPS[step[2]]),
    )
    for apart in (1, 2)
)


def halves(table):
    high = table.astype(ml_dtypes.bfloat16)
    low = (table - high.astype(np.float64)).astype(ml_dtypes.bfloat16)
    return high, low


def lane_circle(extent):
    inner = extent // GROUP
    modes = inner // 2
    pairs = 64 // modes
    fore = np.zeros((2, pairs, modes, 2, pairs, inner))
    back = np.zeros((2, pairs, inner, 2, pairs, modes))
    phase = 2.0 * math.pi * np.outer(np.arange(modes), np.arange(inner)) / inner
    kept = (np.arange(modes) * GROUP <= extent // 3)[None, :]
    for pair in range(pairs):
        cosine, sine = 2.0 / extent * np.cos(phase), 2.0 / extent * np.sin(phase)
        fore[0, pair, :, 0, pair] = cosine
        fore[1, pair, :, 0, pair] = -sine
        fore[0, pair, :, 1, pair] = sine
        fore[1, pair, :, 1, pair] = cosine
        target = pair
        sources = [(pair, pair)]
        if extent < EDGE:
            slot, rest = divmod(pair, 2)
            sources = [(((1, 2, 0, 1)[slot]) * 2 + rest, pair)]
        for source, target in sources:
            cosine = 1.0 / extent * np.cos(phase).T * kept
            sine = 1.0 / extent * np.sin(phase).T * kept
            back[0, source, :, 0, target] = cosine
            back[1, source, :, 0, target] = sine
            back[0, source, :, 1, target] = -sine
            back[1, source, :, 1, target] = cosine
    fore = fore.reshape(128, 256)
    back = back.reshape(256, 128)
    return fore, back


def real_form(table):
    return np.block([[table.real, table.imag], [-table.imag, table.real]])


def doubled(table):
    return np.concatenate([table, table], axis=0)


def lane_maps():
    sign = np.array([[1.0, 1.0], [1.0, -1.0]])
    curl_y, curl_x, partner = np.zeros((4, 4)), np.zeros((4, 4)), np.zeros((4, 4))
    curl_y[2, 0] = curl_y[2, 3] = 1.0
    curl_y[0, 2] = -1.0
    curl_x[2, 1] = -1.0
    curl_x[1, 2] = 1.0
    partner[1, 0] = partner[1, 3] = partner[0, 1] = 1.0

    def coarse(slots):
        table = np.kron(np.kron(slots, sign), np.eye(8)).astype(complex)
        return real_form(table), real_form(1j * table)

    same = coarse(np.eye(4))
    spread_c = doubled(np.concatenate(same, axis=1))
    curl_c = np.concatenate([np.concatenate(coarse(slots), axis=1) for slots in (curl_y, curl_x)], axis=0)
    finish_c = doubled(np.concatenate([same[0], coarse(partner)[0]], axis=1))
    quarters, powers = np.arange(4), np.array([0, 2, 1, 3])
    table = np.kron(1j ** (np.outer(quarters, powers) % 4), np.eye(16))
    spread_f = doubled(np.concatenate([real_form(table), real_form(1j * table)], axis=1))
    finish_f = doubled(real_form(np.conj(table).T))
    place = np.zeros((3, 4, 2, 8, 4, 16))
    for component in range(3):
        for a in range(8):
            place[component, component, 0, a, 0, a] = 1.0
            place[component, component, 1, a, 3, a] = 1.0
    place_f = doubled(np.concatenate([real_form(table.reshape(64, 64).astype(complex)) for table in place], axis=1))
    return [
        np.concatenate(pair, axis=1).astype(ml_dtypes.bfloat16)
        for pair in ((spread_c, curl_c), (finish_c, spread_f), (place_f, finish_f))
    ]


def constant_tables():
    index = np.arange(ROWS)
    phase = 2.0 * math.pi * np.outer(index, index) / ROWS
    along_y = np.concatenate([np.cos(phase), np.sin(phase)], axis=1)
    small = 2.0 * math.pi * np.outer(np.arange(GROUP), np.arange(GROUP)) / GROUP
    eye = np.eye(8)
    along_x = np.concatenate([np.kron(np.cos(small), eye), -np.kron(np.sin(small), eye)], axis=1)
    maps = lane_maps()
    matrices = list(halves(along_y)) + [maps[0]] + list(halves(along_x))
    matrices.append(np.concatenate(halves(along_x.T), axis=1))
    lane = np.arange(LANES)
    turns, inner_parts = [], []
    for extent in (EDGE // 2, EDGE):
        fore, back = lane_circle(extent)
        fore_high, fore_low = halves(fore)
        back_high, back_low = halves(back)
        inner_parts.append(
            np.concatenate([fore_high, fore_high, fore_low, np.concatenate([back_high, back_low], axis=1)], axis=0)
        )
        inner = extent // GROUP
        turn = 2.0 * math.pi * np.outer(index // 8, lane % inner) / extent
        turns += [np.cos(turn), np.sin(turn)]
        if extent < EDGE:
            offset = (lane % 16) // 8
        else:
            offset = np.array([0, 2, 1, 3])[(lane % 64) // 16]
        turn = 2.0 * math.pi * np.outer(index, offset) / extent
        turns += [np.cos(turn), np.sin(turn)]
    matrices.append(np.concatenate(inner_parts, axis=1))
    matrices += maps[1:]
    return np.concatenate(matrices, axis=0), np.concatenate(turns, axis=0).astype(np.float32)


def split(value):
    high = value.astype(BF16)
    return high, (value - high.astype(F32)).astype(BF16)


def dot(left, right):
    return jnp.dot(left, right, preferred_element_type=F32)


def roll(value, shift):
    return pltpu.roll(value, shift % LANES, axis=1)


def lanes_like(value):
    return lax.broadcasted_iota(jnp.int32, value.shape, 1)


def turned(value):
    other = roll(value, 64)
    return jnp.where(lanes_like(value) < 64, -other, other)


def tile(index):
    return pl.ds(index * LANES, LANES)


def chunks(size):
    return [pl.ds(start, size) for start in range(0, ROWS, size)]


def iterate(
    state_hbm, terms_hbm, matrices_hbm, turns_hbm,
    nodes_out, term_out, coarse_out,
    rhs_high, rhs_low, grid_buf,
    fore_send, fore_recv, back_send, back_recv, last_recv, hand_recv,
    parcel_send, parcel_recv, sweep, news,
    fine_send, fine_recv, fine_back_send, fine_back_recv, start_send, start_recv,
    right_one, right_two, mix_one, mix_two,
    curl_y, keep_same, keep_cross, damp_c, keep_same_r, keep_cross_r, damp_r, old_one, old_two,
    ky_f, damp_f, stiff_f, cos_f, sin_f, same_x, same_y, cross_f, mask_f,
    right_one_f, right_two_f, node_f,
    state_ref, terms_ref, matrices, turns,
    fore_sent, fore_got, back_sent, back_got, hand_sems, parcel_sems, news_sent, news_got,
    fine_sent, fine_got, fine_back_sent, fine_back_got, start_sems, load_sems,
):
    loads = []
    for source, target, start, size in (
        (state_hbm, state_ref, 0, 768),
        (matrices_hbm, matrices, 0, 768),
        (turns_hbm, turns, 0, 1024),
        (state_hbm, state_ref, 768, 1536),
        (terms_hbm, terms_ref, 0, 2304),
        (matrices_hbm, matrices, 768, 2176),
        (turns_hbm, turns, 1024, 1024),
    ):
        rows = pl.ds(start, size)
        loads.append(pltpu.make_async_copy(source.at[rows], target.at[rows], load_sems.at[len(loads)]))
        loads[-1].start()

    def matrix(start, size, first=0, width=512):
        return matrices.at[pl.ds(start, size), pl.ds(first, width)]

    y_high, y_low = matrix(0, 256), matrix(256, 256)
    spread_map, curl_map = matrix(512, 256, 0, 256), matrix(512, 256, 256, 256)
    x_high, x_low = matrix(768, 256), matrix(1024, 256)
    xt_high, xt_low = matrix(1280, 512, 0, 256), matrix(1280, 512, 256, 256)
    fore_high_c, fore_low_c, back_c = (matrix(*rows, 0, 256) for rows in ((1792, 256), (2048, 128), (2176, 256)))
    fore_high_f, fore_low_f, back_f = (matrix(*rows, 256, 256) for rows in ((1792, 256), (2048, 128), (2176, 256)))
    finish_map, spread_map_f = matrix(2432, 256, 0, 256), matrix(2432, 256, 256, 256)
    place_map, finish_map_f = matrix(2688, 256, 0, 384), matrix(2688, 256, 384, 128)
    turn_xc_c, turn_xs_c, turn_yc_c, turn_ys_c, turn_xc_f, turn_xs_f, turn_yc_f, turn_ys_f = (
        turns.at[pl.ds(start, ROWS), :] for start in range(0, 8 * ROWS, ROWS)
    )
    rank = lax.axis_index("tm")
    at_y, at_pz = lax.axis_index("py"), lax.axis_index("pz")
    low_z, core, high_z, at_x = rank // 2, rank % 2, at_pz // 4, at_pz % 4
    place = at_y * 8 + at_pz
    duty = high_z * 2 + core
    spot = at_y * 8 + low_z * 4 + at_x
    alone = high_z == low_z
    partner = (duty, at_y, low_z * 4 + at_x)

    barrier = pltpu.get_barrier_semaphore()
    number = rank * GROUP + place

    def greet(step, carry):
        other = (number + step) % (4 * GROUP)
        target = (other // GROUP, (other // 8) % 4, other % 8)
        pl.semaphore_signal(barrier, inc=1, device_id=target, device_id_type=MESH)
        return carry

    lax.fori_loop(1, 4 * GROUP, greet, 0)

    def block(position):
        return pl.ds(pl.multiple_of(position * 8, 8), 8)

    spots_y = [(at_y + step) % 4 for step in range(4)]
    spots_x = [(at_x + step) % 4 for step in range(4)]
    duty_z = [(low_z + step) % 2 for step in range(2)]
    rank_z = [(high_z + step) % 2 for step in range(2)]

    def spot_of(steps, step):
        spot_y, spot_x = spots_y[step[0]], spots_x[step[2]]
        if steps is DUTY:
            spot_z = duty_z[step[1]]
            address = lambda group: (spot_z * 2 + group % 2, spot_y, (group // 2) * 4 + spot_x)
        else:
            spot_z = rank_z[step[1]]
            address = lambda group: (group, spot_y, spot_z * 4 + spot_x)
        return spot_y * 8 + spot_z * 4 + spot_x, address

    def post(source, target, sent, got, steps, group, mine, count):
        for step in steps[:count]:
            index, address = spot_of(steps, step)
            pltpu.make_async_remote_copy(
                src_ref=source.at[block(index)],
                dst_ref=target.at[block(mine)],
                send_sem=sent,
                recv_sem=got,
                device_id=address(group),
                device_id_type=MESH,
            ).start()

    def post_own(source, target, sent, got, steps, group, mine):
        post(source, target, sent, got, steps, group, mine, GROUP - 1)
        pltpu.make_async_copy(source.at[block(mine)], target.at[block(mine)], got).start()

    def post_other(source, target, sent, got, steps, group, mine):
        post(source, target, sent, got, steps, group, mine, GROUP - 1)
        index, address = spot_of(steps, steps[-1])

        @pl.when(alone)
        def _():
            pltpu.make_async_copy(source.at[block(index)], target.at[block(mine)], got).start()

        @pl.when(jnp.logical_not(alone))
        def _():
            pltpu.make_async_remote_copy(
                src_ref=source.at[block(index)],
                dst_ref=target.at[block(mine)],
                send_sem=sent,
                recv_sem=got,
                device_id=address(group),
                device_id_type=MESH,
            ).start()

    def send_one(source, target, sent, got, address):
        return pltpu.make_async_remote_copy(
            src_ref=source, dst_ref=target, send_sem=sent, recv_sem=got, device_id=address, device_id_type=MESH
        )

    def to_partner(source, target, sent, got):
        @pl.when(alone)
        def _():
            pltpu.make_async_copy(source, target, got).start()

        @pl.when(jnp.logical_not(alone))
        def _():
            send_one(source, target, sent, got, partner).start()

    def receive(target, got):
        pltpu.make_async_copy(target, target, got).wait()

    def drain(source, sent, count):
        part = source.at[pl.ds(0, count * 8)]
        pltpu.make_async_copy(part, part, sent).wait()

    def drain_other(source, sent):
        @pl.when(alone)
        def _():
            drain(source, sent, GROUP - 1)

        @pl.when(jnp.logical_not(alone))
        def _():
            drain(source, sent, GROUP)

    place_f32, spot_f32 = place.astype(F32), spot.astype(F32)
    row = lax.broadcasted_iota(jnp.int32, (ROWS, LANES), 0)
    lane = lax.broadcasted_iota(jnp.int32, (ROWS, LANES), 1)

    def wave_tables(extent, mode_x, mode_y):
        wave_x, wave_y = UNIT * mode_x, UNIT * mode_y
        wave_sq = wave_x * wave_x + wave_y * wave_y
        anchor = (mode_x == 0) & (mode_y == 0)
        kept = (mode_x <= extent // 3) & (jnp.abs(mode_y) <= extent // 3) & ~anchor
        mask = jnp.where(kept, 1.0, 0.0).astype(F32)
        inverse = mask / jnp.where(anchor, 1.0, wave_sq)
        damp = 1.0 / (1.0 + HALF_STEP * VISCOSITY * wave_sq)
        return wave_x, wave_y, wave_sq, mask, inverse, damp

    def coarse_tables(position, same_ref, cross_ref, damp_ref):
        slot = (lane % 64) // 16
        mode_x = (lane % 8).astype(F32) * GROUP + position
        mode_y = (row - 256 * ((lane % 16) // 8)).astype(F32)
        wave_x, wave_y, wave_sq, mask, inverse, damp = wave_tables(EDGE // 2, mode_x, mode_y)
        same = jnp.where(slot == 2, mask, jnp.where(slot == 1, wave_x * wave_x, wave_y * wave_y) * inverse)
        same_ref[...] = same * (HALF_STEP * damp)
        cross_ref[...] = jnp.where(slot == 2, 0.0, -wave_x * wave_y * inverse) * (HALF_STEP * damp)
        damp_ref[...] = damp

    curl_y[...] = UNIT * (row - 256 * ((lane % 16) // 8)).astype(F32)

    def coarse_tile(ref, base, scale, target):
        for half in range(2):
            pieces = []
            for part in range(2):
                for component in (0, 1, 2, 0):
                    for quarter in (0, 3):
                        start = base + part * 384 + component * 8 + 2 * quarter + half
                        pieces.append(ref[pl.ds(start, 8, stride=24), :])
            target[pl.ds(half * 128, 128), :] = scale * jnp.concatenate(pieces, axis=0).T

    def fine_tile(ref, component, target):
        for half in range(2):
            pieces = []
            for part in range(2):
                for quarter in range(4):
                    start = part * 384 + component * 8 + 2 * quarter + half
                    pieces.append(ref[pl.ds(start, 16, stride=24), :])
            target[pl.ds(half * 128, 128), tile(component)] = jnp.concatenate(pieces, axis=0).T

    def y_product(first, count, target):
        part = pl.ds(first * LANES, count * LANES)
        high, low = rhs_high[:, part], rhs_low[:, part]
        target[...] = dot(y_high[...], high) + dot(y_high[...], low) + dot(y_low[...], high)

    def pair(high, low):
        return jnp.concatenate([high, low], axis=1)

    def twisted(rows, index, value, value_turned, cosine, sine):
        stack(rows, index, value * cosine + value_turned * sine, value_turned * cosine - value * sine)

    def stack(rows, index, first, second):
        high, low = split(first)
        rhs_high[rows, tile(index)] = high
        rhs_low[rows, tile(index)] = low
        high, low = split(second)
        lower = pl.ds(rows.start + ROWS, rows.size)
        rhs_high[lower, tile(index)] = high
        rhs_low[lower, tile(index)] = low

    def spread_coarse(source, target, position):
        lanes = lax.broadcasted_iota(jnp.int32, (1, LANES), 1) % 8
        mode_x = lanes.astype(F32) * GROUP + position
        weight = jnp.where(mode_x == 0, 0.5, 1.0)
        for rows in chunks(128):
            velocity = source[rows, :] * weight
            high_y, low_y = split(velocity * curl_y[rows, :])
            high_x, low_x = split(velocity * (UNIT * mode_x))
            mixed = dot(pair(*split(velocity)), spread_map[...])
            curled = dot(pair(high_y, high_x), curl_map[...]) + dot(pair(low_y, low_x), curl_map[...])
            cosine, sine = turn_yc_c[rows, :], turn_ys_c[rows, :]
            twisted(rows, 0, mixed[:, :LANES], mixed[:, LANES:], cosine, sine)
            twisted(rows, 1, curled[:, LANES:], -curled[:, :LANES], cosine, sine)
        y_product(0, 2, target)

    def to_grid(source, first, fore_high, fore_low, cosine, sine):
        every = pl.ds(0, ROWS)
        for index in range(2):
            high, low = split(source[:, tile(index)])
            inner = dot(pair(high, low), fore_high[...]) + dot(high, fore_low[...])
            real, imag = inner[:, :LANES], inner[:, LANES:]
            stack(every, first + index, real * cosine - imag * sine, real * sine + imag * cosine)
        part = pl.ds(first * LANES, 2 * LANES)
        high, low = rhs_high[:, part], rhs_low[:, part]
        grid_buf[:, part] = dot(x_high[...], high) + dot(x_high[...], low) + dot(x_low[...], high)

    def from_grid(value, target, back, cosine, sine):
        high, low = split(value)
        both = dot(xt_high[...], pair(high, low))
        outer = both[:, :LANES] + both[:, LANES:] + dot(xt_low[...], high)
        real, imag = outer[:ROWS], outer[ROWS:]
        high, low = split(pair(real * cosine + imag * sine, imag * cosine - real * sine))
        both = dot(high, back[...])
        target[...] = both[:, :LANES] + both[:, LANES:] + dot(low, back[:, :LANES])

    def grid_coarse(source, target):
        cosine, sine = turn_xc_c[...], turn_xs_c[...]
        to_grid(source, 0, fore_high_c, fore_low_c, cosine, sine)
        speed, spin = grid_buf[:, tile(0)], grid_buf[:, tile(1)]
        crossed = speed * roll(spin, -32) - roll(speed, -32) * spin
        from_grid(crossed, target, back_c, cosine, sine)

    def finish_coarse(source, start_ref, right_ref, target, same_ref, cross_ref, damp_ref):
        for rows in chunks(128):
            value = source[rows, :]
            other = turned(value)
            stack(rows, 0, value, -other)
            stack(rows, 1, other, value)
        y_product(0, 2, grid_buf.at[:, pl.ds(0, 2 * LANES)])
        for rows in chunks(128):
            value = grid_buf[rows, tile(0)] * turn_yc_c[rows, :] - grid_buf[rows, tile(1)] * turn_ys_c[rows, :]
            modes = dot(pair(*split(value)), finish_map[...])
            term = same_ref[rows, :] * modes[:, :LANES] + cross_ref[rows, :] * modes[:, LANES:]
            target[rows, :] = damp_ref[rows, :] * (start_ref[rows, :] + right_ref[rows, :]) + term

    loads[0].wait()
    coarse_tile(state_ref, 0, 0.5, parcel_send.at[0])
    loads[1].wait()
    loads[2].wait()

    @pl.when(rank == 0)
    def _():
        spread_coarse(parcel_send.at[0], fore_send.at[0], place_f32)

    pl.semaphore_wait(barrier, 4 * GROUP - 1)

    @pl.when(rank == 0)
    def _():
        post_other(fore_send.at[0], fore_recv.at[0], fore_sent.at[0], fore_got.at[0], DUTY, 0, place)

    def combine(a, carry):
        wave_x = UNIT * (a.astype(F32) * GROUP + place_f32)
        sub = lax.broadcasted_iota(jnp.int32, (8, LANES), 0)
        mode = sub * 128 + lax.broadcasted_iota(jnp.int32, (8, LANES), 1)
        wave_y = UNIT * jnp.where(mode < EDGE // 2, mode, mode - EDGE).astype(F32)
        stiff = VISCOSITY * (wave_x * wave_x + wave_y * wave_y)
        for part in range(2):
            for component in range(3):
                base = pl.multiple_of(a * 24 + (part * 384 + component * 8), 8)
                rows = pl.ds(base, 8)
                states = [state_ref[pl.ds(base + node * 768, 8), :] for node in range(3)]
                terms = [terms_ref[pl.ds(base + node * 768, 8), :] for node in range(3)]
                one = sum(w * s for w, s in zip(STATE_ONE, states))
                two = sum(w * s for w, s in zip(STATE_TWO, states))
                mix_one[rows, :] = one
                mix_two[rows, :] = two
                right_one[rows, :] = sum(w * t for w, t in zip(TERM_ONE, terms)) + stiff * one
                right_two[rows, :] = sum(w * t for w, t in zip(TERM_TWO, terms)) + stiff * two
                start_send[rows, :] = states[2] + HALF_STEP * terms[2]
        return carry

    for index in (3, 4, 5, 6):
        loads[index].wait()
    lax.fori_loop(0, 16, combine, 0, unroll=2)

    following = (rank + 1, at_y, at_pz)

    @pl.when(rank < 3)
    def _():
        send_one(start_send, start_recv, start_sems.at[0], start_sems.at[1], following).start()

    coarse_tile(right_one, 0, 0.5, parcel_send.at[1])
    coarse_tile(right_two, 0, 0.5, parcel_send.at[2])
    to_partner(parcel_send, parcel_recv, parcel_sems.at[0], parcel_sems.at[1])
    coarse_tables(spot_f32, keep_same, keep_cross, damp_c)

    def coarse_sweep():
        receive(fore_recv.at[0], fore_got.at[0])
        grid_coarse(fore_recv.at[0], back_send.at[0])
        post_own(back_send.at[0], back_recv.at[0], back_sent.at[0], back_got.at[0], DUTY, duty, spot)
        receive(parcel_recv, parcel_sems.at[1])

        @pl.when(duty == 0)
        def _():
            sweep[0] = parcel_recv[0]

        @pl.when(duty > 0)
        def _():
            receive(hand_recv, hand_sems.at[1])
            sweep[0] = hand_recv[...]

        receive(back_recv.at[0], back_got.at[0])
        tables = (keep_same, keep_cross, damp_c)
        finish_coarse(back_recv.at[0], sweep.at[0], parcel_recv.at[1], sweep.at[1], *tables)
        spread_coarse(sweep.at[1], fore_send.at[1], spot_f32)
        post_own(fore_send.at[1], fore_recv.at[1], fore_sent.at[1], fore_got.at[1], DUTY, duty, spot)
        to_partner(sweep.at[pl.ds(0, 2)], news.at[pl.ds(0, 2)], news_sent.at[0], news_got.at[0])
        receive(fore_recv.at[1], fore_got.at[1])
        grid_coarse(fore_recv.at[1], back_send.at[1])

        @pl.when(duty == 3)
        def _():
            post_other(back_send.at[1], last_recv, back_sent.at[1], back_got.at[2], RANK, 3, spot)

        @pl.when(duty < 3)
        def _():
            post_own(back_send.at[1], back_recv.at[1], back_sent.at[1], back_got.at[1], DUTY, duty, spot)
            receive(back_recv.at[1], back_got.at[1])
            finish_coarse(back_recv.at[1], sweep.at[1], parcel_recv.at[2], sweep.at[2], *tables)
            spread_coarse(sweep.at[2], fore_send.at[2], spot_f32)
            after = duty + 1
            post(fore_send.at[2], fore_recv.at[0], fore_sent.at[2], fore_got.at[0], DUTY, after, spot, GROUP)
            address = (low_z * 2 + after % 2, at_y, (after // 2) * 4 + at_x)
            send_one(sweep.at[2], hand_recv, hand_sems.at[0], hand_sems.at[1], address).start()
            to_partner(sweep.at[2], news.at[2], news_sent.at[1], news_got.at[1])

    coarse_tile(mix_one, 0, 0.5, old_one)
    coarse_tile(mix_two, 0, 0.5, old_two)
    quarter = (lane % 64) // 16
    mode_x = (lane % 16).astype(F32) * GROUP + place_f32
    mode_y = (row + 256 * quarter - jnp.where(quarter >= 2, EDGE, 0)).astype(F32)
    wave_x, wave_y, wave_sq, mask, inverse, damp = wave_tables(EDGE, mode_x, mode_y)
    ky_f[...] = wave_y
    damp_f[...] = damp
    stiff_f[...] = (2.0 * VISCOSITY) * wave_sq
    same_x[...] = wave_y * wave_y * inverse
    same_y[...] = wave_x * wave_x * inverse
    cross_f[...] = -wave_x * wave_y * inverse
    mask_f[...] = mask
    weight = jnp.where(mode_x == 0, 0.5, 1.0)
    cos_f[...] = turn_yc_f[...] * weight
    sin_f[...] = turn_ys_f[...] * weight

    @pl.when(rank == 3)
    def _():
        coarse_tables(place_f32, keep_same_r, keep_cross_r, damp_r)

    def correct_fine():
        for rows in chunks(128):
            nodes = [news[node, rows, :] for node in range(3)]
            change_one = sum(w * n for w, n in zip(STATE_ONE, nodes)) - old_one[rows, :]
            change_two = sum(w * n for w, n in zip(STATE_TWO, nodes)) - old_two[rows, :]
            placed_one = dot(pair(*split(change_one)), place_map[...])
            placed_two = dot(pair(*split(change_two)), place_map[...])
            stiff, damping = stiff_f[rows, :], damp_f[rows, :]
            for component in range(3):
                part = tile(component)
                lanes = slice(component * LANES, (component + 1) * LANES)
                node_f[rows, part] = (right_one_f[rows, part] + stiff * placed_one[:, lanes]) * damping
                right_two_f[rows, part] = right_two_f[rows, part] + stiff * placed_two[:, lanes]

    def fine_field(index, rows):
        x, y, z = (node_f.at[rows, tile(component)] for component in range(3))
        if index < 3:
            return (x, y, z)[index][...]
        ky = ky_f[rows, :]
        kx = UNIT * ((lanes_like(ky) % 16).astype(F32) * GROUP + place_f32)
        if index == 3:
            return ky * z[...]
        if index == 4:
            return -kx * z[...]
        return kx * y[...] - ky * x[...]

    def spread_fine(first):
        for rows in chunks(128):
            cosine, sine = cos_f[rows, :], sin_f[rows, :]
            for index in (first, first + 1):
                mixed = dot(pair(*split(fine_field(index, rows))), spread_map_f[...])
                if index < 3:
                    twisted(rows, index, mixed[:, :LANES], mixed[:, LANES:], cosine, sine)
                else:
                    twisted(rows, index, mixed[:, LANES:], -mixed[:, :LANES], cosine, sine)
        y_product(first, 2, fine_send.at[first // 2])

    def give_back(source, component, target, base):
        for half in range(2):
            block_t = source[pl.ds(half * 128, 128), tile(component)].T
            for part in range(2):
                for quarter in range(4):
                    start = base + part * 384 + component * 8 + 2 * quarter + half
                    first = (part * 4 + quarter) * 16
                    target[pl.ds(start, 16, stride=24), :] = block_t[first : first + 16]

    def give_back_coarse(source, base):
        for half in range(2):
            block_t = source[pl.ds(half * 128, 128), :].T
            for part in range(2):
                for component in range(3):
                    for quarter in range(2):
                        start = base + part * 96 + component * 4 + 2 * quarter + half
                        first = part * 64 + component * 16 + quarter * 8
                        coarse_out[pl.ds(start, 8, stride=12), :] = block_t[first : first + 8]

    def cross_fine(component):
        second, third = (component + 1) % 3, (component + 2) % 3
        fields = [grid_buf[:, tile(index)] for index in (second, third, second + 3, third + 3)]
        return fields[0] * fields[3] - fields[1] * fields[2]

    def gather_fine(component):
        for rows in chunks(128):
            value = fine_back_recv[component, rows, :]
            stack(rows, component, value, -turned(value))
        y_product(component, 1, grid_buf.at[:, tile(component)])
        for rows in chunks(128):
            value = grid_buf[rows, tile(component)]
            value = value * turn_yc_f[rows, :] - turned(value) * turn_ys_f[rows, :]
            right_one_f[rows, tile(component)] = dot(pair(*split(value)), finish_map_f[...])

    def finish_fine():
        for rows in chunks(64):
            modes = [right_one_f[rows, tile(component)] for component in range(3)]
            cross = cross_f[rows, :]
            results = [
                same_x[rows, :] * modes[0] + cross * modes[1],
                same_y[rows, :] * modes[1] + cross * modes[0],
                mask_f[rows, :] * modes[2],
            ]
            for component, value in enumerate(results):
                part = tile(component)
                right_one_f[rows, part] = value
                total = node_f[rows, part] + HALF_STEP * value + right_two_f[rows, part]
                node_f[rows, part] = total * damp_f[rows, :]

    def fine_sweep():
        @pl.when(rank == 0)
        def _():
            first = pl.ds(0, 768)
            right_one[...] = right_one[...] + state_ref[first, :] + HALF_STEP * terms_ref[first, :]

        @pl.when(rank > 0)
        def _():
            receive(start_recv, start_sems.at[1])
            right_one[...] = right_one[...] + start_recv[...]

        for component in range(3):
            fine_tile(right_one, component, right_one_f)
            fine_tile(right_two, component, right_two_f)
        receive(news.at[pl.ds(0, 2)], news_got.at[0])

        @pl.when(rank < 3)
        def _():
            receive(news.at[2], news_got.at[1])

        @pl.when(rank == 3)
        def _():
            receive(last_recv, back_got.at[2])
            tables = (keep_same_r, keep_cross_r, damp_r)
            finish_coarse(last_recv, news.at[1], parcel_send.at[2], news.at[2], *tables)

        correct_fine()
        for part in range(3):
            spread_fine(2 * part)
            pairs = (fine_send.at[part], fine_recv.at[part], fine_sent.at[part], fine_got.at[part])
            post_own(*pairs, RANK, rank, place)
        give_back_coarse(news.at[1], 0)
        give_back_coarse(news.at[2], 192)
        for part in range(3):
            receive(fine_recv.at[part], fine_got.at[part])
            to_grid(fine_recv.at[part], 2 * part, fore_high_f, fore_low_f, turn_xc_f[...], turn_xs_f[...])
        for part in range(3):
            from_grid(cross_fine(part), fine_back_send.at[part], back_f, turn_xc_f[...], turn_xs_f[...])
            pairs = (fine_back_send.at[part], fine_back_recv.at[part])
            post_own(*pairs, fine_back_sent.at[part], fine_back_got.at[part], RANK, rank, place)
        for component in range(3):
            give_back(node_f, component, nodes_out, 0)
        for part in range(3):
            receive(fine_back_recv.at[part], fine_back_got.at[part])
            gather_fine(part)
        finish_fine()
        for component in range(3):
            give_back(right_one_f, component, term_out, 0)
            give_back(node_f, component, nodes_out, 768)

    early = high_z * (1 - low_z)

    def phase(step, carry):
        fine_now = (step + early) % 2

        @pl.when(fine_now == 0)
        def _():
            coarse_sweep()

        @pl.when(fine_now == 1)
        def _():
            fine_sweep()

        return carry

    lax.fori_loop(0, 2, phase, 0)

    @pl.when(rank == 0)
    def _():
        drain_other(fore_send.at[0], fore_sent.at[0])

    drain(fore_send.at[1], fore_sent.at[1], GROUP - 1)
    drain(back_send.at[0], back_sent.at[0], GROUP - 1)
    for part in range(3):
        drain(fine_send.at[part], fine_sent.at[part], GROUP - 1)
        drain(fine_back_send.at[part], fine_back_sent.at[part], GROUP - 1)

    @pl.when(duty == 3)
    def _():
        drain_other(back_send.at[1], back_sent.at[1])

    @pl.when(duty < 3)
    def _():
        drain(back_send.at[1], back_sent.at[1], GROUP - 1)
        drain(fore_send.at[2], fore_sent.at[2], GROUP)
        receive(sweep.at[2], hand_sems.at[0])

    @pl.when(jnp.logical_not(alone))
    def _():
        receive(parcel_send, parcel_sems.at[0])
        receive(sweep.at[pl.ds(0, 2)], news_sent.at[0])

        @pl.when(duty < 3)
        def _():
            receive(sweep.at[2], news_sent.at[1])

    @pl.when(rank < 3)
    def _():
        receive(start_send, start_sems.at[0])


def hand_out(*refs):
    sources, targets, sems = refs[:3], refs[3:6], refs[6]
    copies = []
    for source, target in zip(sources, targets):
        size = source.shape[0] // PIECES
        for piece in range(PIECES):
            rows = pl.ds(piece * size, size)
            copies.append(pltpu.make_async_copy(source.at[rows], target.at[rows], sems.at[len(copies)]))
    for copy in copies:
        copy.start()
    for copy in copies:
        copy.wait()


def shards(fine_state, fine_terms):
    matrices, turns = constant_tables()
    full, natural, wide = (ROWS, LANES), (768, LANES), (ROWS, 3 * LANES)
    dma = pltpu.SemaphoreType.DMA
    tiles = (3, ROWS, LANES)
    shapes = [(ROWS, 6 * LANES)]
    shapes += [(3, ROWS, 2 * LANES), (2, ROWS, 2 * LANES), (2, ROWS, LANES), (2, ROWS, LANES), full, full]
    shapes += [tiles] * 4 + [(3, ROWS, 2 * LANES)] * 2 + [tiles] * 2
    shapes += [natural] * 6 + [full] * (9 + 9) + [wide] * 3 + [(2304, LANES)] * 2
    scratch = [pltpu.VMEM((2 * ROWS, 6 * LANES), BF16)] * 2 + [pltpu.VMEM(shape, F32) for shape in shapes]
    scratch += [pltpu.VMEM(matrices.shape, BF16), pltpu.VMEM(turns.shape, F32)]
    scratch += [dma((count,)) for count in (3, 2, 2, 3, 2, 2, 2, 2, 3, 3, 3, 3, 2, 7)]
    outs = pl.pallas_call(
        iterate,
        out_shape=(
            jax.ShapeDtypeStruct((1536, LANES), F32),
            jax.ShapeDtypeStruct((768, LANES), F32),
            jax.ShapeDtypeStruct((384, LANES), F32),
        ),
        in_specs=[pl.BlockSpec(memory_space=pltpu.HBM)] * 4,
        out_specs=[pl.BlockSpec(memory_space=pltpu.VMEM)] * 3,
        scratch_shapes=scratch,
        compiler_params=pltpu.CompilerParams(
            collective_id=0, has_side_effects=True, vmem_limit_bytes=62 * 1024 * 1024
        ),
        name="iterate",
    )(fine_state.reshape(2304, LANES), fine_terms.reshape(2304, LANES), jnp.asarray(matrices), jnp.asarray(turns))
    outs = pl.pallas_call(
        hand_out,
        out_shape=[jax.ShapeDtypeStruct(out.shape, F32) for out in outs],
        in_specs=[pl.BlockSpec(memory_space=pltpu.VMEM)] * 3,
        out_specs=[pl.BlockSpec(memory_space=pl.ANY)] * 3,
        scratch_shapes=[dma((3 * PIECES,))],
        name="hand_out",
    )(*outs)
    return (
        outs[0].reshape(1, 2, 2, 16, 1, 3, 1, 1024),
        outs[1].reshape(1, 2, 16, 1, 3, 1, 1024),
        outs[2].reshape(1, 2, 2, 8, 1, 3, 1, 512),
    )


def solution(mesh):
    split_over = P("tm", None, None, None, ("py", "pz"), None, None, None)
    return jax.shard_map(
        shards,
        mesh=mesh,
        in_specs=(split_over, split_over),
        out_specs=(
            split_over,
            P("tm", None, None, ("py", "pz"), None, None, None),
            split_over,
        ),
        check_vma=False,
    )
```

```python
import math

import jax
import jax.numpy as jnp
import ml_dtypes
import numpy as np
from jax import lax
from jax.experimental import pallas as pl
from jax.experimental.pallas import tpu as pltpu
from jax.sharding import PartitionSpec as P

EDGE = 1024
VISCOSITY = 0.5
TIME_STEP = 0.2
HALF_STEP = 0.5 * TIME_STEP
WEIGHTS = ((5.0 / 24.0, 1.0 / 3.0, -1.0 / 24.0), (-1.0 / 24.0, 1.0 / 3.0, 5.0 / 24.0))
UNIT = 2.0 * math.pi / EDGE
GROUP = 32
ROWS = 256
LANES = 128
PIECES = 4
F32 = jnp.float32
BF16 = jnp.bfloat16
MESH = pl.DeviceIdType.MESH
TERM_ONE = [TIME_STEP * w for w in WEIGHTS[0]]
TERM_ONE[0] -= HALF_STEP
TERM_TWO = [TIME_STEP * w for w in WEIGHTS[1]]
TERM_TWO[1] -= HALF_STEP
STATE_ONE = [-TIME_STEP * w for w in WEIGHTS[0]]
STATE_ONE[1] += HALF_STEP
STATE_TWO = [-TIME_STEP * w for w in WEIGHTS[1]]
STATE_TWO[2] += HALF_STEP


HOPS = (0, 1, 2, 1)
DUTY, RANK = (
    sorted(
        ((y, z, x) for y in range(4) for z in range(2) for x in range(4)),
        key=lambda step: -(HOPS[step[0]] + apart * step[1] + HOPS[step[2]]),
    )
    for apart in (1, 2)
)


def halves(table):
    high = table.astype(ml_dtypes.bfloat16)
    low = (table - high.astype(np.float64)).astype(ml_dtypes.bfloat16)
    return high, low


def lane_circle(extent):
    inner = extent // GROUP
    modes = inner // 2
    pairs = 64 // modes
    fore = np.zeros((2, pairs, modes, 2, pairs, inner))
    back = np.zeros((2, pairs, inner, 2, pairs, modes))
    phase = 2.0 * math.pi * np.outer(np.arange(modes), np.arange(inner)) / inner
    kept = (np.arange(modes) * GROUP <= extent // 3)[None, :]
    for pair in range(pairs):
        cosine, sine = 2.0 / extent * np.cos(phase), 2.0 / extent * np.sin(phase)
        fore[0, pair, :, 0, pair] = cosine
        fore[1, pair, :, 0, pair] = -sine
        fore[0, pair, :, 1, pair] = sine
        fore[1, pair, :, 1, pair] = cosine
        target = pair
        sources = [(pair, pair)]
        if extent < EDGE:
            slot, rest = divmod(pair, 2)
            sources = [(((1, 2, 0, 1)[slot]) * 2 + rest, pair)]
        for source, target in sources:
            cosine = 1.0 / extent * np.cos(phase).T * kept
            sine = 1.0 / extent * np.sin(phase).T * kept
            back[0, source, :, 0, target] = cosine
            back[1, source, :, 0, target] = sine
            back[0, source, :, 1, target] = -sine
            back[1, source, :, 1, target] = cosine
    fore = fore.reshape(128, 256)
    back = back.reshape(256, 128)
    return fore, back


def real_form(table):
    return np.block([[table.real, table.imag], [-table.imag, table.real]])


def doubled(table):
    return np.concatenate([table, table], axis=0)


def lane_maps():
    sign = np.array([[1.0, 1.0], [1.0, -1.0]])
    curl_y, curl_x, partner = np.zeros((4, 4)), np.zeros((4, 4)), np.zeros((4, 4))
    curl_y[2, 0] = curl_y[2, 3] = 1.0
    curl_y[0, 2] = -1.0
    curl_x[2, 1] = -1.0
    curl_x[1, 2] = 1.0
    partner[1, 0] = partner[1, 3] = partner[0, 1] = 1.0

    def coarse(slots):
        table = np.kron(np.kron(slots, sign), np.eye(8)).astype(complex)
        return real_form(table), real_form(1j * table)

    same = coarse(np.eye(4))
    spread_c = doubled(np.concatenate(same, axis=1))
    curl_c = np.concatenate([np.concatenate(coarse(slots), axis=1) for slots in (curl_y, curl_x)], axis=0)
    finish_c = doubled(np.concatenate([same[0], coarse(partner)[0]], axis=1))
    quarters, powers = np.arange(4), np.array([0, 2, 1, 3])
    table = np.kron(1j ** (np.outer(quarters, powers) % 4), np.eye(16))
    spread_f = doubled(np.concatenate([real_form(table), real_form(1j * table)], axis=1))
    finish_f = doubled(real_form(np.conj(table).T))
    place = np.zeros((3, 4, 2, 8, 4, 16))
    for component in range(3):
        for a in range(8):
            place[component, component, 0, a, 0, a] = 1.0
            place[component, component, 1, a, 3, a] = 1.0
    place_f = doubled(np.concatenate([real_form(table.reshape(64, 64).astype(complex)) for table in place], axis=1))
    return [
        np.concatenate(pair, axis=1).astype(ml_dtypes.bfloat16)
        for pair in ((spread_c, curl_c), (finish_c, spread_f), (place_f, finish_f))
    ]


def constant_tables():
    index = np.arange(ROWS)
    phase = 2.0 * math.pi * np.outer(np.arange(ROWS // 2) + 0.5, index) / ROWS
    along_y = np.concatenate([np.cos(phase), np.sin(phase)], axis=1)
    back_y = np.concatenate([np.cos(phase).T, np.sin(phase).T], axis=1)
    small = 2.0 * math.pi * np.outer(np.arange(GROUP) + 0.5, np.arange(GROUP)) / GROUP
    along_x = np.concatenate([np.cos(small), -np.sin(small)], axis=1).reshape(GROUP, 2, GROUP)
    half = GROUP // 2
    order = np.stack([np.arange(half), GROUP - 1 - np.arange(half)], axis=1).reshape(-1)
    back_x = np.kron(along_x[order].transpose(1, 2, 0).reshape(2 * GROUP, GROUP), np.eye(8))
    along_x = np.kron(along_x[:half].reshape(half, 2 * GROUP), np.eye(8))
    maps = lane_maps()
    matrices = list(halves(along_y)) + [np.concatenate(halves(back_y), axis=1), maps[0]]
    matrices += list(halves(along_x)) + [np.concatenate(halves(back_x), axis=1)]
    lane = np.arange(LANES)
    turns, inner_parts = [], []
    for extent in (EDGE // 2, EDGE):
        fore, back = lane_circle(extent)
        fore_high, fore_low = halves(fore)
        back_high, back_low = halves(back)
        inner_parts.append(
            np.concatenate([fore_high, fore_high, fore_low, np.concatenate([back_high, back_low], axis=1)], axis=0)
        )
        inner = extent // GROUP
        turn = 2.0 * math.pi * np.outer(index // 8, lane % inner / extent - 0.5 / GROUP)
        turns += [np.cos(turn), np.sin(turn)]
        if extent < EDGE:
            offset = (lane % 16) // 8
        else:
            offset = np.array([0, 2, 1, 3])[(lane % 64) // 16]
        turn = 2.0 * math.pi * np.outer(index, offset / extent - 0.5 / ROWS)
        turns += [np.cos(turn), np.sin(turn)]
    matrices.append(np.concatenate(inner_parts, axis=1))
    matrices += maps[1:]
    return np.concatenate(matrices, axis=0), np.concatenate(turns, axis=0).astype(np.float32)


def split(value):
    high = value.astype(BF16)
    return high, (value - high.astype(F32)).astype(BF16)


def dot(left, right):
    return jnp.dot(left, right, preferred_element_type=F32)


def roll(value, shift):
    return pltpu.roll(value, shift % LANES, axis=1)


def lanes_like(value):
    return lax.broadcasted_iota(jnp.int32, value.shape, 1)


def turned(value):
    other = roll(value, 64)
    return jnp.where(lanes_like(value) < 64, -other, other)


def tile(index):
    return pl.ds(index * LANES, LANES)


def chunks(size):
    return [pl.ds(start, size) for start in range(0, ROWS, size)]


def iterate(
    state_hbm, terms_hbm, matrices_hbm, turns_hbm,
    nodes_out, term_out, coarse_out,
    rhs_high, rhs_low, grid_buf,
    fore_send, fore_recv, back_send, back_recv, last_recv, hand_recv,
    parcel_send, parcel_recv, sweep, news,
    fine_send, fine_recv, fine_back_send, fine_back_recv, start_send, start_recv,
    right_one, right_two, mix_one, mix_two,
    curl_y, keep_same, keep_cross, damp_c, keep_same_r, keep_cross_r, damp_r, old_one, old_two,
    ky_f, damp_f, stiff_f, cos_f, sin_f, same_x, same_y, cross_f, mask_f,
    right_one_f, right_two_f, node_f,
    state_ref, terms_ref, matrices, turns,
    fore_sent, fore_got, back_sent, back_got, hand_sems, parcel_sems, news_sent, news_got,
    fine_sent, fine_got, fine_back_sent, fine_back_got, start_sems, load_sems,
):
    loads = []
    for source, target, start, size in (
        (state_hbm, state_ref, 0, 768),
        (matrices_hbm, matrices, 0, 768),
        (turns_hbm, turns, 0, 1024),
        (state_hbm, state_ref, 768, 1536),
        (terms_hbm, terms_ref, 0, 2304),
        (matrices_hbm, matrices, 768, 1920),
        (turns_hbm, turns, 1024, 1024),
    ):
        rows = pl.ds(start, size)
        loads.append(pltpu.make_async_copy(source.at[rows], target.at[rows], load_sems.at[len(loads)]))
        loads[-1].start()

    def matrix(start, size, first=0, width=512):
        return matrices.at[pl.ds(start, size), pl.ds(first, width)]

    y_halves = (matrix(0, 256, 0, 256), matrix(0, 256, 256, 256))
    yt_high, yt_low = matrix(256, 256, 0, 256), matrix(256, 256, 256, 256)
    spread_map, curl_map = matrix(512, 256, 0, 256), matrix(512, 256, 256, 256)
    x_halves = (matrix(768, 256, 0, 256), matrix(768, 256, 256, 256))
    xt_high, xt_low = matrix(1024, 512, 0, 256), matrix(1024, 512, 256, 256)
    fore_high_c, fore_low_c, back_c = (matrix(*rows, 0, 256) for rows in ((1536, 256), (1792, 128), (1920, 256)))
    fore_high_f, fore_low_f, back_f = (matrix(*rows, 256, 256) for rows in ((1536, 256), (1792, 128), (1920, 256)))
    finish_map, spread_map_f = matrix(2176, 256, 0, 256), matrix(2176, 256, 256, 256)
    place_map, finish_map_f = matrix(2432, 256, 0, 384), matrix(2432, 256, 384, 128)
    turn_xc_c, turn_xs_c, turn_yc_c, turn_ys_c, turn_xc_f, turn_xs_f, turn_yc_f, turn_ys_f = (
        turns.at[pl.ds(start, ROWS), :] for start in range(0, 8 * ROWS, ROWS)
    )
    rank = lax.axis_index("tm")
    at_y, at_pz = lax.axis_index("py"), lax.axis_index("pz")
    low_z, core, high_z, at_x = rank // 2, rank % 2, at_pz // 4, at_pz % 4
    place = at_y * 8 + at_pz
    duty = high_z * 2 + core
    spot = at_y * 8 + low_z * 4 + at_x
    alone = high_z == low_z
    partner = (duty, at_y, low_z * 4 + at_x)

    barrier = pltpu.get_barrier_semaphore()
    number = rank * GROUP + place

    def greet(step, carry):
        other = (number + step) % (4 * GROUP)
        target = (other // GROUP, (other // 8) % 4, other % 8)
        pl.semaphore_signal(barrier, inc=1, device_id=target, device_id_type=MESH)
        return carry

    lax.fori_loop(1, 4 * GROUP, greet, 0)

    def block(position):
        return pl.ds(pl.multiple_of(position * 8, 8), 8)

    spots_y = [(at_y + step) % 4 for step in range(4)]
    spots_x = [(at_x + step) % 4 for step in range(4)]
    duty_z = [(low_z + step) % 2 for step in range(2)]
    rank_z = [(high_z + step) % 2 for step in range(2)]

    def spot_of(steps, step):
        spot_y, spot_x = spots_y[step[0]], spots_x[step[2]]
        if steps is DUTY:
            spot_z = duty_z[step[1]]
            address = lambda group: (spot_z * 2 + group % 2, spot_y, (group // 2) * 4 + spot_x)
        else:
            spot_z = rank_z[step[1]]
            address = lambda group: (group, spot_y, spot_z * 4 + spot_x)
        return spot_y * 8 + spot_z * 4 + spot_x, address

    def post(source, target, sent, got, steps, group, mine, count):
        for step in steps[:count]:
            index, address = spot_of(steps, step)
            pltpu.make_async_remote_copy(
                src_ref=source.at[block(index)],
                dst_ref=target.at[block(mine)],
                send_sem=sent,
                recv_sem=got,
                device_id=address(group),
                device_id_type=MESH,
            ).start()

    def post_own(source, target, sent, got, steps, group, mine):
        post(source, target, sent, got, steps, group, mine, GROUP - 1)
        pltpu.make_async_copy(source.at[block(mine)], target.at[block(mine)], got).start()

    def post_other(source, target, sent, got, steps, group, mine):
        post(source, target, sent, got, steps, group, mine, GROUP - 1)
        index, address = spot_of(steps, steps[-1])

        @pl.when(alone)
        def _():
            pltpu.make_async_copy(source.at[block(index)], target.at[block(mine)], got).start()

        @pl.when(jnp.logical_not(alone))
        def _():
            pltpu.make_async_remote_copy(
                src_ref=source.at[block(index)],
                dst_ref=target.at[block(mine)],
                send_sem=sent,
                recv_sem=got,
                device_id=address(group),
                device_id_type=MESH,
            ).start()

    def send_one(source, target, sent, got, address):
        return pltpu.make_async_remote_copy(
            src_ref=source, dst_ref=target, send_sem=sent, recv_sem=got, device_id=address, device_id_type=MESH
        )

    def to_partner(source, target, sent, got):
        @pl.when(alone)
        def _():
            pltpu.make_async_copy(source, target, got).start()

        @pl.when(jnp.logical_not(alone))
        def _():
            send_one(source, target, sent, got, partner).start()

    def receive(target, got):
        pltpu.make_async_copy(target, target, got).wait()

    def drain(source, sent, count):
        part = source.at[pl.ds(0, count * 8)]
        pltpu.make_async_copy(part, part, sent).wait()

    def drain_other(source, sent):
        @pl.when(alone)
        def _():
            drain(source, sent, GROUP - 1)

        @pl.when(jnp.logical_not(alone))
        def _():
            drain(source, sent, GROUP)

    place_f32, spot_f32 = place.astype(F32), spot.astype(F32)
    row = lax.broadcasted_iota(jnp.int32, (ROWS, LANES), 0)
    lane = lax.broadcasted_iota(jnp.int32, (ROWS, LANES), 1)

    def wave_tables(extent, mode_x, mode_y):
        wave_x, wave_y = UNIT * mode_x, UNIT * mode_y
        wave_sq = wave_x * wave_x + wave_y * wave_y
        anchor = (mode_x == 0) & (mode_y == 0)
        kept = (mode_x <= extent // 3) & (jnp.abs(mode_y) <= extent // 3) & ~anchor
        mask = jnp.where(kept, 1.0, 0.0).astype(F32)
        inverse = mask / jnp.where(anchor, 1.0, wave_sq)
        damp = 1.0 / (1.0 + HALF_STEP * VISCOSITY * wave_sq)
        return wave_x, wave_y, wave_sq, mask, inverse, damp

    def coarse_tables(position, same_ref, cross_ref, damp_ref):
        slot = (lane % 64) // 16
        mode_x = (lane % 8).astype(F32) * GROUP + position
        mode_y = (row - 256 * ((lane % 16) // 8)).astype(F32)
        wave_x, wave_y, wave_sq, mask, inverse, damp = wave_tables(EDGE // 2, mode_x, mode_y)
        same = jnp.where(slot == 2, mask, jnp.where(slot == 1, wave_x * wave_x, wave_y * wave_y) * inverse)
        same_ref[...] = same * (HALF_STEP * damp)
        cross_ref[...] = jnp.where(slot == 2, 0.0, -wave_x * wave_y * inverse) * (HALF_STEP * damp)
        damp_ref[...] = damp

    curl_y[...] = UNIT * (row - 256 * ((lane % 16) // 8)).astype(F32)

    def coarse_tile(ref, base, scale, target):
        for half in range(2):
            pieces = []
            for part in range(2):
                for component in (0, 1, 2, 0):
                    for quarter in (0, 3):
                        start = base + part * 384 + component * 8 + 2 * quarter + half
                        pieces.append(ref[pl.ds(start, 8, stride=24), :])
            target[pl.ds(half * 128, 128), :] = scale * jnp.concatenate(pieces, axis=0).T

    def fine_tile(ref, component, target):
        for half in range(2):
            pieces = []
            for part in range(2):
                for quarter in range(4):
                    start = part * 384 + component * 8 + 2 * quarter + half
                    pieces.append(ref[pl.ds(start, 16, stride=24), :])
            target[pl.ds(half * 128, 128), tile(component)] = jnp.concatenate(pieces, axis=0).T

    def half_products(matrices_two, first, count, target):
        part = pl.ds(first * LANES, count * LANES)
        halves_two = []
        for index, both_parts in enumerate(matrices_two):
            rows = pl.ds(index * ROWS, ROWS)
            both = dot(both_parts[...], rhs_high[rows, part])
            rest = dot(both_parts[pl.ds(0, 128), :], rhs_low[rows, part])
            halves_two.append(both[:128] + both[128:] + rest)
        even, odd = halves_two
        total, difference = even + odd, even - odd
        for step in range(16):
            lines = slice(step * 8, step * 8 + 8)
            target[pl.ds(step * 16, 8), :] = total[lines]
            target[pl.ds(step * 16 + 8, 8), :] = difference[lines]

    def y_back(first, count):
        part = pl.ds(first * LANES, count * LANES)
        high, low = rhs_high[pl.ds(0, ROWS), part], rhs_low[pl.ds(0, ROWS), part]
        grid_buf[:, part] = dot(yt_high[...], high) + dot(yt_high[...], low) + dot(yt_low[...], high)

    def folded(value):
        mirrored = value.reshape(16, 2, 8, LANES)
        first, second = mirrored[:, 0].reshape(128, LANES), mirrored[:, 1].reshape(128, LANES)
        return first + second, first - second

    def stack_back(index, upper, lower):
        for start, value in ((0, upper), (128, lower)):
            high, low = split(value)
            rhs_high[pl.ds(start, 128), tile(index)] = high
            rhs_low[pl.ds(start, 128), tile(index)] = low

    def pair(high, low):
        return jnp.concatenate([high, low], axis=1)

    def twisted(rows, index, value, value_turned, cosine, sine):
        stack(rows, index, value * cosine + value_turned * sine, value_turned * cosine - value * sine)

    def stack(rows, index, first, second):
        high, low = split(first)
        rhs_high[rows, tile(index)] = high
        rhs_low[rows, tile(index)] = low
        high, low = split(second)
        lower = pl.ds(rows.start + ROWS, rows.size)
        rhs_high[lower, tile(index)] = high
        rhs_low[lower, tile(index)] = low

    def spread_coarse(source, target, position):
        lanes = lax.broadcasted_iota(jnp.int32, (1, LANES), 1) % 8
        mode_x = lanes.astype(F32) * GROUP + position
        weight = jnp.where(mode_x == 0, 0.5, 1.0)
        for rows in chunks(128):
            velocity = source[rows, :] * weight
            high_y, low_y = split(velocity * curl_y[rows, :])
            high_x, low_x = split(velocity * (UNIT * mode_x))
            mixed = dot(pair(*split(velocity)), spread_map[...])
            curled = dot(pair(high_y, high_x), curl_map[...]) + dot(pair(low_y, low_x), curl_map[...])
            cosine, sine = turn_yc_c[rows, :], turn_ys_c[rows, :]
            twisted(rows, 0, mixed[:, :LANES], mixed[:, LANES:], cosine, sine)
            twisted(rows, 1, curled[:, LANES:], -curled[:, :LANES], cosine, sine)
        half_products(y_halves, 0, 2, target)

    def to_grid(source, first, fore_high, fore_low, cosine, sine):
        every = pl.ds(0, ROWS)
        for index in range(2):
            high, low = split(source[:, tile(index)])
            inner = dot(pair(high, low), fore_high[...]) + dot(high, fore_low[...])
            real, imag = inner[:, :LANES], inner[:, LANES:]
            stack(every, first + index, real * cosine - imag * sine, real * sine + imag * cosine)
        part = pl.ds(first * LANES, 2 * LANES)
        half_products(x_halves, first, 2, grid_buf.at[:, part])

    def from_grid(value, target, back, cosine, sine):
        high, low = split(value)
        both = dot(xt_high[...], pair(high, low))
        outer = both[:, :LANES] + both[:, LANES:] + dot(xt_low[...], high)
        real, imag = outer[:ROWS], outer[ROWS:]
        high, low = split(pair(real * cosine + imag * sine, imag * cosine - real * sine))
        both = dot(high, back[...])
        target[...] = both[:, :LANES] + both[:, LANES:] + dot(low, back[:, :LANES])

    def grid_coarse(source, target):
        cosine, sine = turn_xc_c[...], turn_xs_c[...]
        to_grid(source, 0, fore_high_c, fore_low_c, cosine, sine)
        speed, spin = grid_buf[:, tile(0)], grid_buf[:, tile(1)]
        crossed = speed * roll(spin, -32) - roll(speed, -32) * spin
        from_grid(crossed, target, back_c, cosine, sine)

    def finish_coarse(source, start_ref, right_ref, target, same_ref, cross_ref, damp_ref):
        even, odd = folded(source[...])
        stack_back(0, even, -turned(odd))
        stack_back(1, turned(even), odd)
        y_back(0, 2)
        for rows in chunks(128):
            value = grid_buf[rows, tile(0)] * turn_yc_c[rows, :] - grid_buf[rows, tile(1)] * turn_ys_c[rows, :]
            modes = dot(pair(*split(value)), finish_map[...])
            term = same_ref[rows, :] * modes[:, :LANES] + cross_ref[rows, :] * modes[:, LANES:]
            target[rows, :] = damp_ref[rows, :] * (start_ref[rows, :] + right_ref[rows, :]) + term

    loads[0].wait()
    coarse_tile(state_ref, 0, 0.5, parcel_send.at[0])
    loads[1].wait()
    loads[2].wait()

    @pl.when(rank == 0)
    def _():
        spread_coarse(parcel_send.at[0], fore_send.at[0], place_f32)

    pl.semaphore_wait(barrier, 4 * GROUP - 1)

    @pl.when(rank == 0)
    def _():
        post_other(fore_send.at[0], fore_recv.at[0], fore_sent.at[0], fore_got.at[0], DUTY, 0, place)

    def combine(a, carry):
        wave_x = UNIT * (a.astype(F32) * GROUP + place_f32)
        sub = lax.broadcasted_iota(jnp.int32, (8, LANES), 0)
        mode = sub * 128 + lax.broadcasted_iota(jnp.int32, (8, LANES), 1)
        wave_y = UNIT * jnp.where(mode < EDGE // 2, mode, mode - EDGE).astype(F32)
        stiff = VISCOSITY * (wave_x * wave_x + wave_y * wave_y)
        for part in range(2):
            for component in range(3):
                base = pl.multiple_of(a * 24 + (part * 384 + component * 8), 8)
                rows = pl.ds(base, 8)
                states = [state_ref[pl.ds(base + node * 768, 8), :] for node in range(3)]
                terms = [terms_ref[pl.ds(base + node * 768, 8), :] for node in range(3)]
                one = sum(w * s for w, s in zip(STATE_ONE, states))
                two = sum(w * s for w, s in zip(STATE_TWO, states))
                mix_one[rows, :] = one
                mix_two[rows, :] = two
                right_one[rows, :] = sum(w * t for w, t in zip(TERM_ONE, terms)) + stiff * one
                right_two[rows, :] = sum(w * t for w, t in zip(TERM_TWO, terms)) + stiff * two
                start_send[rows, :] = states[2] + HALF_STEP * terms[2]
        return carry

    for index in (3, 4, 5, 6):
        loads[index].wait()
    lax.fori_loop(0, 16, combine, 0, unroll=2)

    following = (rank + 1, at_y, at_pz)

    @pl.when(rank < 3)
    def _():
        send_one(start_send, start_recv, start_sems.at[0], start_sems.at[1], following).start()

    coarse_tile(right_one, 0, 0.5, parcel_send.at[1])
    coarse_tile(right_two, 0, 0.5, parcel_send.at[2])
    to_partner(parcel_send, parcel_recv, parcel_sems.at[0], parcel_sems.at[1])
    coarse_tables(spot_f32, keep_same, keep_cross, damp_c)

    def coarse_sweep():
        receive(fore_recv.at[0], fore_got.at[0])
        grid_coarse(fore_recv.at[0], back_send.at[0])
        post_own(back_send.at[0], back_recv.at[0], back_sent.at[0], back_got.at[0], DUTY, duty, spot)
        receive(parcel_recv, parcel_sems.at[1])

        @pl.when(duty == 0)
        def _():
            sweep[0] = parcel_recv[0]

        @pl.when(duty > 0)
        def _():
            receive(hand_recv, hand_sems.at[1])
            sweep[0] = hand_recv[...]

        receive(back_recv.at[0], back_got.at[0])
        tables = (keep_same, keep_cross, damp_c)
        finish_coarse(back_recv.at[0], sweep.at[0], parcel_recv.at[1], sweep.at[1], *tables)
        spread_coarse(sweep.at[1], fore_send.at[1], spot_f32)
        post_own(fore_send.at[1], fore_recv.at[1], fore_sent.at[1], fore_got.at[1], DUTY, duty, spot)
        to_partner(sweep.at[pl.ds(0, 2)], news.at[pl.ds(0, 2)], news_sent.at[0], news_got.at[0])
        receive(fore_recv.at[1], fore_got.at[1])
        grid_coarse(fore_recv.at[1], back_send.at[1])

        @pl.when(duty == 3)
        def _():
            post_other(back_send.at[1], last_recv, back_sent.at[1], back_got.at[2], RANK, 3, spot)

        @pl.when(duty < 3)
        def _():
            post_own(back_send.at[1], back_recv.at[1], back_sent.at[1], back_got.at[1], DUTY, duty, spot)
            receive(back_recv.at[1], back_got.at[1])
            finish_coarse(back_recv.at[1], sweep.at[1], parcel_recv.at[2], sweep.at[2], *tables)
            spread_coarse(sweep.at[2], fore_send.at[2], spot_f32)
            after = duty + 1
            post(fore_send.at[2], fore_recv.at[0], fore_sent.at[2], fore_got.at[0], DUTY, after, spot, GROUP)
            address = (low_z * 2 + after % 2, at_y, (after // 2) * 4 + at_x)
            send_one(sweep.at[2], hand_recv, hand_sems.at[0], hand_sems.at[1], address).start()
            to_partner(sweep.at[2], news.at[2], news_sent.at[1], news_got.at[1])

    coarse_tile(mix_one, 0, 0.5, old_one)
    coarse_tile(mix_two, 0, 0.5, old_two)
    quarter = (lane % 64) // 16
    mode_x = (lane % 16).astype(F32) * GROUP + place_f32
    mode_y = (row + 256 * quarter - jnp.where(quarter >= 2, EDGE, 0)).astype(F32)
    wave_x, wave_y, wave_sq, mask, inverse, damp = wave_tables(EDGE, mode_x, mode_y)
    ky_f[...] = wave_y
    damp_f[...] = damp
    stiff_f[...] = (2.0 * VISCOSITY) * wave_sq
    same_x[...] = wave_y * wave_y * inverse
    same_y[...] = wave_x * wave_x * inverse
    cross_f[...] = -wave_x * wave_y * inverse
    mask_f[...] = mask
    weight = jnp.where(mode_x == 0, 0.5, 1.0)
    cos_f[...] = turn_yc_f[...] * weight
    sin_f[...] = turn_ys_f[...] * weight

    @pl.when(rank == 3)
    def _():
        coarse_tables(place_f32, keep_same_r, keep_cross_r, damp_r)

    def correct_fine():
        for rows in chunks(128):
            nodes = [news[node, rows, :] for node in range(3)]
            change_one = sum(w * n for w, n in zip(STATE_ONE, nodes)) - old_one[rows, :]
            change_two = sum(w * n for w, n in zip(STATE_TWO, nodes)) - old_two[rows, :]
            placed_one = dot(pair(*split(change_one)), place_map[...])
            placed_two = dot(pair(*split(change_two)), place_map[...])
            stiff, damping = stiff_f[rows, :], damp_f[rows, :]
            for component in range(3):
                part = tile(component)
                lanes = slice(component * LANES, (component + 1) * LANES)
                node_f[rows, part] = (right_one_f[rows, part] + stiff * placed_one[:, lanes]) * damping
                right_two_f[rows, part] = right_two_f[rows, part] + stiff * placed_two[:, lanes]

    def fine_field(index, rows):
        x, y, z = (node_f.at[rows, tile(component)] for component in range(3))
        if index < 3:
            return (x, y, z)[index][...]
        ky = ky_f[rows, :]
        kx = UNIT * ((lanes_like(ky) % 16).astype(F32) * GROUP + place_f32)
        if index == 3:
            return ky * z[...]
        if index == 4:
            return -kx * z[...]
        return kx * y[...] - ky * x[...]

    def spread_fine(first):
        for rows in chunks(128):
            cosine, sine = cos_f[rows, :], sin_f[rows, :]
            for index in (first, first + 1):
                mixed = dot(pair(*split(fine_field(index, rows))), spread_map_f[...])
                if index < 3:
                    twisted(rows, index, mixed[:, :LANES], mixed[:, LANES:], cosine, sine)
                else:
                    twisted(rows, index, mixed[:, LANES:], -mixed[:, :LANES], cosine, sine)
        half_products(y_halves, first, 2, fine_send.at[first // 2])

    def give_back(source, component, target, base):
        for half in range(2):
            block_t = source[pl.ds(half * 128, 128), tile(component)].T
            for part in range(2):
                for quarter in range(4):
                    start = base + part * 384 + component * 8 + 2 * quarter + half
                    first = (part * 4 + quarter) * 16
                    target[pl.ds(start, 16, stride=24), :] = block_t[first : first + 16]

    def give_back_coarse(source, base):
        for half in range(2):
            block_t = source[pl.ds(half * 128, 128), :].T
            for part in range(2):
                for component in range(3):
                    for quarter in range(2):
                        start = base + part * 96 + component * 4 + 2 * quarter + half
                        first = part * 64 + component * 16 + quarter * 8
                        coarse_out[pl.ds(start, 8, stride=12), :] = block_t[first : first + 8]

    def cross_fine(component):
        second, third = (component + 1) % 3, (component + 2) % 3
        fields = [grid_buf[:, tile(index)] for index in (second, third, second + 3, third + 3)]
        return fields[0] * fields[3] - fields[1] * fields[2]

    def gather_fine(component):
        even, odd = folded(fine_back_recv[component])
        stack_back(component, even, -turned(odd))
        y_back(component, 1)
        for rows in chunks(128):
            value = grid_buf[rows, tile(component)]
            value = value * turn_yc_f[rows, :] - turned(value) * turn_ys_f[rows, :]
            right_one_f[rows, tile(component)] = dot(pair(*split(value)), finish_map_f[...])

    def finish_fine():
        for rows in chunks(64):
            modes = [right_one_f[rows, tile(component)] for component in range(3)]
            cross = cross_f[rows, :]
            results = [
                same_x[rows, :] * modes[0] + cross * modes[1],
                same_y[rows, :] * modes[1] + cross * modes[0],
                mask_f[rows, :] * modes[2],
            ]
            for component, value in enumerate(results):
                part = tile(component)
                right_one_f[rows, part] = value
                total = node_f[rows, part] + HALF_STEP * value + right_two_f[rows, part]
                node_f[rows, part] = total * damp_f[rows, :]

    def fine_sweep():
        @pl.when(rank == 0)
        def _():
            first = pl.ds(0, 768)
            right_one[...] = right_one[...] + state_ref[first, :] + HALF_STEP * terms_ref[first, :]

        @pl.when(rank > 0)
        def _():
            receive(start_recv, start_sems.at[1])
            right_one[...] = right_one[...] + start_recv[...]

        for component in range(3):
            fine_tile(right_one, component, right_one_f)
            fine_tile(right_two, component, right_two_f)
        receive(news.at[pl.ds(0, 2)], news_got.at[0])

        @pl.when(rank < 3)
        def _():
            receive(news.at[2], news_got.at[1])

        @pl.when(rank == 3)
        def _():
            receive(last_recv, back_got.at[2])
            tables = (keep_same_r, keep_cross_r, damp_r)
            finish_coarse(last_recv, news.at[1], parcel_send.at[2], news.at[2], *tables)

        correct_fine()
        for part in range(3):
            spread_fine(2 * part)
            pairs = (fine_send.at[part], fine_recv.at[part], fine_sent.at[part], fine_got.at[part])
            post_own(*pairs, RANK, rank, place)
        give_back_coarse(news.at[1], 0)
        give_back_coarse(news.at[2], 192)
        for part in range(3):
            receive(fine_recv.at[part], fine_got.at[part])
            to_grid(fine_recv.at[part], 2 * part, fore_high_f, fore_low_f, turn_xc_f[...], turn_xs_f[...])
        for part in range(3):
            from_grid(cross_fine(part), fine_back_send.at[part], back_f, turn_xc_f[...], turn_xs_f[...])
            pairs = (fine_back_send.at[part], fine_back_recv.at[part])
            post_own(*pairs, fine_back_sent.at[part], fine_back_got.at[part], RANK, rank, place)
        for component in range(3):
            give_back(node_f, component, nodes_out, 0)
        for part in range(3):
            receive(fine_back_recv.at[part], fine_back_got.at[part])
            gather_fine(part)
        finish_fine()
        for component in range(3):
            give_back(right_one_f, component, term_out, 0)
            give_back(node_f, component, nodes_out, 768)

    early = high_z * (1 - low_z)

    def phase(step, carry):
        fine_now = (step + early) % 2

        @pl.when(fine_now == 0)
        def _():
            coarse_sweep()

        @pl.when(fine_now == 1)
        def _():
            fine_sweep()

        return carry

    lax.fori_loop(0, 2, phase, 0)

    @pl.when(rank == 0)
    def _():
        drain_other(fore_send.at[0], fore_sent.at[0])

    drain(fore_send.at[1], fore_sent.at[1], GROUP - 1)
    drain(back_send.at[0], back_sent.at[0], GROUP - 1)
    for part in range(3):
        drain(fine_send.at[part], fine_sent.at[part], GROUP - 1)
        drain(fine_back_send.at[part], fine_back_sent.at[part], GROUP - 1)

    @pl.when(duty == 3)
    def _():
        drain_other(back_send.at[1], back_sent.at[1])

    @pl.when(duty < 3)
    def _():
        drain(back_send.at[1], back_sent.at[1], GROUP - 1)
        drain(fore_send.at[2], fore_sent.at[2], GROUP)
        receive(sweep.at[2], hand_sems.at[0])

    @pl.when(jnp.logical_not(alone))
    def _():
        receive(parcel_send, parcel_sems.at[0])
        receive(sweep.at[pl.ds(0, 2)], news_sent.at[0])

        @pl.when(duty < 3)
        def _():
            receive(sweep.at[2], news_sent.at[1])

    @pl.when(rank < 3)
    def _():
        receive(start_send, start_sems.at[0])


def hand_out(*refs):
    sources, targets, buffers, load_sems, save_sems = refs[:3], refs[3:6], refs[6:9], refs[9], refs[10]
    loads, saves = [], []
    for source, target, buffer in zip(sources, targets, buffers):
        size = source.shape[0] // PIECES
        for piece in range(PIECES):
            rows, number = pl.ds(piece * size, size), len(loads)
            loads.append(pltpu.make_async_copy(source.at[rows], buffer.at[rows], load_sems.at[number]))
            saves.append(pltpu.make_async_copy(buffer.at[rows], target.at[rows], save_sems.at[number]))
    for load in loads:
        load.start()
    for load, save in zip(loads, saves):
        load.wait()
        save.start()
    for save in saves:
        save.wait()


def shards(fine_state, fine_terms):
    matrices, turns = constant_tables()
    full, natural, wide = (ROWS, LANES), (768, LANES), (ROWS, 3 * LANES)
    dma = pltpu.SemaphoreType.DMA
    tiles = (3, ROWS, LANES)
    shapes = [(ROWS, 6 * LANES)]
    shapes += [(3, ROWS, 2 * LANES), (2, ROWS, 2 * LANES), (2, ROWS, LANES), (2, ROWS, LANES), full, full]
    shapes += [tiles] * 4 + [(3, ROWS, 2 * LANES)] * 2 + [tiles] * 2
    shapes += [natural] * 6 + [full] * (9 + 9) + [wide] * 3 + [(2304, LANES)] * 2
    scratch = [pltpu.VMEM((2 * ROWS, 6 * LANES), BF16)] * 2 + [pltpu.VMEM(shape, F32) for shape in shapes]
    scratch += [pltpu.VMEM(matrices.shape, BF16), pltpu.VMEM(turns.shape, F32)]
    scratch += [dma((count,)) for count in (3, 2, 2, 3, 2, 2, 2, 2, 3, 3, 3, 3, 2, 7)]
    outs = pl.pallas_call(
        iterate,
        out_shape=(
            jax.ShapeDtypeStruct((1536, LANES), F32),
            jax.ShapeDtypeStruct((768, LANES), F32),
            jax.ShapeDtypeStruct((384, LANES), F32),
        ),
        in_specs=[pl.BlockSpec(memory_space=pltpu.HBM)] * 4,
        out_specs=[pl.BlockSpec(memory_space=pltpu.VMEM)] * 3,
        scratch_shapes=scratch,
        compiler_params=pltpu.CompilerParams(
            collective_id=0, has_side_effects=True, vmem_limit_bytes=62 * 1024 * 1024
        ),
        name="iterate",
    )(fine_state.reshape(2304, LANES), fine_terms.reshape(2304, LANES), jnp.asarray(matrices), jnp.asarray(turns))
    outs = pl.pallas_call(
        hand_out,
        out_shape=[jax.ShapeDtypeStruct(out.shape, F32) for out in outs],
        in_specs=[pl.BlockSpec(memory_space=pl.ANY)] * 3,
        out_specs=[pl.BlockSpec(memory_space=pl.ANY)] * 3,
        scratch_shapes=[pltpu.VMEM(out.shape, F32) for out in outs] + [dma((3 * PIECES,))] * 2,
        compiler_params=pltpu.CompilerParams(vmem_limit_bytes=62 * 1024 * 1024),
        name="hand_out",
    )(*outs)
    return (
        outs[0].reshape(1, 2, 2, 16, 1, 3, 1, 1024),
        outs[1].reshape(1, 2, 16, 1, 3, 1, 1024),
        outs[2].reshape(1, 2, 2, 8, 1, 3, 1, 512),
    )


def solution(mesh):
    split_over = P("tm", None, None, None, ("py", "pz"), None, None, None)
    return jax.shard_map(
        shards,
        mesh=mesh,
        in_specs=(split_over, split_over),
        out_specs=(
            split_over,
            P("tm", None, None, ("py", "pz"), None, None, None),
            split_over,
        ),
        check_vma=False,
    )
```

```python
import math

import jax
import jax.numpy as jnp
import ml_dtypes
import numpy as np
from jax import lax
from jax.experimental import pallas as pl
from jax.experimental.pallas import tpu as pltpu
from jax.sharding import PartitionSpec as P

EDGE = 1024
VISCOSITY = 0.5
TIME_STEP = 0.2
HALF_STEP = 0.5 * TIME_STEP
WEIGHTS = ((5.0 / 24.0, 1.0 / 3.0, -1.0 / 24.0), (-1.0 / 24.0, 1.0 / 3.0, 5.0 / 24.0))
UNIT = 2.0 * math.pi / EDGE
GROUP = 32
ROWS = 256
LANES = 128
F32 = jnp.float32
BF16 = jnp.bfloat16
MESH = pl.DeviceIdType.MESH
TERM_ONE = [TIME_STEP * w for w in WEIGHTS[0]]
TERM_ONE[0] -= HALF_STEP
TERM_TWO = [TIME_STEP * w for w in WEIGHTS[1]]
TERM_TWO[1] -= HALF_STEP
STATE_ONE = [-TIME_STEP * w for w in WEIGHTS[0]]
STATE_ONE[1] += HALF_STEP
STATE_TWO = [-TIME_STEP * w for w in WEIGHTS[1]]
STATE_TWO[2] += HALF_STEP


HOPS = (0, 1, 2, 1)
DUTY, RANK = (
    sorted(
        ((y, z, x) for y in range(4) for z in range(2) for x in range(4)),
        key=lambda step: -(HOPS[step[0]] + apart * step[1] + HOPS[step[2]]),
    )
    for apart in (1, 2)
)


def halves(table):
    high = table.astype(ml_dtypes.bfloat16)
    low = (table - high.astype(np.float64)).astype(ml_dtypes.bfloat16)
    return high, low


def lane_circle(extent):
    inner = extent // GROUP
    modes = inner // 2
    pairs = 64 // modes
    fore = np.zeros((2, pairs, modes, 2, pairs, inner))
    back = np.zeros((2, pairs, inner, 2, pairs, modes))
    phase = 2.0 * math.pi * np.outer(np.arange(modes), np.arange(inner)) / inner
    kept = (np.arange(modes) * GROUP <= extent // 3)[None, :]
    for pair in range(pairs):
        cosine, sine = 2.0 / extent * np.cos(phase), 2.0 / extent * np.sin(phase)
        fore[0, pair, :, 0, pair] = cosine
        fore[1, pair, :, 0, pair] = -sine
        fore[0, pair, :, 1, pair] = sine
        fore[1, pair, :, 1, pair] = cosine
        target = pair
        sources = [(pair, pair)]
        if extent < EDGE:
            slot, rest = divmod(pair, 2)
            sources = [(((1, 2, 0, 1)[slot]) * 2 + rest, pair)]
        for source, target in sources:
            cosine = 1.0 / extent * np.cos(phase).T * kept
            sine = 1.0 / extent * np.sin(phase).T * kept
            back[0, source, :, 0, target] = cosine
            back[1, source, :, 0, target] = sine
            back[0, source, :, 1, target] = -sine
            back[1, source, :, 1, target] = cosine
    fore = fore.reshape(128, 256)
    back = back.reshape(256, 128)
    return fore, back


def real_form(table):
    return np.block([[table.real, table.imag], [-table.imag, table.real]])


def doubled(table):
    return np.concatenate([table, table], axis=0)


def lane_maps():
    sign = np.array([[1.0, 1.0], [1.0, -1.0]])
    curl_y, curl_x, partner = np.zeros((4, 4)), np.zeros((4, 4)), np.zeros((4, 4))
    curl_y[2, 0] = curl_y[2, 3] = 1.0
    curl_y[0, 2] = -1.0
    curl_x[2, 1] = -1.0
    curl_x[1, 2] = 1.0
    partner[1, 0] = partner[1, 3] = partner[0, 1] = 1.0

    def coarse(slots):
        table = np.kron(np.kron(slots, sign), np.eye(8)).astype(complex)
        return real_form(table), real_form(1j * table)

    same = coarse(np.eye(4))
    spread_c = doubled(np.concatenate(same, axis=1))
    curl_c = np.concatenate([np.concatenate(coarse(slots), axis=1) for slots in (curl_y, curl_x)], axis=0)
    finish_c = doubled(np.concatenate([same[0], coarse(partner)[0]], axis=1))
    quarters, powers = np.arange(4), np.array([0, 2, 1, 3])
    table = np.kron(1j ** (np.outer(quarters, powers) % 4), np.eye(16))
    spread_f = doubled(np.concatenate([real_form(table), real_form(1j * table)], axis=1))
    finish_f = doubled(real_form(np.conj(table).T))
    place = np.zeros((3, 4, 2, 8, 4, 16))
    for component in range(3):
        for a in range(8):
            place[component, component, 0, a, 0, a] = 1.0
            place[component, component, 1, a, 3, a] = 1.0
    place_f = doubled(np.concatenate([real_form(table.reshape(64, 64).astype(complex)) for table in place], axis=1))
    return [
        np.concatenate(pair, axis=1).astype(ml_dtypes.bfloat16)
        for pair in ((spread_c, curl_c), (finish_c, spread_f), (place_f, finish_f))
    ]


def constant_tables():
    index = np.arange(ROWS)
    phase = 2.0 * math.pi * np.outer(np.arange(ROWS // 2) + 0.5, index) / ROWS
    along_y = np.concatenate([np.cos(phase), np.sin(phase)], axis=1)
    back_y = np.concatenate([np.cos(phase).T, np.sin(phase).T], axis=1)
    small = 2.0 * math.pi * np.outer(np.arange(GROUP) + 0.5, np.arange(GROUP)) / GROUP
    along_x = np.concatenate([np.cos(small), -np.sin(small)], axis=1).reshape(GROUP, 2, GROUP)
    half = GROUP // 2
    order = np.stack([np.arange(half), GROUP - 1 - np.arange(half)], axis=1).reshape(-1)
    back_x = np.kron(along_x[order].transpose(1, 2, 0).reshape(2 * GROUP, GROUP), np.eye(8))
    along_x = np.kron(along_x[:half].reshape(half, 2 * GROUP), np.eye(8))
    maps = lane_maps()
    matrices = list(halves(along_y)) + [np.concatenate(halves(back_y), axis=1), maps[0]]
    matrices += list(halves(along_x)) + [np.concatenate(halves(back_x), axis=1)]
    lane = np.arange(LANES)
    turns, inner_parts = [], []
    for extent in (EDGE // 2, EDGE):
        fore, back = lane_circle(extent)
        fore_high, fore_low = halves(fore)
        back_high, back_low = halves(back)
        inner_parts.append(
            np.concatenate([fore_high, fore_high, fore_low, np.concatenate([back_high, back_low], axis=1)], axis=0)
        )
        inner = extent // GROUP
        turn = 2.0 * math.pi * np.outer(index // 8, lane % inner / extent - 0.5 / GROUP)
        turns += [np.cos(turn), np.sin(turn)]
        if extent < EDGE:
            offset = (lane % 16) // 8
        else:
            offset = np.array([0, 2, 1, 3])[(lane % 64) // 16]
        turn = 2.0 * math.pi * np.outer(index, offset / extent - 0.5 / ROWS)
        turns += [np.cos(turn), np.sin(turn)]
    matrices.append(np.concatenate(inner_parts, axis=1))
    matrices += maps[1:]
    return np.concatenate(matrices, axis=0), np.concatenate(turns, axis=0).astype(np.float32)


def split(value):
    high = value.astype(BF16)
    return high, (value - high.astype(F32)).astype(BF16)


def dot(left, right):
    return jnp.dot(left, right, preferred_element_type=F32)


def roll(value, shift):
    return pltpu.roll(value, shift % LANES, axis=1)


def lanes_like(value):
    return lax.broadcasted_iota(jnp.int32, value.shape, 1)


def turned(value):
    other = roll(value, 64)
    return jnp.where(lanes_like(value) < 64, -other, other)


def tile(index):
    return pl.ds(index * LANES, LANES)


def chunks(size):
    return [pl.ds(start, size) for start in range(0, ROWS, size)]


def iterate(
    state_hbm, terms_hbm, matrices_hbm, turns_hbm,
    nodes_out, term_out, coarse_out,
    rhs_high, rhs_low, grid_buf,
    fore_send, fore_recv, back_send, back_recv, last_recv, hand_recv,
    parcel_send, parcel_recv, sweep, news,
    fine_send, fine_recv, fine_back_send, fine_back_recv, start_send, start_recv,
    right_one, right_two, mix_one, mix_two,
    curl_y, keep_same, keep_cross, damp_c, keep_same_r, keep_cross_r, damp_r, old_one, old_two,
    ky_f, damp_f, stiff_f, cos_f, sin_f, same_x, same_y, cross_f, mask_f,
    right_one_f, right_two_f, node_f,
    state_ref, terms_ref, matrices, turns,
    fore_sent, fore_got, back_sent, back_got, hand_sems, parcel_sems, news_sent, news_got,
    fine_sent, fine_got, fine_back_sent, fine_back_got, start_sems, load_sems,
    ready,
):
    loads = []
    for source, target, start, size in (
        (state_hbm, state_ref, 0, 768),
        (matrices_hbm, matrices, 0, 768),
        (turns_hbm, turns, 0, 1024),
        (state_hbm, state_ref, 768, 1536),
        (terms_hbm, terms_ref, 0, 2304),
        (matrices_hbm, matrices, 768, 1920),
        (turns_hbm, turns, 1024, 1024),
    ):
        rows = pl.ds(start, size)
        loads.append(pltpu.make_async_copy(source.at[rows], target.at[rows], load_sems.at[len(loads)]))
        loads[-1].start()

    def matrix(start, size, first=0, width=512):
        return matrices.at[pl.ds(start, size), pl.ds(first, width)]

    y_halves = (matrix(0, 256, 0, 256), matrix(0, 256, 256, 256))
    yt_high, yt_low = matrix(256, 256, 0, 256), matrix(256, 256, 256, 256)
    spread_map, curl_map = matrix(512, 256, 0, 256), matrix(512, 256, 256, 256)
    x_halves = (matrix(768, 256, 0, 256), matrix(768, 256, 256, 256))
    xt_high, xt_low = matrix(1024, 512, 0, 256), matrix(1024, 512, 256, 256)
    fore_high_c, fore_low_c, back_c = (matrix(*rows, 0, 256) for rows in ((1536, 256), (1792, 128), (1920, 256)))
    fore_high_f, fore_low_f, back_f = (matrix(*rows, 256, 256) for rows in ((1536, 256), (1792, 128), (1920, 256)))
    finish_map, spread_map_f = matrix(2176, 256, 0, 256), matrix(2176, 256, 256, 256)
    place_map, finish_map_f = matrix(2432, 256, 0, 384), matrix(2432, 256, 384, 128)
    turn_xc_c, turn_xs_c, turn_yc_c, turn_ys_c, turn_xc_f, turn_xs_f, turn_yc_f, turn_ys_f = (
        turns.at[pl.ds(start, ROWS), :] for start in range(0, 8 * ROWS, ROWS)
    )
    rank = lax.axis_index("tm")
    at_y, at_pz = lax.axis_index("py"), lax.axis_index("pz")
    low_z, core, high_z, at_x = rank // 2, rank % 2, at_pz // 4, at_pz % 4
    place = at_y * 8 + at_pz
    duty = high_z * 2 + core
    spot = at_y * 8 + low_z * 4 + at_x
    alone = high_z == low_z
    partner = (duty, at_y, low_z * 4 + at_x)

    barrier = pltpu.get_barrier_semaphore()
    number = rank * GROUP + place
    near = (core == 0) & (high_z + low_z < 2)

    def signal(semaphore, other):
        target = (other // GROUP, (other // 8) % 4, other % 8)
        pl.semaphore_signal(semaphore, inc=1, device_id=target, device_id_type=MESH)

    def greet_first(step, carry):
        signal(barrier, (place + step) % GROUP)
        return carry

    @pl.when(near)
    def _():
        @pl.when(rank > 0)
        def _():
            signal(barrier, place)

        lax.fori_loop(1, GROUP, greet_first, 0)

    def greet(step, carry):
        signal(barrier, GROUP + (number + 2 * GROUP + step) % (3 * GROUP))
        return carry

    @pl.when(rank == 0)
    def _():
        greet(0, 0)

    lax.fori_loop(1, 3 * GROUP, greet, 0)

    def block(position):
        return pl.ds(pl.multiple_of(position * 8, 8), 8)

    spots_y = [(at_y + step) % 4 for step in range(4)]
    spots_x = [(at_x + step) % 4 for step in range(4)]
    duty_z = [(low_z + step) % 2 for step in range(2)]
    rank_z = [(high_z + step) % 2 for step in range(2)]

    def spot_of(steps, step):
        spot_y, spot_x = spots_y[step[0]], spots_x[step[2]]
        if steps is DUTY:
            spot_z = duty_z[step[1]]
            address = lambda group: (spot_z * 2 + group % 2, spot_y, (group // 2) * 4 + spot_x)
        else:
            spot_z = rank_z[step[1]]
            address = lambda group: (group, spot_y, spot_z * 4 + spot_x)
        return spot_y * 8 + spot_z * 4 + spot_x, address

    def post(source, target, sent, got, steps, group, mine, count):
        for step in steps[:count]:
            index, address = spot_of(steps, step)
            pltpu.make_async_remote_copy(
                src_ref=source.at[block(index)],
                dst_ref=target.at[block(mine)],
                send_sem=sent,
                recv_sem=got,
                device_id=address(group),
                device_id_type=MESH,
            ).start()

    def post_own(source, target, sent, got, steps, group, mine):
        post(source, target, sent, got, steps, group, mine, GROUP - 1)
        pltpu.make_async_copy(source.at[block(mine)], target.at[block(mine)], got).start()

    def post_other(source, target, sent, got, steps, group, mine):
        post(source, target, sent, got, steps, group, mine, GROUP - 1)
        index, address = spot_of(steps, steps[-1])

        @pl.when(alone)
        def _():
            pltpu.make_async_copy(source.at[block(index)], target.at[block(mine)], got).start()

        @pl.when(jnp.logical_not(alone))
        def _():
            pltpu.make_async_remote_copy(
                src_ref=source.at[block(index)],
                dst_ref=target.at[block(mine)],
                send_sem=sent,
                recv_sem=got,
                device_id=address(group),
                device_id_type=MESH,
            ).start()

    def send_one(source, target, sent, got, address):
        return pltpu.make_async_remote_copy(
            src_ref=source, dst_ref=target, send_sem=sent, recv_sem=got, device_id=address, device_id_type=MESH
        )

    def to_partner(source, target, sent, got):
        @pl.when(alone)
        def _():
            pltpu.make_async_copy(source, target, got).start()

        @pl.when(jnp.logical_not(alone))
        def _():
            send_one(source, target, sent, got, partner).start()

    def receive(target, got):
        pltpu.make_async_copy(target, target, got).wait()

    def drain(source, sent, count):
        part = source.at[pl.ds(0, count * 8)]
        pltpu.make_async_copy(part, part, sent).wait()

    def drain_other(source, sent):
        @pl.when(alone)
        def _():
            drain(source, sent, GROUP - 1)

        @pl.when(jnp.logical_not(alone))
        def _():
            drain(source, sent, GROUP)

    place_f32, spot_f32 = place.astype(F32), spot.astype(F32)
    row = lax.broadcasted_iota(jnp.int32, (ROWS, LANES), 0)
    lane = lax.broadcasted_iota(jnp.int32, (ROWS, LANES), 1)

    def wave_tables(extent, mode_x, mode_y):
        wave_x, wave_y = UNIT * mode_x, UNIT * mode_y
        wave_sq = wave_x * wave_x + wave_y * wave_y
        anchor = (mode_x == 0) & (mode_y == 0)
        kept = (mode_x <= extent // 3) & (jnp.abs(mode_y) <= extent // 3) & ~anchor
        mask = jnp.where(kept, 1.0, 0.0).astype(F32)
        inverse = mask / jnp.where(anchor, 1.0, wave_sq)
        damp = 1.0 / (1.0 + HALF_STEP * VISCOSITY * wave_sq)
        return wave_x, wave_y, wave_sq, mask, inverse, damp

    def coarse_tables(position, same_ref, cross_ref, damp_ref):
        slot = (lane % 64) // 16
        mode_x = (lane % 8).astype(F32) * GROUP + position
        mode_y = (row - 256 * ((lane % 16) // 8)).astype(F32)
        wave_x, wave_y, wave_sq, mask, inverse, damp = wave_tables(EDGE // 2, mode_x, mode_y)
        same = jnp.where(slot == 2, mask, jnp.where(slot == 1, wave_x * wave_x, wave_y * wave_y) * inverse)
        same_ref[...] = same * (HALF_STEP * damp)
        cross_ref[...] = jnp.where(slot == 2, 0.0, -wave_x * wave_y * inverse) * (HALF_STEP * damp)
        damp_ref[...] = damp

    curl_y[...] = UNIT * (row - 256 * ((lane % 16) // 8)).astype(F32)

    def coarse_tile(ref, base, scale, target):
        for half in range(2):
            pieces = []
            for part in range(2):
                for component in (0, 1, 2, 0):
                    for quarter in (0, 3):
                        start = base + part * 384 + component * 8 + 2 * quarter + half
                        pieces.append(ref[pl.ds(start, 8, stride=24), :])
            target[pl.ds(half * 128, 128), :] = scale * jnp.concatenate(pieces, axis=0).T

    def fine_tile(ref, component, target):
        for half in range(2):
            pieces = []
            for part in range(2):
                for quarter in range(4):
                    start = part * 384 + component * 8 + 2 * quarter + half
                    pieces.append(ref[pl.ds(start, 16, stride=24), :])
            target[pl.ds(half * 128, 128), tile(component)] = jnp.concatenate(pieces, axis=0).T

    def half_products(matrices_two, first, count, target):
        part = pl.ds(first * LANES, count * LANES)
        halves_two = []
        for index, both_parts in enumerate(matrices_two):
            rows = pl.ds(index * ROWS, ROWS)
            both = dot(both_parts[...], rhs_high[rows, part])
            rest = dot(both_parts[pl.ds(0, 128), :], rhs_low[rows, part])
            halves_two.append(both[:128] + both[128:] + rest)
        even, odd = halves_two
        total, difference = even + odd, even - odd
        for step in range(16):
            lines = slice(step * 8, step * 8 + 8)
            target[pl.ds(step * 16, 8), :] = total[lines]
            target[pl.ds(step * 16 + 8, 8), :] = difference[lines]

    def y_back(first, count):
        part = pl.ds(first * LANES, count * LANES)
        high, low = rhs_high[pl.ds(0, ROWS), part], rhs_low[pl.ds(0, ROWS), part]
        grid_buf[:, part] = dot(yt_high[...], high) + dot(yt_high[...], low) + dot(yt_low[...], high)

    def folded(value):
        mirrored = value.reshape(16, 2, 8, LANES)
        first, second = mirrored[:, 0].reshape(128, LANES), mirrored[:, 1].reshape(128, LANES)
        return first + second, first - second

    def stack_back(index, upper, lower):
        for start, value in ((0, upper), (128, lower)):
            high, low = split(value)
            rhs_high[pl.ds(start, 128), tile(index)] = high
            rhs_low[pl.ds(start, 128), tile(index)] = low

    def pair(high, low):
        return jnp.concatenate([high, low], axis=1)

    def twisted(rows, index, value, value_turned, cosine, sine):
        stack(rows, index, value * cosine + value_turned * sine, value_turned * cosine - value * sine)

    def stack(rows, index, first, second):
        high, low = split(first)
        rhs_high[rows, tile(index)] = high
        rhs_low[rows, tile(index)] = low
        high, low = split(second)
        lower = pl.ds(rows.start + ROWS, rows.size)
        rhs_high[lower, tile(index)] = high
        rhs_low[lower, tile(index)] = low

    def spread_coarse(source, target, position):
        lanes = lax.broadcasted_iota(jnp.int32, (1, LANES), 1) % 8
        mode_x = lanes.astype(F32) * GROUP + position
        weight = jnp.where(mode_x == 0, 0.5, 1.0)
        for rows in chunks(128):
            velocity = source[rows, :] * weight
            high_y, low_y = split(velocity * curl_y[rows, :])
            high_x, low_x = split(velocity * (UNIT * mode_x))
            mixed = dot(pair(*split(velocity)), spread_map[...])
            curled = dot(pair(high_y, high_x), curl_map[...]) + dot(pair(low_y, low_x), curl_map[...])
            cosine, sine = turn_yc_c[rows, :], turn_ys_c[rows, :]
            twisted(rows, 0, mixed[:, :LANES], mixed[:, LANES:], cosine, sine)
            twisted(rows, 1, curled[:, LANES:], -curled[:, :LANES], cosine, sine)
        half_products(y_halves, 0, 2, target)

    def to_grid(source, first, fore_high, fore_low, cosine, sine):
        every = pl.ds(0, ROWS)
        for index in range(2):
            high, low = split(source[:, tile(index)])
            inner = dot(pair(high, low), fore_high[...]) + dot(high, fore_low[...])
            real, imag = inner[:, :LANES], inner[:, LANES:]
            stack(every, first + index, real * cosine - imag * sine, real * sine + imag * cosine)
        part = pl.ds(first * LANES, 2 * LANES)
        half_products(x_halves, first, 2, grid_buf.at[:, part])

    def from_grid(value, target, back, cosine, sine):
        high, low = split(value)
        both = dot(xt_high[...], pair(high, low))
        outer = both[:, :LANES] + both[:, LANES:] + dot(xt_low[...], high)
        real, imag = outer[:ROWS], outer[ROWS:]
        high, low = split(pair(real * cosine + imag * sine, imag * cosine - real * sine))
        both = dot(high, back[...])
        target[...] = both[:, :LANES] + both[:, LANES:] + dot(low, back[:, :LANES])

    def grid_coarse(source, target):
        cosine, sine = turn_xc_c[...], turn_xs_c[...]
        to_grid(source, 0, fore_high_c, fore_low_c, cosine, sine)
        speed, spin = grid_buf[:, tile(0)], grid_buf[:, tile(1)]
        crossed = speed * roll(spin, -32) - roll(speed, -32) * spin
        from_grid(crossed, target, back_c, cosine, sine)

    def finish_coarse(source, start_ref, right_ref, target, same_ref, cross_ref, damp_ref):
        even, odd = folded(source[...])
        stack_back(0, even, -turned(odd))
        stack_back(1, turned(even), odd)
        y_back(0, 2)
        for rows in chunks(128):
            value = grid_buf[rows, tile(0)] * turn_yc_c[rows, :] - grid_buf[rows, tile(1)] * turn_ys_c[rows, :]
            modes = dot(pair(*split(value)), finish_map[...])
            term = same_ref[rows, :] * modes[:, :LANES] + cross_ref[rows, :] * modes[:, LANES:]
            target[rows, :] = damp_ref[rows, :] * (start_ref[rows, :] + right_ref[rows, :]) + term

    loads[0].wait()
    coarse_tile(state_ref, 0, 0.5, parcel_send.at[0])
    loads[1].wait()
    loads[2].wait()

    @pl.when(rank == 0)
    def _():
        spread_coarse(parcel_send.at[0], fore_send.at[0], place_f32)

    @pl.when(rank > 0)
    def _():
        pl.semaphore_wait(barrier, 4 * GROUP - 1)

    def greet_last(step, carry):
        signal(ready, (place + step) % GROUP)
        return carry

    @pl.when(jnp.logical_not(near))
    def _():
        lax.fori_loop(0, GROUP, greet_last, 0)

    @pl.when(rank == 0)
    def _():
        pl.semaphore_wait(barrier, 3 * GROUP // 2 - 1)
        post_other(fore_send.at[0], fore_recv.at[0], fore_sent.at[0], fore_got.at[0], DUTY, 0, place)

    def combine(a, carry):
        wave_x = UNIT * (a.astype(F32) * GROUP + place_f32)
        sub = lax.broadcasted_iota(jnp.int32, (8, LANES), 0)
        mode = sub * 128 + lax.broadcasted_iota(jnp.int32, (8, LANES), 1)
        wave_y = UNIT * jnp.where(mode < EDGE // 2, mode, mode - EDGE).astype(F32)
        stiff = VISCOSITY * (wave_x * wave_x + wave_y * wave_y)
        for part in range(2):
            for component in range(3):
                base = pl.multiple_of(a * 24 + (part * 384 + component * 8), 8)
                rows = pl.ds(base, 8)
                states = [state_ref[pl.ds(base + node * 768, 8), :] for node in range(3)]
                terms = [terms_ref[pl.ds(base + node * 768, 8), :] for node in range(3)]
                one = sum(w * s for w, s in zip(STATE_ONE, states))
                two = sum(w * s for w, s in zip(STATE_TWO, states))
                mix_one[rows, :] = one
                mix_two[rows, :] = two
                right_one[rows, :] = sum(w * t for w, t in zip(TERM_ONE, terms)) + stiff * one
                right_two[rows, :] = sum(w * t for w, t in zip(TERM_TWO, terms)) + stiff * two
                start_send[rows, :] = states[2] + HALF_STEP * terms[2]
        return carry

    for index in (3, 4, 5, 6):
        loads[index].wait()
    lax.fori_loop(0, 16, combine, 0, unroll=2)

    following = (rank + 1, at_y, at_pz)

    @pl.when(rank == 0)
    def _():
        pl.semaphore_wait(ready, 5 * GROUP // 2)

    @pl.when(rank < 3)
    def _():
        send_one(start_send, start_recv, start_sems.at[0], start_sems.at[1], following).start()

    coarse_tile(right_one, 0, 0.5, parcel_send.at[1])
    coarse_tile(right_two, 0, 0.5, parcel_send.at[2])
    to_partner(parcel_send, parcel_recv, parcel_sems.at[0], parcel_sems.at[1])
    coarse_tables(spot_f32, keep_same, keep_cross, damp_c)

    def coarse_sweep():
        receive(fore_recv.at[0], fore_got.at[0])
        grid_coarse(fore_recv.at[0], back_send.at[0])
        post_own(back_send.at[0], back_recv.at[0], back_sent.at[0], back_got.at[0], DUTY, duty, spot)
        receive(parcel_recv, parcel_sems.at[1])

        @pl.when(duty == 0)
        def _():
            sweep[0] = parcel_recv[0]

        @pl.when(duty > 0)
        def _():
            receive(hand_recv, hand_sems.at[1])
            sweep[0] = hand_recv[...]

        receive(back_recv.at[0], back_got.at[0])
        tables = (keep_same, keep_cross, damp_c)
        finish_coarse(back_recv.at[0], sweep.at[0], parcel_recv.at[1], sweep.at[1], *tables)
        spread_coarse(sweep.at[1], fore_send.at[1], spot_f32)
        post_own(fore_send.at[1], fore_recv.at[1], fore_sent.at[1], fore_got.at[1], DUTY, duty, spot)
        to_partner(sweep.at[pl.ds(0, 2)], news.at[pl.ds(0, 2)], news_sent.at[0], news_got.at[0])
        receive(fore_recv.at[1], fore_got.at[1])
        grid_coarse(fore_recv.at[1], back_send.at[1])

        @pl.when(duty == 3)
        def _():
            post_other(back_send.at[1], last_recv, back_sent.at[1], back_got.at[2], RANK, 3, spot)

        @pl.when(duty < 3)
        def _():
            post_own(back_send.at[1], back_recv.at[1], back_sent.at[1], back_got.at[1], DUTY, duty, spot)
            receive(back_recv.at[1], back_got.at[1])
            finish_coarse(back_recv.at[1], sweep.at[1], parcel_recv.at[2], sweep.at[2], *tables)
            spread_coarse(sweep.at[2], fore_send.at[2], spot_f32)
            after = duty + 1
            post(fore_send.at[2], fore_recv.at[0], fore_sent.at[2], fore_got.at[0], DUTY, after, spot, GROUP)
            address = (low_z * 2 + after % 2, at_y, (after // 2) * 4 + at_x)
            send_one(sweep.at[2], hand_recv, hand_sems.at[0], hand_sems.at[1], address).start()
            to_partner(sweep.at[2], news.at[2], news_sent.at[1], news_got.at[1])

    coarse_tile(mix_one, 0, 0.5, old_one)
    coarse_tile(mix_two, 0, 0.5, old_two)
    quarter = (lane % 64) // 16
    mode_x = (lane % 16).astype(F32) * GROUP + place_f32
    mode_y = (row + 256 * quarter - jnp.where(quarter >= 2, EDGE, 0)).astype(F32)
    wave_x, wave_y, wave_sq, mask, inverse, damp = wave_tables(EDGE, mode_x, mode_y)
    ky_f[...] = wave_y
    damp_f[...] = damp
    stiff_f[...] = (2.0 * VISCOSITY) * wave_sq
    same_x[...] = wave_y * wave_y * inverse
    same_y[...] = wave_x * wave_x * inverse
    cross_f[...] = -wave_x * wave_y * inverse
    mask_f[...] = mask
    weight = jnp.where(mode_x == 0, 0.5, 1.0)
    cos_f[...] = turn_yc_f[...] * weight
    sin_f[...] = turn_ys_f[...] * weight

    @pl.when(rank == 3)
    def _():
        coarse_tables(place_f32, keep_same_r, keep_cross_r, damp_r)

    def correct_fine(weights, old_ref, target):
        for rows in chunks(128):
            nodes = [news[node, rows, :] for node in range(3)]
            change = sum(w * n for w, n in zip(weights, nodes)) - old_ref[rows, :]
            placed = dot(pair(*split(change)), place_map[...])
            stiff = stiff_f[rows, :]
            for component in range(3):
                part = tile(component)
                lanes = slice(component * LANES, (component + 1) * LANES)
                target[rows, part] = target[rows, part] + stiff * placed[:, lanes]

    def start_fine():
        correct_fine(STATE_ONE, old_one, right_one_f)
        for component in range(3):
            node_f[:, tile(component)] = right_one_f[:, tile(component)] * damp_f[...]

    def fine_field(index, rows):
        x, y, z = (node_f.at[rows, tile(component)] for component in range(3))
        if index < 3:
            return (x, y, z)[index][...]
        ky = ky_f[rows, :]
        kx = UNIT * ((lanes_like(ky) % 16).astype(F32) * GROUP + place_f32)
        if index == 3:
            return ky * z[...]
        if index == 4:
            return -kx * z[...]
        return kx * y[...] - ky * x[...]

    def spread_fine(first):
        for rows in chunks(128):
            cosine, sine = cos_f[rows, :], sin_f[rows, :]
            for index in (first, first + 1):
                mixed = dot(pair(*split(fine_field(index, rows))), spread_map_f[...])
                if index < 3:
                    twisted(rows, index, mixed[:, :LANES], mixed[:, LANES:], cosine, sine)
                else:
                    twisted(rows, index, mixed[:, LANES:], -mixed[:, :LANES], cosine, sine)
        half_products(y_halves, first, 2, fine_send.at[first // 2])

    def give_back(source, component, target, base):
        for half in range(2):
            block_t = source[pl.ds(half * 128, 128), tile(component)].T
            for part in range(2):
                for quarter in range(4):
                    start = base + part * 384 + component * 8 + 2 * quarter + half
                    first = (part * 4 + quarter) * 16
                    target[pl.ds(start, 16, stride=24), :] = block_t[first : first + 16]

    def give_back_coarse(source, base):
        for half in range(2):
            block_t = source[pl.ds(half * 128, 128), :].T
            for part in range(2):
                for component in range(3):
                    for quarter in range(2):
                        start = base + part * 96 + component * 4 + 2 * quarter + half
                        first = part * 64 + component * 16 + quarter * 8
                        coarse_out[pl.ds(start, 8, stride=12), :] = block_t[first : first + 8]

    def cross_fine(component):
        second, third = (component + 1) % 3, (component + 2) % 3
        fields = [grid_buf[:, tile(index)] for index in (second, third, second + 3, third + 3)]
        return fields[0] * fields[3] - fields[1] * fields[2]

    def gather_fine(component):
        even, odd = folded(fine_back_recv[component])
        stack_back(component, even, -turned(odd))
        y_back(component, 1)
        for rows in chunks(128):
            value = grid_buf[rows, tile(component)]
            value = value * turn_yc_f[rows, :] - turned(value) * turn_ys_f[rows, :]
            right_one_f[rows, tile(component)] = dot(pair(*split(value)), finish_map_f[...])

    def finish_fine():
        for rows in chunks(64):
            modes = [right_one_f[rows, tile(component)] for component in range(3)]
            cross = cross_f[rows, :]
            results = [
                same_x[rows, :] * modes[0] + cross * modes[1],
                same_y[rows, :] * modes[1] + cross * modes[0],
                mask_f[rows, :] * modes[2],
            ]
            for component, value in enumerate(results):
                part = tile(component)
                right_one_f[rows, part] = value
                total = node_f[rows, part] + HALF_STEP * value + right_two_f[rows, part]
                node_f[rows, part] = total * damp_f[rows, :]

    def fine_sweep():
        @pl.when(rank == 0)
        def _():
            first = pl.ds(0, 768)
            right_one[...] = right_one[...] + state_ref[first, :] + HALF_STEP * terms_ref[first, :]

        @pl.when(rank > 0)
        def _():
            receive(start_recv, start_sems.at[1])
            right_one[...] = right_one[...] + start_recv[...]

        for component in range(3):
            fine_tile(right_one, component, right_one_f)
            fine_tile(right_two, component, right_two_f)
        receive(news.at[pl.ds(0, 2)], news_got.at[0])

        @pl.when(rank < 3)
        def _():
            receive(news.at[2], news_got.at[1])

        @pl.when(rank == 3)
        def _():
            receive(last_recv, back_got.at[2])
            tables = (keep_same_r, keep_cross_r, damp_r)
            finish_coarse(last_recv, news.at[1], parcel_send.at[2], news.at[2], *tables)

        start_fine()
        for part in range(3):
            spread_fine(2 * part)
            pairs = (fine_send.at[part], fine_recv.at[part], fine_sent.at[part], fine_got.at[part])
            post_own(*pairs, RANK, rank, place)
        correct_fine(STATE_TWO, old_two, right_two_f)
        give_back_coarse(news.at[1], 0)
        give_back_coarse(news.at[2], 192)
        for part in range(3):
            receive(fine_recv.at[part], fine_got.at[part])
            to_grid(fine_recv.at[part], 2 * part, fore_high_f, fore_low_f, turn_xc_f[...], turn_xs_f[...])
        for part in range(3):
            from_grid(cross_fine(part), fine_back_send.at[part], back_f, turn_xc_f[...], turn_xs_f[...])
            pairs = (fine_back_send.at[part], fine_back_recv.at[part])
            post_own(*pairs, fine_back_sent.at[part], fine_back_got.at[part], RANK, rank, place)
        for component in range(3):
            give_back(node_f, component, nodes_out, 0)
        for part in range(3):
            receive(fine_back_recv.at[part], fine_back_got.at[part])
            gather_fine(part)
        finish_fine()
        for component in range(3):
            give_back(right_one_f, component, term_out, 0)
            give_back(node_f, component, nodes_out, 768)

    early = high_z * (1 - low_z)

    def phase(step, carry):
        fine_now = (step + early) % 2

        @pl.when(fine_now == 0)
        def _():
            coarse_sweep()

        @pl.when(fine_now == 1)
        def _():
            fine_sweep()

        return carry

    lax.fori_loop(0, 2, phase, 0)

    @pl.when(rank == 0)
    def _():
        drain_other(fore_send.at[0], fore_sent.at[0])

    drain(fore_send.at[1], fore_sent.at[1], GROUP - 1)
    drain(back_send.at[0], back_sent.at[0], GROUP - 1)
    for part in range(3):
        drain(fine_send.at[part], fine_sent.at[part], GROUP - 1)
        drain(fine_back_send.at[part], fine_back_sent.at[part], GROUP - 1)

    @pl.when(duty == 3)
    def _():
        drain_other(back_send.at[1], back_sent.at[1])

    @pl.when(duty < 3)
    def _():
        drain(back_send.at[1], back_sent.at[1], GROUP - 1)
        drain(fore_send.at[2], fore_sent.at[2], GROUP)
        receive(sweep.at[2], hand_sems.at[0])

    @pl.when(jnp.logical_not(alone))
    def _():
        receive(parcel_send, parcel_sems.at[0])
        receive(sweep.at[pl.ds(0, 2)], news_sent.at[0])

        @pl.when(duty < 3)
        def _():
            receive(sweep.at[2], news_sent.at[1])

    @pl.when(rank < 3)
    def _():
        receive(start_send, start_sems.at[0])


def shards(fine_state, fine_terms):
    matrices, turns = constant_tables()
    full, natural, wide = (ROWS, LANES), (768, LANES), (ROWS, 3 * LANES)
    dma = pltpu.SemaphoreType.DMA
    tiles = (3, ROWS, LANES)
    shapes = [(ROWS, 6 * LANES)]
    shapes += [(3, ROWS, 2 * LANES), (2, ROWS, 2 * LANES), (2, ROWS, LANES), (2, ROWS, LANES), full, full]
    shapes += [tiles] * 4 + [(3, ROWS, 2 * LANES)] * 2 + [tiles] * 2
    shapes += [natural] * 6 + [full] * (9 + 9) + [wide] * 3 + [(2304, LANES)] * 2
    scratch = [pltpu.VMEM((2 * ROWS, 6 * LANES), BF16)] * 2 + [pltpu.VMEM(shape, F32) for shape in shapes]
    scratch += [pltpu.VMEM(matrices.shape, BF16), pltpu.VMEM(turns.shape, F32)]
    scratch += [dma((count,)) for count in (3, 2, 2, 3, 2, 2, 2, 2, 3, 3, 3, 3, 2, 7)]
    scratch += [pltpu.SemaphoreType.REGULAR]
    outs = pl.pallas_call(
        iterate,
        out_shape=(
            jax.ShapeDtypeStruct((1536, LANES), F32),
            jax.ShapeDtypeStruct((768, LANES), F32),
            jax.ShapeDtypeStruct((384, LANES), F32),
        ),
        in_specs=[pl.BlockSpec(memory_space=pltpu.HBM)] * 4,
        out_specs=[pl.BlockSpec(memory_space=pltpu.VMEM)] * 3,
        scratch_shapes=scratch,
        compiler_params=pltpu.CompilerParams(
            collective_id=0, has_side_effects=True, vmem_limit_bytes=52 * 1024 * 1024
        ),
        name="iterate",
    )(fine_state.reshape(2304, LANES), fine_terms.reshape(2304, LANES), jnp.asarray(matrices), jnp.asarray(turns))
    return (
        outs[0].reshape(1, 2, 2, 16, 1, 3, 1, 1024),
        outs[1].reshape(1, 2, 16, 1, 3, 1, 1024),
        outs[2].reshape(1, 2, 2, 8, 1, 3, 1, 512),
    )


def solution(mesh):
    split_over = P("tm", None, None, None, ("py", "pz"), None, None, None)
    return jax.shard_map(
        shards,
        mesh=mesh,
        in_specs=(split_over, split_over),
        out_specs=(
            split_over,
            P("tm", None, None, ("py", "pz"), None, None, None),
            split_over,
        ),
        check_vma=False,
    )
```

```python
import math

import jax
import jax.numpy as jnp
import ml_dtypes
import numpy as np
from jax import lax
from jax.experimental import pallas as pl
from jax.experimental.pallas import tpu as pltpu
from jax.sharding import PartitionSpec as P

EDGE = 1024
VISCOSITY = 0.5
TIME_STEP = 0.2
HALF_STEP = 0.5 * TIME_STEP
WEIGHTS = ((5.0 / 24.0, 1.0 / 3.0, -1.0 / 24.0), (-1.0 / 24.0, 1.0 / 3.0, 5.0 / 24.0))
UNIT = 2.0 * math.pi / EDGE
GROUP = 32
ROWS = 256
LANES = 128
F32 = jnp.float32
BF16 = jnp.bfloat16
MESH = pl.DeviceIdType.MESH
TERM_ONE = [TIME_STEP * w for w in WEIGHTS[0]]
TERM_ONE[0] -= HALF_STEP
TERM_TWO = [TIME_STEP * w for w in WEIGHTS[1]]
TERM_TWO[1] -= HALF_STEP
STATE_ONE = [-TIME_STEP * w for w in WEIGHTS[0]]
STATE_ONE[1] += HALF_STEP
STATE_TWO = [-TIME_STEP * w for w in WEIGHTS[1]]
STATE_TWO[2] += HALF_STEP


HOPS = (0, 1, 2, 1)
DUTY, RANK = (
    sorted(
        ((y, z, x) for y in range(4) for z in range(2) for x in range(4)),
        key=lambda step: -(HOPS[step[0]] + apart * step[1] + HOPS[step[2]]),
    )
    for apart in (1, 2)
)


def halves(table):
    high = table.astype(ml_dtypes.bfloat16)
    low = (table - high.astype(np.float64)).astype(ml_dtypes.bfloat16)
    return high, low


def lane_circle(extent):
    inner = extent // GROUP
    modes = inner // 2
    pairs = 64 // modes
    fore = np.zeros((2, pairs, modes, 2, pairs, inner))
    back = np.zeros((2, pairs, inner, 2, pairs, modes))
    phase = 2.0 * math.pi * np.outer(np.arange(modes), np.arange(inner)) / inner
    kept = (np.arange(modes) * GROUP <= extent // 3)[None, :]
    for pair in range(pairs):
        cosine, sine = 2.0 / extent * np.cos(phase), 2.0 / extent * np.sin(phase)
        fore[0, pair, :, 0, pair] = cosine
        fore[1, pair, :, 0, pair] = -sine
        fore[0, pair, :, 1, pair] = sine
        fore[1, pair, :, 1, pair] = cosine
        target = pair
        sources = [(pair, pair)]
        if extent < EDGE:
            slot, rest = divmod(pair, 2)
            sources = [(((1, 2, 0, 1)[slot]) * 2 + rest, pair)]
        for source, target in sources:
            cosine = 1.0 / extent * np.cos(phase).T * kept
            sine = 1.0 / extent * np.sin(phase).T * kept
            back[0, source, :, 0, target] = cosine
            back[1, source, :, 0, target] = sine
            back[0, source, :, 1, target] = -sine
            back[1, source, :, 1, target] = cosine
    fore = fore.reshape(128, 256)
    back = back.reshape(256, 128)
    return fore, back


def real_form(table):
    return np.block([[table.real, table.imag], [-table.imag, table.real]])


def doubled(table):
    return np.concatenate([table, table], axis=0)


def lane_maps():
    sign = np.array([[1.0, 1.0], [1.0, -1.0]])
    curl_y, curl_x, partner = np.zeros((4, 4)), np.zeros((4, 4)), np.zeros((4, 4))
    curl_y[2, 0] = curl_y[2, 3] = 1.0
    curl_y[0, 2] = -1.0
    curl_x[2, 1] = -1.0
    curl_x[1, 2] = 1.0
    partner[1, 0] = partner[1, 3] = partner[0, 1] = 1.0

    def coarse(slots):
        table = np.kron(np.kron(slots, sign), np.eye(8)).astype(complex)
        return real_form(table), real_form(1j * table)

    same = coarse(np.eye(4))
    spread_c = doubled(np.concatenate(same, axis=1))
    curl_c = np.concatenate([np.concatenate(coarse(slots), axis=1) for slots in (curl_y, curl_x)], axis=0)
    finish_c = doubled(np.concatenate([same[0], coarse(partner)[0]], axis=1))
    quarters, powers = np.arange(4), np.array([0, 2, 1, 3])
    table = np.kron(1j ** (np.outer(quarters, powers) % 4), np.eye(16))
    spread_f = doubled(np.concatenate([real_form(table), real_form(1j * table)], axis=1))
    finish_f = doubled(real_form(np.conj(table).T))
    place = np.zeros((3, 4, 2, 8, 4, 16))
    for component in range(3):
        for a in range(8):
            place[component, component, 0, a, 0, a] = 1.0
            place[component, component, 1, a, 3, a] = 1.0
    place_f = doubled(np.concatenate([real_form(table.reshape(64, 64).astype(complex)) for table in place], axis=1))
    return [
        np.concatenate(pair, axis=1).astype(ml_dtypes.bfloat16)
        for pair in ((spread_c, curl_c), (finish_c, spread_f), (place_f, finish_f))
    ]


def constant_tables():
    index = np.arange(ROWS)
    phase = 2.0 * math.pi * np.outer(np.arange(ROWS // 2) + 0.5, index) / ROWS
    along_y = np.concatenate([np.cos(phase), np.sin(phase)], axis=1)
    back_y = np.concatenate([np.cos(phase).T, np.sin(phase).T], axis=1)
    small = 2.0 * math.pi * np.outer(np.arange(GROUP) + 0.5, np.arange(GROUP)) / GROUP
    along_x = np.concatenate([np.cos(small), -np.sin(small)], axis=1).reshape(GROUP, 2, GROUP)
    half = GROUP // 2
    order = np.stack([np.arange(half), GROUP - 1 - np.arange(half)], axis=1).reshape(-1)
    back_x = np.kron(along_x[order].transpose(1, 2, 0).reshape(2 * GROUP, GROUP), np.eye(8))
    along_x = np.kron(along_x[:half].reshape(half, 2 * GROUP), np.eye(8))
    maps = lane_maps()
    matrices = list(halves(along_y)) + [np.concatenate(halves(back_y), axis=1), maps[0]]
    matrices += list(halves(along_x)) + [np.concatenate(halves(back_x), axis=1)]
    lane = np.arange(LANES)
    turns, inner_parts = [], []
    for extent in (EDGE // 2, EDGE):
        fore, back = lane_circle(extent)
        fore_high, fore_low = halves(fore)
        back_high, back_low = halves(back)
        inner_parts.append(
            np.concatenate([fore_high, fore_high, fore_low, np.concatenate([back_high, back_low], axis=1)], axis=0)
        )
        inner = extent // GROUP
        turn = 2.0 * math.pi * np.outer(index // 8, lane % inner / extent - 0.5 / GROUP)
        turns += [np.cos(turn), np.sin(turn)]
        if extent < EDGE:
            offset = (lane % 16) // 8
        else:
            offset = np.array([0, 2, 1, 3])[(lane % 64) // 16]
        turn = 2.0 * math.pi * np.outer(index, offset / extent - 0.5 / ROWS)
        turns += [np.cos(turn), np.sin(turn)]
    matrices.append(np.concatenate(inner_parts, axis=1))
    matrices += maps[1:]
    return np.concatenate(matrices, axis=0), np.concatenate(turns, axis=0).astype(np.float32)


def split(value):
    high = value.astype(BF16)
    return high, (value - high.astype(F32)).astype(BF16)


def dot(left, right):
    return jnp.dot(left, right, preferred_element_type=F32)


def roll(value, shift):
    return pltpu.roll(value, shift % LANES, axis=1)


def lanes_like(value):
    return lax.broadcasted_iota(jnp.int32, value.shape, 1)


def turned(value):
    other = roll(value, 64)
    return jnp.where(lanes_like(value) < 64, -other, other)


def tile(index):
    return pl.ds(index * LANES, LANES)


def chunks(size):
    return [pl.ds(start, size) for start in range(0, ROWS, size)]


def iterate(
    state_hbm, terms_hbm, matrices_hbm, turns_hbm,
    nodes_out, term_out, coarse_out,
    rhs_high, rhs_low, grid_buf,
    fore_send, fore_recv, back_send, back_recv, last_recv, hand_recv,
    parcel_send, parcel_recv, sweep, news,
    fine_send, fine_recv, fine_back_send, fine_back_recv, start_send, start_recv,
    right_one, right_two, mix_one, mix_two,
    curl_y, keep_same, keep_cross, damp_c, keep_same_r, keep_cross_r, damp_r, old_one, old_two,
    ky_f, damp_f, stiff_f, cos_f, sin_f, same_x, same_y, cross_f, mask_f,
    right_one_f, right_two_f, node_f,
    state_ref, terms_ref, matrices, turns,
    fore_sent, fore_got, back_sent, back_got, hand_sems, parcel_sems, news_sent, news_got,
    fine_sent, fine_got, fine_back_sent, fine_back_got, start_sems, load_sems,
    ready,
):
    loads = []
    for source, target, start, size in (
        (state_hbm, state_ref, 0, 768),
        (matrices_hbm, matrices, 0, 768),
        (turns_hbm, turns, 0, 1024),
        (state_hbm, state_ref, 768, 1536),
        (terms_hbm, terms_ref, 0, 2304),
        (matrices_hbm, matrices, 768, 1920),
        (turns_hbm, turns, 1024, 1024),
    ):
        rows = pl.ds(start, size)
        loads.append(pltpu.make_async_copy(source.at[rows], target.at[rows], load_sems.at[len(loads)]))
        loads[-1].start()

    def matrix(start, size, first=0, width=512):
        return matrices.at[pl.ds(start, size), pl.ds(first, width)]

    y_halves = (matrix(0, 256, 0, 256), matrix(0, 256, 256, 256))
    yt_high, yt_low = matrix(256, 256, 0, 256), matrix(256, 256, 256, 256)
    spread_map, curl_map = matrix(512, 256, 0, 256), matrix(512, 256, 256, 256)
    x_halves = (matrix(768, 256, 0, 256), matrix(768, 256, 256, 256))
    xt_high, xt_low = matrix(1024, 512, 0, 256), matrix(1024, 512, 256, 256)
    fore_high_c, fore_low_c, back_c = (matrix(*rows, 0, 256) for rows in ((1536, 256), (1792, 128), (1920, 256)))
    fore_high_f, fore_low_f, back_f = (matrix(*rows, 256, 256) for rows in ((1536, 256), (1792, 128), (1920, 256)))
    finish_map, spread_map_f = matrix(2176, 256, 0, 256), matrix(2176, 256, 256, 256)
    place_map, finish_map_f = matrix(2432, 256, 0, 384), matrix(2432, 256, 384, 128)
    turn_xc_c, turn_xs_c, turn_yc_c, turn_ys_c, turn_xc_f, turn_xs_f, turn_yc_f, turn_ys_f = (
        turns.at[pl.ds(start, ROWS), :] for start in range(0, 8 * ROWS, ROWS)
    )
    rank = lax.axis_index("tm")
    at_y, at_pz = lax.axis_index("py"), lax.axis_index("pz")
    low_z, core, high_z, at_x = rank // 2, rank % 2, at_pz // 4, at_pz % 4
    place = at_y * 8 + at_pz
    duty = high_z * 2 + core
    spot = at_y * 8 + low_z * 4 + at_x
    alone = high_z == low_z
    partner = (duty, at_y, low_z * 4 + at_x)

    barrier = pltpu.get_barrier_semaphore()
    number = rank * GROUP + place
    near = (core == 0) & (high_z + low_z < 2)

    def signal(semaphore, other):
        target = (other // GROUP, (other // 8) % 4, other % 8)
        pl.semaphore_signal(semaphore, inc=1, device_id=target, device_id_type=MESH)

    def greet_first(step, carry):
        signal(barrier, (place + step) % GROUP)
        return carry

    @pl.when(near)
    def _():
        @pl.when(rank > 0)
        def _():
            signal(barrier, place)

        lax.fori_loop(1, GROUP, greet_first, 0)

    def greet(step, carry):
        signal(barrier, GROUP + (number + 2 * GROUP + step) % (3 * GROUP))
        return carry

    @pl.when(rank == 0)
    def _():
        greet(0, 0)

    lax.fori_loop(1, 3 * GROUP, greet, 0)

    def block(position):
        return pl.ds(pl.multiple_of(position * 8, 8), 8)

    spots_y = [(at_y + step) % 4 for step in range(4)]
    spots_x = [(at_x + step) % 4 for step in range(4)]
    duty_z = [(low_z + step) % 2 for step in range(2)]
    rank_z = [(high_z + step) % 2 for step in range(2)]

    def spot_of(steps, step):
        spot_y, spot_x = spots_y[step[0]], spots_x[step[2]]
        if steps is DUTY:
            spot_z = duty_z[step[1]]
            address = lambda group: (spot_z * 2 + group % 2, spot_y, (group // 2) * 4 + spot_x)
        else:
            spot_z = rank_z[step[1]]
            address = lambda group: (group, spot_y, spot_z * 4 + spot_x)
        return spot_y * 8 + spot_z * 4 + spot_x, address

    def post(source, target, sent, got, steps, group, mine, count):
        for step in steps[:count]:
            index, address = spot_of(steps, step)
            pltpu.make_async_remote_copy(
                src_ref=source.at[block(index)],
                dst_ref=target.at[block(mine)],
                send_sem=sent,
                recv_sem=got,
                device_id=address(group),
                device_id_type=MESH,
            ).start()

    def post_own(source, target, sent, got, steps, group, mine):
        post(source, target, sent, got, steps, group, mine, GROUP - 1)
        pltpu.make_async_copy(source.at[block(mine)], target.at[block(mine)], got).start()

    def post_other(source, target, sent, got, steps, group, mine):
        post(source, target, sent, got, steps, group, mine, GROUP - 1)
        index, address = spot_of(steps, steps[-1])

        @pl.when(alone)
        def _():
            pltpu.make_async_copy(source.at[block(index)], target.at[block(mine)], got).start()

        @pl.when(jnp.logical_not(alone))
        def _():
            pltpu.make_async_remote_copy(
                src_ref=source.at[block(index)],
                dst_ref=target.at[block(mine)],
                send_sem=sent,
                recv_sem=got,
                device_id=address(group),
                device_id_type=MESH,
            ).start()

    def send_one(source, target, sent, got, address):
        return pltpu.make_async_remote_copy(
            src_ref=source, dst_ref=target, send_sem=sent, recv_sem=got, device_id=address, device_id_type=MESH
        )

    def to_partner(source, target, sent, got):
        @pl.when(alone)
        def _():
            pltpu.make_async_copy(source, target, got).start()

        @pl.when(jnp.logical_not(alone))
        def _():
            send_one(source, target, sent, got, partner).start()

    def receive(target, got):
        pltpu.make_async_copy(target, target, got).wait()

    def drain(source, sent, count):
        part = source.at[pl.ds(0, count * 8)]
        pltpu.make_async_copy(part, part, sent).wait()

    def drain_other(source, sent):
        @pl.when(alone)
        def _():
            drain(source, sent, GROUP - 1)

        @pl.when(jnp.logical_not(alone))
        def _():
            drain(source, sent, GROUP)

    place_f32, spot_f32 = place.astype(F32), spot.astype(F32)
    row = lax.broadcasted_iota(jnp.int32, (ROWS, LANES), 0)
    lane = lax.broadcasted_iota(jnp.int32, (ROWS, LANES), 1)

    def wave_tables(extent, mode_x, mode_y):
        wave_x, wave_y = UNIT * mode_x, UNIT * mode_y
        wave_sq = wave_x * wave_x + wave_y * wave_y
        anchor = (mode_x == 0) & (mode_y == 0)
        kept = (mode_x <= extent // 3) & (jnp.abs(mode_y) <= extent // 3) & ~anchor
        mask = jnp.where(kept, 1.0, 0.0).astype(F32)
        inverse = mask / jnp.where(anchor, 1.0, wave_sq)
        damp = 1.0 / (1.0 + HALF_STEP * VISCOSITY * wave_sq)
        return wave_x, wave_y, wave_sq, mask, inverse, damp

    def coarse_tables(position, same_ref, cross_ref, damp_ref):
        slot = (lane % 64) // 16
        mode_x = (lane % 8).astype(F32) * GROUP + position
        mode_y = (row - 256 * ((lane % 16) // 8)).astype(F32)
        wave_x, wave_y, wave_sq, mask, inverse, damp = wave_tables(EDGE // 2, mode_x, mode_y)
        same = jnp.where(slot == 2, mask, jnp.where(slot == 1, wave_x * wave_x, wave_y * wave_y) * inverse)
        same_ref[...] = same * (HALF_STEP * damp)
        cross_ref[...] = jnp.where(slot == 2, 0.0, -wave_x * wave_y * inverse) * (HALF_STEP * damp)
        damp_ref[...] = damp

    curl_y[...] = UNIT * (row - 256 * ((lane % 16) // 8)).astype(F32)

    def coarse_tile(ref, base, scale, target):
        for half in range(2):
            pieces = []
            for part in range(2):
                for component in (0, 1, 2, 0):
                    for quarter in (0, 3):
                        start = base + part * 384 + component * 8 + 2 * quarter + half
                        pieces.append(ref[pl.ds(start, 8, stride=24), :])
            target[pl.ds(half * 128, 128), :] = scale * jnp.concatenate(pieces, axis=0).T

    def fine_tile(ref, component, target):
        for half in range(2):
            pieces = []
            for part in range(2):
                for quarter in range(4):
                    start = part * 384 + component * 8 + 2 * quarter + half
                    pieces.append(ref[pl.ds(start, 16, stride=24), :])
            target[pl.ds(half * 128, 128), tile(component)] = jnp.concatenate(pieces, axis=0).T

    def half_products(matrices_two, first, count, target):
        part = pl.ds(first * LANES, count * LANES)
        halves_two = []
        for index, both_parts in enumerate(matrices_two):
            rows = pl.ds(index * ROWS, ROWS)
            if count == 1:
                both = dot(both_parts[...], pair(rhs_high[rows, part], rhs_low[rows, part]))
                halves_two.append(both[:128, :LANES] + both[128:, :LANES] + both[:128, LANES:])
                continue
            both = dot(both_parts[...], rhs_high[rows, part])
            rest = dot(both_parts[pl.ds(0, 128), :], rhs_low[rows, part])
            halves_two.append(both[:128] + both[128:] + rest)
        even, odd = halves_two
        total, difference = even + odd, even - odd
        for step in range(16):
            lines = slice(step * 8, step * 8 + 8)
            target[pl.ds(step * 16, 8), :] = total[lines]
            target[pl.ds(step * 16 + 8, 8), :] = difference[lines]

    def y_back(first, count):
        part = pl.ds(first * LANES, count * LANES)
        high, low = rhs_high[pl.ds(0, ROWS), part], rhs_low[pl.ds(0, ROWS), part]
        grid_buf[:, part] = dot(yt_high[...], high) + dot(yt_high[...], low) + dot(yt_low[...], high)

    def folded(value):
        mirrored = value.reshape(16, 2, 8, LANES)
        first, second = mirrored[:, 0].reshape(128, LANES), mirrored[:, 1].reshape(128, LANES)
        return first + second, first - second

    def stack_back(index, upper, lower):
        for start, value in ((0, upper), (128, lower)):
            high, low = split(value)
            rhs_high[pl.ds(start, 128), tile(index)] = high
            rhs_low[pl.ds(start, 128), tile(index)] = low

    def pair(high, low):
        return jnp.concatenate([high, low], axis=1)

    def twisted(rows, index, value, value_turned, cosine, sine):
        stack(rows, index, value * cosine + value_turned * sine, value_turned * cosine - value * sine)

    def stack(rows, index, first, second):
        high, low = split(first)
        rhs_high[rows, tile(index)] = high
        rhs_low[rows, tile(index)] = low
        high, low = split(second)
        lower = pl.ds(rows.start + ROWS, rows.size)
        rhs_high[lower, tile(index)] = high
        rhs_low[lower, tile(index)] = low

    def spread_coarse(source, target, position, deliver):
        lanes = lax.broadcasted_iota(jnp.int32, (1, LANES), 1) % 8
        mode_x = lanes.astype(F32) * GROUP + position
        weight = jnp.where(mode_x == 0, 0.5, 1.0)
        for index in range(2):
            for rows in chunks(128):
                velocity = source[rows, :] * weight
                cosine, sine = turn_yc_c[rows, :], turn_ys_c[rows, :]
                if index == 0:
                    mixed = dot(pair(*split(velocity)), spread_map[...])
                    twisted(rows, 0, mixed[:, :LANES], mixed[:, LANES:], cosine, sine)
                else:
                    high_y, low_y = split(velocity * curl_y[rows, :])
                    high_x, low_x = split(velocity * (UNIT * mode_x))
                    curled = dot(pair(high_y, high_x), curl_map[...]) + dot(pair(low_y, low_x), curl_map[...])
                    twisted(rows, 1, curled[:, LANES:], -curled[:, :LANES], cosine, sine)
            half_products(y_halves, index, 1, target.at[:, tile(index)])
            deliver(index)

    def fields_to(slot, target, index):
        return (
            fore_send.at[slot].at[:, tile(index)],
            fore_recv.at[target].at[:, tile(index)],
            fore_sent.at[2 * slot + index],
            fore_got.at[2 * target + index],
        )

    def to_grid(source, first, count, fore_high, fore_low, cosine, sine):
        every = pl.ds(0, ROWS)
        for index in range(count):
            high, low = split(source[:, tile(index)])
            inner = dot(pair(high, low), fore_high[...]) + dot(high, fore_low[...])
            real, imag = inner[:, :LANES], inner[:, LANES:]
            stack(every, first + index, real * cosine - imag * sine, real * sine + imag * cosine)
        part = pl.ds(first * LANES, count * LANES)
        half_products(x_halves, first, count, grid_buf.at[:, part])

    def from_grid(value, target, back, cosine, sine):
        high, low = split(value)
        both = dot(xt_high[...], pair(high, low))
        outer = both[:, :LANES] + both[:, LANES:] + dot(xt_low[...], high)
        real, imag = outer[:ROWS], outer[ROWS:]
        high, low = split(pair(real * cosine + imag * sine, imag * cosine - real * sine))
        both = dot(high, back[...])
        target[...] = both[:, :LANES] + both[:, LANES:] + dot(low, back[:, :LANES])

    def grid_coarse(slot, target):
        cosine, sine = turn_xc_c[...], turn_xs_c[...]
        for index in range(2):
            source = fore_recv.at[slot].at[:, tile(index)]
            receive(source, fore_got.at[2 * slot + index])
            to_grid(source, index, 1, fore_high_c, fore_low_c, cosine, sine)
        speed, spin = grid_buf[:, tile(0)], grid_buf[:, tile(1)]
        crossed = speed * roll(spin, -32) - roll(speed, -32) * spin
        from_grid(crossed, target, back_c, cosine, sine)

    def finish_coarse(source, start_ref, right_ref, target, same_ref, cross_ref, damp_ref):
        even, odd = folded(source[...])
        stack_back(0, even, -turned(odd))
        stack_back(1, turned(even), odd)
        y_back(0, 2)
        for rows in chunks(128):
            value = grid_buf[rows, tile(0)] * turn_yc_c[rows, :] - grid_buf[rows, tile(1)] * turn_ys_c[rows, :]
            modes = dot(pair(*split(value)), finish_map[...])
            term = same_ref[rows, :] * modes[:, :LANES] + cross_ref[rows, :] * modes[:, LANES:]
            target[rows, :] = damp_ref[rows, :] * (start_ref[rows, :] + right_ref[rows, :]) + term

    loads[0].wait()
    coarse_tile(state_ref, 0, 0.5, parcel_send.at[0])
    loads[1].wait()
    loads[2].wait()

    @pl.when(rank == 0)
    def _():
        spread_coarse(parcel_send.at[0], fore_send.at[0], place_f32, lambda index: None)

    @pl.when(rank > 0)
    def _():
        pl.semaphore_wait(barrier, 4 * GROUP - 1)

    def greet_last(step, carry):
        signal(ready, (place + step) % GROUP)
        return carry

    @pl.when(jnp.logical_not(near))
    def _():
        lax.fori_loop(0, GROUP, greet_last, 0)

    @pl.when(rank == 0)
    def _():
        pl.semaphore_wait(barrier, 3 * GROUP // 2 - 1)
        for index in range(2):
            post_other(*fields_to(0, 0, index), DUTY, 0, place)

    def combine(a, carry):
        wave_x = UNIT * (a.astype(F32) * GROUP + place_f32)
        sub = lax.broadcasted_iota(jnp.int32, (8, LANES), 0)
        mode = sub * 128 + lax.broadcasted_iota(jnp.int32, (8, LANES), 1)
        wave_y = UNIT * jnp.where(mode < EDGE // 2, mode, mode - EDGE).astype(F32)
        stiff = VISCOSITY * (wave_x * wave_x + wave_y * wave_y)
        for part in range(2):
            for component in range(3):
                base = pl.multiple_of(a * 24 + (part * 384 + component * 8), 8)
                rows = pl.ds(base, 8)
                states = [state_ref[pl.ds(base + node * 768, 8), :] for node in range(3)]
                terms = [terms_ref[pl.ds(base + node * 768, 8), :] for node in range(3)]
                one = sum(w * s for w, s in zip(STATE_ONE, states))
                two = sum(w * s for w, s in zip(STATE_TWO, states))
                mix_one[rows, :] = one
                mix_two[rows, :] = two
                right_one[rows, :] = sum(w * t for w, t in zip(TERM_ONE, terms)) + stiff * one
                right_two[rows, :] = sum(w * t for w, t in zip(TERM_TWO, terms)) + stiff * two
                start_send[rows, :] = states[2] + HALF_STEP * terms[2]
        return carry

    for index in (3, 4, 5, 6):
        loads[index].wait()
    lax.fori_loop(0, 16, combine, 0, unroll=2)

    following = (rank + 1, at_y, at_pz)

    @pl.when(rank == 0)
    def _():
        pl.semaphore_wait(ready, 5 * GROUP // 2)

    @pl.when(rank < 3)
    def _():
        send_one(start_send, start_recv, start_sems.at[0], start_sems.at[1], following).start()

    coarse_tile(right_one, 0, 0.5, parcel_send.at[1])
    coarse_tile(right_two, 0, 0.5, parcel_send.at[2])
    to_partner(parcel_send, parcel_recv, parcel_sems.at[0], parcel_sems.at[1])
    coarse_tables(spot_f32, keep_same, keep_cross, damp_c)

    def coarse_sweep():
        grid_coarse(0, back_send.at[0])
        post_own(back_send.at[0], back_recv.at[0], back_sent.at[0], back_got.at[0], DUTY, duty, spot)
        receive(parcel_recv, parcel_sems.at[1])

        @pl.when(duty == 0)
        def _():
            sweep[0] = parcel_recv[0]

        @pl.when(duty > 0)
        def _():
            receive(hand_recv, hand_sems.at[1])
            sweep[0] = hand_recv[...]

        receive(back_recv.at[0], back_got.at[0])
        tables = (keep_same, keep_cross, damp_c)
        finish_coarse(back_recv.at[0], sweep.at[0], parcel_recv.at[1], sweep.at[1], *tables)
        spread_coarse(
            sweep.at[1],
            fore_send.at[1],
            spot_f32,
            lambda index: post_own(*fields_to(1, 1, index), DUTY, duty, spot),
        )
        to_partner(sweep.at[pl.ds(0, 2)], news.at[pl.ds(0, 2)], news_sent.at[0], news_got.at[0])
        grid_coarse(1, back_send.at[1])

        @pl.when(duty == 3)
        def _():
            post_other(back_send.at[1], last_recv, back_sent.at[1], back_got.at[2], RANK, 3, spot)

        @pl.when(duty < 3)
        def _():
            post_own(back_send.at[1], back_recv.at[1], back_sent.at[1], back_got.at[1], DUTY, duty, spot)
            receive(back_recv.at[1], back_got.at[1])
            finish_coarse(back_recv.at[1], sweep.at[1], parcel_recv.at[2], sweep.at[2], *tables)
            after = duty + 1
            spread_coarse(
                sweep.at[2],
                fore_send.at[2],
                spot_f32,
                lambda index: post(*fields_to(2, 0, index), DUTY, after, spot, GROUP),
            )
            address = (low_z * 2 + after % 2, at_y, (after // 2) * 4 + at_x)
            send_one(sweep.at[2], hand_recv, hand_sems.at[0], hand_sems.at[1], address).start()
            to_partner(sweep.at[2], news.at[2], news_sent.at[1], news_got.at[1])

    coarse_tile(mix_one, 0, 0.5, old_one)
    coarse_tile(mix_two, 0, 0.5, old_two)
    quarter = (lane % 64) // 16
    mode_x = (lane % 16).astype(F32) * GROUP + place_f32
    mode_y = (row + 256 * quarter - jnp.where(quarter >= 2, EDGE, 0)).astype(F32)
    wave_x, wave_y, wave_sq, mask, inverse, damp = wave_tables(EDGE, mode_x, mode_y)
    ky_f[...] = wave_y
    damp_f[...] = damp
    stiff_f[...] = (2.0 * VISCOSITY) * wave_sq
    same_x[...] = wave_y * wave_y * inverse
    same_y[...] = wave_x * wave_x * inverse
    cross_f[...] = -wave_x * wave_y * inverse
    mask_f[...] = mask
    weight = jnp.where(mode_x == 0, 0.5, 1.0)
    cos_f[...] = turn_yc_f[...] * weight
    sin_f[...] = turn_ys_f[...] * weight

    @pl.when(rank == 3)
    def _():
        coarse_tables(place_f32, keep_same_r, keep_cross_r, damp_r)

    def correct_fine(weights, old_ref, target):
        for rows in chunks(128):
            nodes = [news[node, rows, :] for node in range(3)]
            change = sum(w * n for w, n in zip(weights, nodes)) - old_ref[rows, :]
            placed = dot(pair(*split(change)), place_map[...])
            stiff = stiff_f[rows, :]
            for component in range(3):
                part = tile(component)
                lanes = slice(component * LANES, (component + 1) * LANES)
                target[rows, part] = target[rows, part] + stiff * placed[:, lanes]

    def start_fine():
        correct_fine(STATE_ONE, old_one, right_one_f)
        for component in range(3):
            node_f[:, tile(component)] = right_one_f[:, tile(component)] * damp_f[...]

    def fine_field(index, rows):
        x, y, z = (node_f.at[rows, tile(component)] for component in range(3))
        if index < 3:
            return (x, y, z)[index][...]
        ky = ky_f[rows, :]
        kx = UNIT * ((lanes_like(ky) % 16).astype(F32) * GROUP + place_f32)
        if index == 3:
            return ky * z[...]
        if index == 4:
            return -kx * z[...]
        return kx * y[...] - ky * x[...]

    def spread_fine(first):
        for rows in chunks(128):
            cosine, sine = cos_f[rows, :], sin_f[rows, :]
            for index in (first, first + 1):
                mixed = dot(pair(*split(fine_field(index, rows))), spread_map_f[...])
                if index < 3:
                    twisted(rows, index, mixed[:, :LANES], mixed[:, LANES:], cosine, sine)
                else:
                    twisted(rows, index, mixed[:, LANES:], -mixed[:, :LANES], cosine, sine)
        half_products(y_halves, first, 2, fine_send.at[first // 2])

    def give_back(source, component, target, base):
        for half in range(2):
            block_t = source[pl.ds(half * 128, 128), tile(component)].T
            for part in range(2):
                for quarter in range(4):
                    start = base + part * 384 + component * 8 + 2 * quarter + half
                    first = (part * 4 + quarter) * 16
                    target[pl.ds(start, 16, stride=24), :] = block_t[first : first + 16]

    def give_back_coarse(source, base):
        for half in range(2):
            block_t = source[pl.ds(half * 128, 128), :].T
            for part in range(2):
                for component in range(3):
                    for quarter in range(2):
                        start = base + part * 96 + component * 4 + 2 * quarter + half
                        first = part * 64 + component * 16 + quarter * 8
                        coarse_out[pl.ds(start, 8, stride=12), :] = block_t[first : first + 8]

    def cross_fine(component):
        second, third = (component + 1) % 3, (component + 2) % 3
        fields = [grid_buf[:, tile(index)] for index in (second, third, second + 3, third + 3)]
        return fields[0] * fields[3] - fields[1] * fields[2]

    def gather_fine(component):
        even, odd = folded(fine_back_recv[component])
        stack_back(component, even, -turned(odd))
        y_back(component, 1)
        for rows in chunks(128):
            value = grid_buf[rows, tile(component)]
            value = value * turn_yc_f[rows, :] - turned(value) * turn_ys_f[rows, :]
            right_one_f[rows, tile(component)] = dot(pair(*split(value)), finish_map_f[...])

    def finish_fine():
        for rows in chunks(64):
            modes = [right_one_f[rows, tile(component)] for component in range(3)]
            cross = cross_f[rows, :]
            results = [
                same_x[rows, :] * modes[0] + cross * modes[1],
                same_y[rows, :] * modes[1] + cross * modes[0],
                mask_f[rows, :] * modes[2],
            ]
            for component, value in enumerate(results):
                part = tile(component)
                right_one_f[rows, part] = value
                total = node_f[rows, part] + HALF_STEP * value + right_two_f[rows, part]
                node_f[rows, part] = total * damp_f[rows, :]

    def fine_sweep():
        @pl.when(rank == 0)
        def _():
            first = pl.ds(0, 768)
            right_one[...] = right_one[...] + state_ref[first, :] + HALF_STEP * terms_ref[first, :]

        @pl.when(rank > 0)
        def _():
            receive(start_recv, start_sems.at[1])
            right_one[...] = right_one[...] + start_recv[...]

        for component in range(3):
            fine_tile(right_one, component, right_one_f)
            fine_tile(right_two, component, right_two_f)
        receive(news.at[pl.ds(0, 2)], news_got.at[0])

        @pl.when(rank < 3)
        def _():
            receive(news.at[2], news_got.at[1])

        @pl.when(rank == 3)
        def _():
            receive(last_recv, back_got.at[2])
            tables = (keep_same_r, keep_cross_r, damp_r)
            finish_coarse(last_recv, news.at[1], parcel_send.at[2], news.at[2], *tables)

        start_fine()
        for part in range(3):
            spread_fine(2 * part)
            pairs = (fine_send.at[part], fine_recv.at[part], fine_sent.at[part], fine_got.at[part])
            post_own(*pairs, RANK, rank, place)
        correct_fine(STATE_TWO, old_two, right_two_f)
        give_back_coarse(news.at[1], 0)
        give_back_coarse(news.at[2], 192)
        for part in range(3):
            receive(fine_recv.at[part], fine_got.at[part])
            to_grid(fine_recv.at[part], 2 * part, 2, fore_high_f, fore_low_f, turn_xc_f[...], turn_xs_f[...])
        for part in range(3):
            from_grid(cross_fine(part), fine_back_send.at[part], back_f, turn_xc_f[...], turn_xs_f[...])
            pairs = (fine_back_send.at[part], fine_back_recv.at[part])
            post_own(*pairs, fine_back_sent.at[part], fine_back_got.at[part], RANK, rank, place)
        for component in range(3):
            give_back(node_f, component, nodes_out, 0)
        for part in range(3):
            receive(fine_back_recv.at[part], fine_back_got.at[part])
            gather_fine(part)
        finish_fine()
        for component in range(3):
            give_back(right_one_f, component, term_out, 0)
            give_back(node_f, component, nodes_out, 768)

    early = high_z * (1 - low_z)

    def phase(step, carry):
        fine_now = (step + early) % 2

        @pl.when(fine_now == 0)
        def _():
            coarse_sweep()

        @pl.when(fine_now == 1)
        def _():
            fine_sweep()

        return carry

    lax.fori_loop(0, 2, phase, 0)

    @pl.when(rank == 0)
    def _():
        for index in range(2):
            drain_other(fore_send.at[0].at[:, tile(index)], fore_sent.at[index])

    for index in range(2):
        drain(fore_send.at[1].at[:, tile(index)], fore_sent.at[2 + index], GROUP - 1)
    drain(back_send.at[0], back_sent.at[0], GROUP - 1)
    for part in range(3):
        drain(fine_send.at[part], fine_sent.at[part], GROUP - 1)
        drain(fine_back_send.at[part], fine_back_sent.at[part], GROUP - 1)

    @pl.when(duty == 3)
    def _():
        drain_other(back_send.at[1], back_sent.at[1])

    @pl.when(duty < 3)
    def _():
        drain(back_send.at[1], back_sent.at[1], GROUP - 1)
        for index in range(2):
            drain(fore_send.at[2].at[:, tile(index)], fore_sent.at[4 + index], GROUP)
        receive(sweep.at[2], hand_sems.at[0])

    @pl.when(jnp.logical_not(alone))
    def _():
        receive(parcel_send, parcel_sems.at[0])
        receive(sweep.at[pl.ds(0, 2)], news_sent.at[0])

        @pl.when(duty < 3)
        def _():
            receive(sweep.at[2], news_sent.at[1])

    @pl.when(rank < 3)
    def _():
        receive(start_send, start_sems.at[0])


def shards(fine_state, fine_terms):
    matrices, turns = constant_tables()
    full, natural, wide = (ROWS, LANES), (768, LANES), (ROWS, 3 * LANES)
    dma = pltpu.SemaphoreType.DMA
    tiles = (3, ROWS, LANES)
    shapes = [(ROWS, 6 * LANES)]
    shapes += [(3, ROWS, 2 * LANES), (2, ROWS, 2 * LANES), (2, ROWS, LANES), (2, ROWS, LANES), full, full]
    shapes += [tiles] * 4 + [(3, ROWS, 2 * LANES)] * 2 + [tiles] * 2
    shapes += [natural] * 6 + [full] * (9 + 9) + [wide] * 3 + [(2304, LANES)] * 2
    scratch = [pltpu.VMEM((2 * ROWS, 6 * LANES), BF16)] * 2 + [pltpu.VMEM(shape, F32) for shape in shapes]
    scratch += [pltpu.VMEM(matrices.shape, BF16), pltpu.VMEM(turns.shape, F32)]
    scratch += [dma((count,)) for count in (6, 4, 2, 3, 2, 2, 2, 2, 3, 3, 3, 3, 2, 7)]
    scratch += [pltpu.SemaphoreType.REGULAR]
    outs = pl.pallas_call(
        iterate,
        out_shape=(
            jax.ShapeDtypeStruct((1536, LANES), F32),
            jax.ShapeDtypeStruct((768, LANES), F32),
            jax.ShapeDtypeStruct((384, LANES), F32),
        ),
        in_specs=[pl.BlockSpec(memory_space=pltpu.HBM)] * 4,
        out_specs=[pl.BlockSpec(memory_space=pltpu.VMEM)] * 3,
        scratch_shapes=scratch,
        compiler_params=pltpu.CompilerParams(
            collective_id=0, has_side_effects=True, vmem_limit_bytes=52 * 1024 * 1024
        ),
        name="iterate",
    )(fine_state.reshape(2304, LANES), fine_terms.reshape(2304, LANES), jnp.asarray(matrices), jnp.asarray(turns))
    return (
        outs[0].reshape(1, 2, 2, 16, 1, 3, 1, 1024),
        outs[1].reshape(1, 2, 16, 1, 3, 1, 1024),
        outs[2].reshape(1, 2, 2, 8, 1, 3, 1, 512),
    )


def solution(mesh):
    split_over = P("tm", None, None, None, ("py", "pz"), None, None, None)
    return jax.shard_map(
        shards,
        mesh=mesh,
        in_specs=(split_over, split_over),
        out_specs=(
            split_over,
            P("tm", None, None, ("py", "pz"), None, None, None),
            split_over,
        ),
        check_vma=False,
    )
```

```python
import math

import jax
import jax.numpy as jnp
import ml_dtypes
import numpy as np
from jax import lax
from jax.experimental import pallas as pl
from jax.experimental.pallas import tpu as pltpu
from jax.sharding import PartitionSpec as P

EDGE = 1024
VISCOSITY = 0.5
TIME_STEP = 0.2
HALF_STEP = 0.5 * TIME_STEP
WEIGHTS = ((5.0 / 24.0, 1.0 / 3.0, -1.0 / 24.0), (-1.0 / 24.0, 1.0 / 3.0, 5.0 / 24.0))
UNIT = 2.0 * math.pi / EDGE
GROUP = 32
ROWS = 256
LANES = 128
F32 = jnp.float32
BF16 = jnp.bfloat16
MESH = pl.DeviceIdType.MESH
TERM_ONE = [TIME_STEP * w for w in WEIGHTS[0]]
TERM_ONE[0] -= HALF_STEP
TERM_TWO = [TIME_STEP * w for w in WEIGHTS[1]]
TERM_TWO[1] -= HALF_STEP
STATE_ONE = [-TIME_STEP * w for w in WEIGHTS[0]]
STATE_ONE[1] += HALF_STEP
STATE_TWO = [-TIME_STEP * w for w in WEIGHTS[1]]
STATE_TWO[2] += HALF_STEP


HOPS = (0, 1, 2, 1)
DUTY, RANK = (
    sorted(
        ((y, z, x) for y in range(4) for z in range(2) for x in range(4)),
        key=lambda step: -(HOPS[step[0]] + apart * step[1] + HOPS[step[2]]),
    )
    for apart in (1, 2)
)


def halves(table):
    high = table.astype(ml_dtypes.bfloat16)
    low = (table - high.astype(np.float64)).astype(ml_dtypes.bfloat16)
    return high, low


def lane_circle(extent):
    inner = extent // GROUP
    modes = inner // 2
    pairs = 64 // modes
    fore = np.zeros((2, pairs, modes, 2, pairs, inner))
    back = np.zeros((2, pairs, inner, 2, pairs, modes))
    phase = 2.0 * math.pi * np.outer(np.arange(modes), np.arange(inner)) / inner
    kept = (np.arange(modes) * GROUP <= extent // 3)[None, :]
    for pair in range(pairs):
        cosine, sine = 2.0 / extent * np.cos(phase), 2.0 / extent * np.sin(phase)
        fore[0, pair, :, 0, pair] = cosine
        fore[1, pair, :, 0, pair] = -sine
        fore[0, pair, :, 1, pair] = sine
        fore[1, pair, :, 1, pair] = cosine
        target = pair
        sources = [(pair, pair)]
        if extent < EDGE:
            slot, rest = divmod(pair, 2)
            sources = [(((1, 2, 0, 1)[slot]) * 2 + rest, pair)]
        for source, target in sources:
            cosine = 1.0 / extent * np.cos(phase).T * kept
            sine = 1.0 / extent * np.sin(phase).T * kept
            back[0, source, :, 0, target] = cosine
            back[1, source, :, 0, target] = sine
            back[0, source, :, 1, target] = -sine
            back[1, source, :, 1, target] = cosine
    fore = fore.reshape(128, 256)
    back = back.reshape(256, 128)
    return fore, back


def real_form(table):
    return np.block([[table.real, table.imag], [-table.imag, table.real]])


def doubled(table):
    return np.concatenate([table, table], axis=0)


def lane_maps():
    sign = np.array([[1.0, 1.0], [1.0, -1.0]])
    curl_y, curl_x, partner = np.zeros((4, 4)), np.zeros((4, 4)), np.zeros((4, 4))
    curl_y[2, 0] = curl_y[2, 3] = 1.0
    curl_y[0, 2] = -1.0
    curl_x[2, 1] = -1.0
    curl_x[1, 2] = 1.0
    partner[1, 0] = partner[1, 3] = partner[0, 1] = 1.0

    def coarse(slots):
        table = np.kron(np.kron(slots, sign), np.eye(8)).astype(complex)
        return real_form(table), real_form(1j * table)

    same = coarse(np.eye(4))
    spread_c = doubled(np.concatenate(same, axis=1))
    curl_c = np.concatenate([np.concatenate(coarse(slots), axis=1) for slots in (curl_y, curl_x)], axis=0)
    finish_c = doubled(np.concatenate([same[0], coarse(partner)[0]], axis=1))
    quarters, powers = np.arange(4), np.array([0, 2, 1, 3])
    table = np.kron(1j ** (np.outer(quarters, powers) % 4), np.eye(16))
    spread_f = doubled(np.concatenate([real_form(table), real_form(1j * table)], axis=1))
    finish_f = doubled(real_form(np.conj(table).T))
    phases = 1j ** (np.outer((0, 3), powers) % 4)

    def change(sources):
        moves = np.zeros((4, 2), dtype=complex)
        for field, source, factor in sources:
            moves[source, field] = factor
        table = np.kron(np.kron(moves, phases), np.eye(8))
        return np.concatenate([real_form(table), real_form(1j * table)], axis=1)

    change_one = doubled(change(((0, 0, 1), (1, 1, 1))))
    change_two = np.concatenate([change(((0, 2, 1),)), change(((1, 2, 1j),))], axis=0)
    change_three = np.concatenate([change(((1, 0, -1j),)), change(((0, 2, -1j), (1, 1, 1j)))], axis=0)
    place = np.zeros((3, 4, 2, 8, 4, 16))
    for component in range(3):
        for a in range(8):
            place[component, component, 0, a, 0, a] = 1.0
            place[component, component, 1, a, 3, a] = 1.0
    place_f = doubled(np.concatenate([real_form(table.reshape(64, 64).astype(complex)) for table in place], axis=1))
    return [
        np.concatenate(pair, axis=1).astype(ml_dtypes.bfloat16)
        for pair in (
            (spread_c, curl_c),
            (finish_c, spread_f),
            (place_f, finish_f),
            (change_one, change_two),
            (change_three, 0.0 * change_three),
        )
    ]


def constant_tables():
    index = np.arange(ROWS)
    phase = 2.0 * math.pi * np.outer(np.arange(ROWS // 2) + 0.5, index) / ROWS
    along_y = np.concatenate([np.cos(phase), np.sin(phase)], axis=1)
    back_y = np.concatenate([np.cos(phase).T, np.sin(phase).T], axis=1)
    small = 2.0 * math.pi * np.outer(np.arange(GROUP) + 0.5, np.arange(GROUP)) / GROUP
    along_x = np.concatenate([np.cos(small), -np.sin(small)], axis=1).reshape(GROUP, 2, GROUP)
    half = GROUP // 2
    order = np.stack([np.arange(half), GROUP - 1 - np.arange(half)], axis=1).reshape(-1)
    back_x = np.kron(along_x[order].transpose(1, 2, 0).reshape(2 * GROUP, GROUP), np.eye(8))
    along_x = np.kron(along_x[:half].reshape(half, 2 * GROUP), np.eye(8))
    maps = lane_maps()
    matrices = list(halves(along_y)) + [np.concatenate(halves(back_y), axis=1), maps[0]]
    matrices += list(halves(along_x)) + [np.concatenate(halves(back_x), axis=1)]
    lane = np.arange(LANES)
    turns, inner_parts = [], []
    for extent in (EDGE // 2, EDGE):
        fore, back = lane_circle(extent)
        fore_high, fore_low = halves(fore)
        back_high, back_low = halves(back)
        inner_parts.append(
            np.concatenate([fore_high, fore_high, fore_low, np.concatenate([back_high, back_low], axis=1)], axis=0)
        )
        inner = extent // GROUP
        turn = 2.0 * math.pi * np.outer(index // 8, lane % inner / extent - 0.5 / GROUP)
        turns += [np.cos(turn), np.sin(turn)]
        if extent < EDGE:
            offset = (lane % 16) // 8
        else:
            offset = np.array([0, 2, 1, 3])[(lane % 64) // 16]
        turn = 2.0 * math.pi * np.outer(index, offset / extent - 0.5 / ROWS)
        turns += [np.cos(turn), np.sin(turn)]
    matrices.append(np.concatenate(inner_parts, axis=1))
    matrices += maps[1:]
    inner = EDGE // GROUP
    phase = 2.0 * math.pi * np.outer(np.arange(8), np.arange(inner)) / inner
    table = np.zeros((2, 4, 8, 2, 2, 4, inner))
    for field in range(2):
        for position in range(4):
            table[field, position, :, field, 0, position] = 2.0 / EDGE * np.cos(phase)
            table[field, position, :, field, 1, position] = 2.0 / EDGE * np.sin(phase)
    table = table.reshape(64, 2, 2, 128)
    table = np.concatenate([table, np.stack([-table[:, :, 1], table[:, :, 0]], axis=2)], axis=0)
    high, low = halves(table.reshape(128, 512))
    matrices += [high, high, low]
    turn = 2.0 * math.pi * np.outer(index, np.array([0, 2, 1, 3])[(lane % 32) // 8] / EDGE - 0.5 / ROWS)
    turns += [np.cos(turn), np.sin(turn)]
    return np.concatenate(matrices, axis=0), np.concatenate(turns, axis=0).astype(np.float32)


def split(value):
    high = value.astype(BF16)
    return high, (value - high.astype(F32)).astype(BF16)


def dot(left, right):
    return jnp.dot(left, right, preferred_element_type=F32)


def roll(value, shift):
    return pltpu.roll(value, shift % LANES, axis=1)


def lanes_like(value):
    return lax.broadcasted_iota(jnp.int32, value.shape, 1)


def turned(value):
    other = roll(value, 64)
    return jnp.where(lanes_like(value) < 64, -other, other)


def tile(index):
    return pl.ds(index * LANES, LANES)


def chunks(size):
    return [pl.ds(start, size) for start in range(0, ROWS, size)]


def iterate(
    state_hbm, terms_hbm, matrices_hbm, turns_hbm,
    nodes_out, term_out, coarse_out,
    rhs_high, rhs_low, grid_buf,
    fore_send, fore_recv, back_send, back_recv, last_recv, hand_recv,
    parcel_send, parcel_recv, sweep, news,
    fine_send, fine_recv, fine_back_send, fine_back_recv, start_send, start_recv,
    right_one, right_two, mix_one, mix_two,
    curl_y, keep_same, keep_cross, damp_c, keep_same_r, keep_cross_r, damp_r, old_one, old_two,
    ky_f, damp_f, stiff_f, cos_f, sin_f, same_x, same_y, cross_f, mask_f,
    right_one_f, right_two_f, node_f,
    base_grid, change_send, change_recv, stiff_r,
    state_ref, terms_ref, matrices, turns,
    fore_sent, fore_got, back_sent, back_got, hand_sems, parcel_sems, news_sent, news_got,
    fine_sent, fine_got, fine_back_sent, fine_back_got, start_sems, load_sems,
    change_sent, change_got, ready,
):
    loads = []
    for source, target, start, size in (
        (state_hbm, state_ref, 0, 768),
        (matrices_hbm, matrices, 0, 768),
        (turns_hbm, turns, 0, 1024),
        (state_hbm, state_ref, 768, 1536),
        (terms_hbm, terms_ref, 0, 2304),
        (matrices_hbm, matrices, 768, 2816),
        (turns_hbm, turns, 1024, 1536),
    ):
        rows = pl.ds(start, size)
        loads.append(pltpu.make_async_copy(source.at[rows], target.at[rows], load_sems.at[len(loads)]))
        loads[-1].start()

    def matrix(start, size, first=0, width=512):
        return matrices.at[pl.ds(start, size), pl.ds(first, width)]

    y_halves = (matrix(0, 256, 0, 256), matrix(0, 256, 256, 256))
    yt_high, yt_low = matrix(256, 256, 0, 256), matrix(256, 256, 256, 256)
    spread_map, curl_map = matrix(512, 256, 0, 256), matrix(512, 256, 256, 256)
    x_halves = (matrix(768, 256, 0, 256), matrix(768, 256, 256, 256))
    xt_high, xt_low = matrix(1024, 512, 0, 256), matrix(1024, 512, 256, 256)
    fore_high_c, fore_low_c, back_c = (matrix(*rows, 0, 256) for rows in ((1536, 256), (1792, 128), (1920, 256)))
    fore_high_f, fore_low_f, back_f = (matrix(*rows, 256, 256) for rows in ((1536, 256), (1792, 128), (1920, 256)))
    finish_map, spread_map_f = matrix(2176, 256, 0, 256), matrix(2176, 256, 256, 256)
    place_map, finish_map_f = matrix(2432, 256, 0, 384), matrix(2432, 256, 384, 128)
    change_maps = (matrix(2688, 256, 0, 256), matrix(2688, 256, 256, 256), matrix(2944, 256, 0, 256))
    change_fore_high, change_fore_low = matrix(3200, 256), matrix(3456, 128)
    turn_xc_c, turn_xs_c, turn_yc_c, turn_ys_c, turn_xc_f, turn_xs_f, turn_yc_f, turn_ys_f, turn_c, turn_s = (
        turns.at[pl.ds(start, ROWS), :] for start in range(0, 10 * ROWS, ROWS)
    )
    rank = lax.axis_index("tm")
    at_y, at_pz = lax.axis_index("py"), lax.axis_index("pz")
    low_z, core, high_z, at_x = rank // 2, rank % 2, at_pz // 4, at_pz % 4
    place = at_y * 8 + at_pz
    duty = high_z * 2 + core
    spot = at_y * 8 + low_z * 4 + at_x
    alone = high_z == low_z
    partner = (duty, at_y, low_z * 4 + at_x)

    barrier = pltpu.get_barrier_semaphore()
    number = rank * GROUP + place
    near = (core == 0) & (high_z + low_z < 2)

    def signal(semaphore, other):
        target = (other // GROUP, (other // 8) % 4, other % 8)
        pl.semaphore_signal(semaphore, inc=1, device_id=target, device_id_type=MESH)

    def greet_first(step, carry):
        signal(barrier, (place + step) % GROUP)
        return carry

    @pl.when(near)
    def _():
        @pl.when(rank > 0)
        def _():
            signal(barrier, place)

        lax.fori_loop(1, GROUP, greet_first, 0)

    def greet(step, carry):
        signal(barrier, GROUP + (number + 2 * GROUP + step) % (3 * GROUP))
        return carry

    @pl.when(rank == 0)
    def _():
        greet(0, 0)

    lax.fori_loop(1, 3 * GROUP, greet, 0)

    def block(position):
        return pl.ds(pl.multiple_of(position * 8, 8), 8)

    spots_y = [(at_y + step) % 4 for step in range(4)]
    spots_x = [(at_x + step) % 4 for step in range(4)]
    duty_z = [(low_z + step) % 2 for step in range(2)]
    rank_z = [(high_z + step) % 2 for step in range(2)]

    def spot_of(steps, step):
        spot_y, spot_x = spots_y[step[0]], spots_x[step[2]]
        if steps is DUTY:
            spot_z = duty_z[step[1]]
            address = lambda group: (spot_z * 2 + group % 2, spot_y, (group // 2) * 4 + spot_x)
        else:
            spot_z = rank_z[step[1]]
            address = lambda group: (group, spot_y, spot_z * 4 + spot_x)
        return spot_y * 8 + spot_z * 4 + spot_x, address

    def post(source, target, sent, got, steps, group, mine, count):
        for step in steps[:count]:
            index, address = spot_of(steps, step)
            pltpu.make_async_remote_copy(
                src_ref=source.at[block(index)],
                dst_ref=target.at[block(mine)],
                send_sem=sent,
                recv_sem=got,
                device_id=address(group),
                device_id_type=MESH,
            ).start()

    def post_own(source, target, sent, got, steps, group, mine):
        post(source, target, sent, got, steps, group, mine, GROUP - 1)
        pltpu.make_async_copy(source.at[block(mine)], target.at[block(mine)], got).start()

    def post_other(source, target, sent, got, steps, group, mine):
        post(source, target, sent, got, steps, group, mine, GROUP - 1)
        index, address = spot_of(steps, steps[-1])

        @pl.when(alone)
        def _():
            pltpu.make_async_copy(source.at[block(index)], target.at[block(mine)], got).start()

        @pl.when(jnp.logical_not(alone))
        def _():
            pltpu.make_async_remote_copy(
                src_ref=source.at[block(index)],
                dst_ref=target.at[block(mine)],
                send_sem=sent,
                recv_sem=got,
                device_id=address(group),
                device_id_type=MESH,
            ).start()

    def send_one(source, target, sent, got, address):
        return pltpu.make_async_remote_copy(
            src_ref=source, dst_ref=target, send_sem=sent, recv_sem=got, device_id=address, device_id_type=MESH
        )

    def to_partner(source, target, sent, got):
        @pl.when(alone)
        def _():
            pltpu.make_async_copy(source, target, got).start()

        @pl.when(jnp.logical_not(alone))
        def _():
            send_one(source, target, sent, got, partner).start()

    def receive(target, got):
        pltpu.make_async_copy(target, target, got).wait()

    def drain(source, sent, count):
        part = source.at[pl.ds(0, count * 8)]
        pltpu.make_async_copy(part, part, sent).wait()

    def drain_other(source, sent):
        @pl.when(alone)
        def _():
            drain(source, sent, GROUP - 1)

        @pl.when(jnp.logical_not(alone))
        def _():
            drain(source, sent, GROUP)

    place_f32, spot_f32 = place.astype(F32), spot.astype(F32)
    row = lax.broadcasted_iota(jnp.int32, (ROWS, LANES), 0)
    lane = lax.broadcasted_iota(jnp.int32, (ROWS, LANES), 1)

    def wave_tables(extent, mode_x, mode_y):
        wave_x, wave_y = UNIT * mode_x, UNIT * mode_y
        wave_sq = wave_x * wave_x + wave_y * wave_y
        anchor = (mode_x == 0) & (mode_y == 0)
        kept = (mode_x <= extent // 3) & (jnp.abs(mode_y) <= extent // 3) & ~anchor
        mask = jnp.where(kept, 1.0, 0.0).astype(F32)
        inverse = mask / jnp.where(anchor, 1.0, wave_sq)
        damp = 1.0 / (1.0 + HALF_STEP * VISCOSITY * wave_sq)
        return wave_x, wave_y, wave_sq, mask, inverse, damp

    def coarse_tables(position, same_ref, cross_ref, damp_ref, stiff_ref=None):
        slot = (lane % 64) // 16
        mode_x = (lane % 8).astype(F32) * GROUP + position
        mode_y = (row - 256 * ((lane % 16) // 8)).astype(F32)
        wave_x, wave_y, wave_sq, mask, inverse, damp = wave_tables(EDGE // 2, mode_x, mode_y)
        same = jnp.where(slot == 2, mask, jnp.where(slot == 1, wave_x * wave_x, wave_y * wave_y) * inverse)
        same_ref[...] = same * (HALF_STEP * damp)
        cross_ref[...] = jnp.where(slot == 2, 0.0, -wave_x * wave_y * inverse) * (HALF_STEP * damp)
        damp_ref[...] = damp
        if stiff_ref is not None:
            stiff_ref[...] = (2.0 * VISCOSITY) * wave_sq * damp

    curl_y[...] = UNIT * (row - 256 * ((lane % 16) // 8)).astype(F32)

    def coarse_tile(ref, base, scale, target):
        for half in range(2):
            pieces = []
            for part in range(2):
                for component in (0, 1, 2, 0):
                    for quarter in (0, 3):
                        start = base + part * 384 + component * 8 + 2 * quarter + half
                        pieces.append(ref[pl.ds(start, 8, stride=24), :])
            target[pl.ds(half * 128, 128), :] = scale * jnp.concatenate(pieces, axis=0).T

    def fine_tile(ref, component, target):
        for half in range(2):
            pieces = []
            for part in range(2):
                for quarter in range(4):
                    start = part * 384 + component * 8 + 2 * quarter + half
                    pieces.append(ref[pl.ds(start, 16, stride=24), :])
            target[pl.ds(half * 128, 128), tile(component)] = jnp.concatenate(pieces, axis=0).T

    def half_products(matrices_two, first, count, target):
        part = pl.ds(first * LANES, count * LANES)
        halves_two = []
        for index, both_parts in enumerate(matrices_two):
            rows = pl.ds(index * ROWS, ROWS)
            if count == 1:
                both = dot(both_parts[...], pair(rhs_high[rows, part], rhs_low[rows, part]))
                halves_two.append(both[:128, :LANES] + both[128:, :LANES] + both[:128, LANES:])
                continue
            both = dot(both_parts[...], rhs_high[rows, part])
            rest = dot(both_parts[pl.ds(0, 128), :], rhs_low[rows, part])
            halves_two.append(both[:128] + both[128:] + rest)
        even, odd = halves_two
        total, difference = even + odd, even - odd
        for step in range(16):
            lines = slice(step * 8, step * 8 + 8)
            target[pl.ds(step * 16, 8), :] = total[lines]
            target[pl.ds(step * 16 + 8, 8), :] = difference[lines]

    def y_back(first, count):
        part = pl.ds(first * LANES, count * LANES)
        high, low = rhs_high[pl.ds(0, ROWS), part], rhs_low[pl.ds(0, ROWS), part]
        grid_buf[:, part] = dot(yt_high[...], high) + dot(yt_high[...], low) + dot(yt_low[...], high)

    def folded(value):
        mirrored = value.reshape(16, 2, 8, LANES)
        first, second = mirrored[:, 0].reshape(128, LANES), mirrored[:, 1].reshape(128, LANES)
        return first + second, first - second

    def stack_back(index, upper, lower):
        for start, value in ((0, upper), (128, lower)):
            high, low = split(value)
            rhs_high[pl.ds(start, 128), tile(index)] = high
            rhs_low[pl.ds(start, 128), tile(index)] = low

    def pair(high, low):
        return jnp.concatenate([high, low], axis=1)

    def twisted(rows, index, value, value_turned, cosine, sine):
        stack(rows, index, value * cosine + value_turned * sine, value_turned * cosine - value * sine)

    def stack(rows, index, first, second):
        high, low = split(first)
        rhs_high[rows, tile(index)] = high
        rhs_low[rows, tile(index)] = low
        high, low = split(second)
        lower = pl.ds(rows.start + ROWS, rows.size)
        rhs_high[lower, tile(index)] = high
        rhs_low[lower, tile(index)] = low

    def spread_coarse(source, target, position):
        lanes = lax.broadcasted_iota(jnp.int32, (1, LANES), 1) % 8
        mode_x = lanes.astype(F32) * GROUP + position
        weight = jnp.where(mode_x == 0, 0.5, 1.0)
        for rows in chunks(128):
            velocity = source[rows, :] * weight
            high_y, low_y = split(velocity * curl_y[rows, :])
            high_x, low_x = split(velocity * (UNIT * mode_x))
            mixed = dot(pair(*split(velocity)), spread_map[...])
            curled = dot(pair(high_y, high_x), curl_map[...]) + dot(pair(low_y, low_x), curl_map[...])
            cosine, sine = turn_yc_c[rows, :], turn_ys_c[rows, :]
            twisted(rows, 0, mixed[:, :LANES], mixed[:, LANES:], cosine, sine)
            twisted(rows, 1, curled[:, LANES:], -curled[:, :LANES], cosine, sine)
        half_products(y_halves, 0, 2, target)

    def to_grid(source, first, fore_high, fore_low, cosine, sine):
        every = pl.ds(0, ROWS)
        for index in range(2):
            high, low = split(source[:, tile(index)])
            inner = dot(pair(high, low), fore_high[...]) + dot(high, fore_low[...])
            real, imag = inner[:, :LANES], inner[:, LANES:]
            stack(every, first + index, real * cosine - imag * sine, real * sine + imag * cosine)
        part = pl.ds(first * LANES, 2 * LANES)
        half_products(x_halves, first, 2, grid_buf.at[:, part])

    def from_grid(value, target, back, cosine, sine):
        high, low = split(value)
        both = dot(xt_high[...], pair(high, low))
        outer = both[:, :LANES] + both[:, LANES:] + dot(xt_low[...], high)
        real, imag = outer[:ROWS], outer[ROWS:]
        high, low = split(pair(real * cosine + imag * sine, imag * cosine - real * sine))
        both = dot(high, back[...])
        target[...] = both[:, :LANES] + both[:, LANES:] + dot(low, back[:, :LANES])

    def grid_coarse(source, target):
        cosine, sine = turn_xc_c[...], turn_xs_c[...]
        to_grid(source, 0, fore_high_c, fore_low_c, cosine, sine)
        speed, spin = grid_buf[:, tile(0)], grid_buf[:, tile(1)]
        crossed = speed * roll(spin, -32) - roll(speed, -32) * spin
        from_grid(crossed, target, back_c, cosine, sine)

    def finish_coarse(source, start_ref, right_ref, target, same_ref, cross_ref, damp_ref):
        even, odd = folded(source[...])
        stack_back(0, even, -turned(odd))
        stack_back(1, turned(even), odd)
        y_back(0, 2)
        for rows in chunks(128):
            value = grid_buf[rows, tile(0)] * turn_yc_c[rows, :] - grid_buf[rows, tile(1)] * turn_ys_c[rows, :]
            modes = dot(pair(*split(value)), finish_map[...])
            term = same_ref[rows, :] * modes[:, :LANES] + cross_ref[rows, :] * modes[:, LANES:]
            target[rows, :] = damp_ref[rows, :] * (start_ref[rows, :] + right_ref[rows, :]) + term

    loads[0].wait()
    coarse_tile(state_ref, 0, 0.5, parcel_send.at[0])
    loads[1].wait()
    loads[2].wait()

    @pl.when(rank == 0)
    def _():
        spread_coarse(parcel_send.at[0], fore_send.at[0], place_f32)

    @pl.when(rank > 0)
    def _():
        pl.semaphore_wait(barrier, 4 * GROUP - 1)

    def greet_last(step, carry):
        signal(ready, (place + step) % GROUP)
        return carry

    @pl.when(jnp.logical_not(near))
    def _():
        lax.fori_loop(0, GROUP, greet_last, 0)

    @pl.when(rank == 0)
    def _():
        pl.semaphore_wait(barrier, 3 * GROUP // 2 - 1)
        post_other(fore_send.at[0], fore_recv.at[0], fore_sent.at[0], fore_got.at[0], DUTY, 0, place)

    def combine(a, carry):
        wave_x = UNIT * (a.astype(F32) * GROUP + place_f32)
        sub = lax.broadcasted_iota(jnp.int32, (8, LANES), 0)
        mode = sub * 128 + lax.broadcasted_iota(jnp.int32, (8, LANES), 1)
        wave_y = UNIT * jnp.where(mode < EDGE // 2, mode, mode - EDGE).astype(F32)
        stiff = VISCOSITY * (wave_x * wave_x + wave_y * wave_y)
        for part in range(2):
            for component in range(3):
                base = pl.multiple_of(a * 24 + (part * 384 + component * 8), 8)
                rows = pl.ds(base, 8)
                states = [state_ref[pl.ds(base + node * 768, 8), :] for node in range(3)]
                terms = [terms_ref[pl.ds(base + node * 768, 8), :] for node in range(3)]
                one = sum(w * s for w, s in zip(STATE_ONE, states))
                two = sum(w * s for w, s in zip(STATE_TWO, states))
                mix_one[rows, :] = one
                mix_two[rows, :] = two
                right_one[rows, :] = sum(w * t for w, t in zip(TERM_ONE, terms)) + stiff * one
                right_two[rows, :] = sum(w * t for w, t in zip(TERM_TWO, terms)) + stiff * two
                start_send[rows, :] = states[2] + HALF_STEP * terms[2]
        return carry

    for index in (3, 4, 5, 6):
        loads[index].wait()
    lax.fori_loop(0, 16, combine, 0, unroll=2)

    following = (rank + 1, at_y, at_pz)

    @pl.when(rank == 0)
    def _():
        pl.semaphore_wait(ready, 5 * GROUP // 2)

    @pl.when(rank < 3)
    def _():
        send_one(start_send, start_recv, start_sems.at[0], start_sems.at[1], following).start()

    coarse_tile(right_one, 0, 0.5, parcel_send.at[1])
    coarse_tile(right_two, 0, 0.5, parcel_send.at[2])
    to_partner(parcel_send, parcel_recv, parcel_sems.at[0], parcel_sems.at[1])
    coarse_tables(spot_f32, keep_same, keep_cross, damp_c)

    def coarse_sweep():
        receive(fore_recv.at[0], fore_got.at[0])
        grid_coarse(fore_recv.at[0], back_send.at[0])
        post_own(back_send.at[0], back_recv.at[0], back_sent.at[0], back_got.at[0], DUTY, duty, spot)
        receive(parcel_recv, parcel_sems.at[1])

        @pl.when(duty == 0)
        def _():
            sweep[0] = parcel_recv[0]

        @pl.when(duty > 0)
        def _():
            receive(hand_recv, hand_sems.at[1])
            sweep[0] = hand_recv[...]

        receive(back_recv.at[0], back_got.at[0])
        tables = (keep_same, keep_cross, damp_c)
        finish_coarse(back_recv.at[0], sweep.at[0], parcel_recv.at[1], sweep.at[1], *tables)
        spread_coarse(sweep.at[1], fore_send.at[1], spot_f32)
        post_own(fore_send.at[1], fore_recv.at[1], fore_sent.at[1], fore_got.at[1], DUTY, duty, spot)
        to_partner(sweep.at[pl.ds(0, 2)], news.at[pl.ds(0, 2)], news_sent.at[0], news_got.at[0])
        receive(fore_recv.at[1], fore_got.at[1])
        grid_coarse(fore_recv.at[1], back_send.at[1])

        @pl.when(duty == 3)
        def _():
            post_other(back_send.at[1], last_recv, back_sent.at[1], back_got.at[2], RANK, 3, spot)

        @pl.when(duty < 3)
        def _():
            post_own(back_send.at[1], back_recv.at[1], back_sent.at[1], back_got.at[1], DUTY, duty, spot)
            receive(back_recv.at[1], back_got.at[1])
            finish_coarse(back_recv.at[1], sweep.at[1], parcel_recv.at[2], sweep.at[2], *tables)
            spread_coarse(sweep.at[2], fore_send.at[2], spot_f32)
            after = duty + 1
            post(fore_send.at[2], fore_recv.at[0], fore_sent.at[2], fore_got.at[0], DUTY, after, spot, GROUP)
            address = (low_z * 2 + after % 2, at_y, (after // 2) * 4 + at_x)
            send_one(sweep.at[2], hand_recv, hand_sems.at[0], hand_sems.at[1], address).start()
            to_partner(sweep.at[2], news.at[2], news_sent.at[1], news_got.at[1])

    coarse_tile(mix_one, 0, 0.5, old_one)
    coarse_tile(mix_two, 0, 0.5, old_two)
    quarter = (lane % 64) // 16
    mode_x = (lane % 16).astype(F32) * GROUP + place_f32
    mode_y = (row + 256 * quarter - jnp.where(quarter >= 2, EDGE, 0)).astype(F32)
    wave_x, wave_y, wave_sq, mask, inverse, damp = wave_tables(EDGE, mode_x, mode_y)
    ky_f[...] = wave_y
    damp_f[...] = damp
    stiff_f[...] = (2.0 * VISCOSITY) * wave_sq
    same_x[...] = wave_y * wave_y * inverse
    same_y[...] = wave_x * wave_x * inverse
    cross_f[...] = -wave_x * wave_y * inverse
    mask_f[...] = mask
    weight = jnp.where(mode_x == 0, 0.5, 1.0)
    cos_f[...] = turn_yc_f[...] * weight
    sin_f[...] = turn_ys_f[...] * weight

    @pl.when(rank == 3)
    def _():
        coarse_tables(place_f32, keep_same_r, keep_cross_r, damp_r, stiff_r)

    def correct_fine(weights, old_ref, target):
        for rows in chunks(128):
            nodes = [news[node, rows, :] for node in range(3)]
            change = sum(w * n for w, n in zip(weights, nodes)) - old_ref[rows, :]
            placed = dot(pair(*split(change)), place_map[...])
            stiff = stiff_f[rows, :]
            for component in range(3):
                part = tile(component)
                lanes = slice(component * LANES, (component + 1) * LANES)
                target[rows, part] = target[rows, part] + stiff * placed[:, lanes]

    def spread_change(index):
        mode_x = (lax.broadcasted_iota(jnp.int32, (1, LANES), 1) % 8).astype(F32) * GROUP + place_f32
        weight = jnp.where(mode_x == 0, 0.5, 1.0)
        for rows in chunks(128):
            nodes = [news[node, rows, :] for node in range(3)]
            value = sum(w * n for w, n in zip(STATE_ONE, nodes)) - old_one[rows, :]
            value = value * stiff_r[rows, :] * weight
            if index == 0:
                mixed = dot(pair(*split(value)), change_maps[0][...])
            else:
                first, second = value, value * curl_y[rows, :]
                if index == 2:
                    first, second = second, value * (UNIT * mode_x)
                first_high, first_low = split(first)
                second_high, second_low = split(second)
                mixed = dot(pair(first_high, second_high), change_maps[index][...])
                mixed = mixed + dot(pair(first_low, second_low), change_maps[index][...])
            twisted(rows, index, mixed[:, :LANES], mixed[:, LANES:], turn_c[rows, :], turn_s[rows, :])
        half_products(y_halves, index, 1, change_send.at[index])

    def change_to_grid(index, cosine, sine):
        every = pl.ds(0, ROWS)
        high, low = split(change_recv[index])
        inner = dot(pair(high, low), change_fore_high[...]) + dot(high, change_fore_low[...])
        for field in range(2):
            real = inner[:, 2 * field * LANES : (2 * field + 1) * LANES]
            imag = inner[:, (2 * field + 1) * LANES : (2 * field + 2) * LANES]
            stack(every, 2 * index + field, real * cosine - imag * sine, real * sine + imag * cosine)
        half_products(x_halves, 2 * index, 2, grid_buf.at[:, pl.ds(2 * index * LANES, 2 * LANES)])

    def start_fine():
        correct_fine(STATE_ONE, old_one, right_one_f)
        set_node()

    def set_node():
        for component in range(3):
            node_f[:, tile(component)] = right_one_f[:, tile(component)] * damp_f[...]

    def fine_field(index, rows):
        x, y, z = (node_f.at[rows, tile(component)] for component in range(3))
        if index < 3:
            return (x, y, z)[index][...]
        ky = ky_f[rows, :]
        kx = UNIT * ((lanes_like(ky) % 16).astype(F32) * GROUP + place_f32)
        if index == 3:
            return ky * z[...]
        if index == 4:
            return -kx * z[...]
        return kx * y[...] - ky * x[...]

    def spread_fine(first):
        for rows in chunks(128):
            cosine, sine = cos_f[rows, :], sin_f[rows, :]
            for index in (first, first + 1):
                mixed = dot(pair(*split(fine_field(index, rows))), spread_map_f[...])
                if index < 3:
                    twisted(rows, index, mixed[:, :LANES], mixed[:, LANES:], cosine, sine)
                else:
                    twisted(rows, index, mixed[:, LANES:], -mixed[:, :LANES], cosine, sine)
        half_products(y_halves, first, 2, fine_send.at[first // 2])

    def give_back(source, component, target, base):
        for half in range(2):
            block_t = source[pl.ds(half * 128, 128), tile(component)].T
            for part in range(2):
                for quarter in range(4):
                    start = base + part * 384 + component * 8 + 2 * quarter + half
                    first = (part * 4 + quarter) * 16
                    target[pl.ds(start, 16, stride=24), :] = block_t[first : first + 16]

    def give_back_coarse(source, base):
        for half in range(2):
            block_t = source[pl.ds(half * 128, 128), :].T
            for part in range(2):
                for component in range(3):
                    for quarter in range(2):
                        start = base + part * 96 + component * 4 + 2 * quarter + half
                        first = part * 64 + component * 16 + quarter * 8
                        coarse_out[pl.ds(start, 8, stride=12), :] = block_t[first : first + 8]

    def cross_fine(component):
        second, third = (component + 1) % 3, (component + 2) % 3
        fields = [grid_buf[:, tile(index)] for index in (second, third, second + 3, third + 3)]
        return fields[0] * fields[3] - fields[1] * fields[2]

    def gather_fine(component):
        even, odd = folded(fine_back_recv[component])
        stack_back(component, even, -turned(odd))
        y_back(component, 1)
        for rows in chunks(128):
            value = grid_buf[rows, tile(component)]
            value = value * turn_yc_f[rows, :] - turned(value) * turn_ys_f[rows, :]
            right_one_f[rows, tile(component)] = dot(pair(*split(value)), finish_map_f[...])

    def finish_fine():
        for rows in chunks(64):
            modes = [right_one_f[rows, tile(component)] for component in range(3)]
            cross = cross_f[rows, :]
            results = [
                same_x[rows, :] * modes[0] + cross * modes[1],
                same_y[rows, :] * modes[1] + cross * modes[0],
                mask_f[rows, :] * modes[2],
            ]
            for component, value in enumerate(results):
                part = tile(component)
                right_one_f[rows, part] = value
                total = node_f[rows, part] + HALF_STEP * value + right_two_f[rows, part]
                node_f[rows, part] = total * damp_f[rows, :]

    def prepare_fine():
        @pl.when(rank == 0)
        def _():
            first = pl.ds(0, 768)
            right_one[...] = right_one[...] + state_ref[first, :] + HALF_STEP * terms_ref[first, :]

        @pl.when(rank > 0)
        def _():
            receive(start_recv, start_sems.at[1])
            right_one[...] = right_one[...] + start_recv[...]

        for component in range(3):
            fine_tile(right_one, component, right_one_f)
            fine_tile(right_two, component, right_two_f)

    def send_fine():
        for part in range(3):
            spread_fine(2 * part)
            pairs = (fine_send.at[part], fine_recv.at[part], fine_sent.at[part], fine_got.at[part])
            post_own(*pairs, RANK, rank, place)

    def take_fine():
        for part in range(3):
            receive(fine_recv.at[part], fine_got.at[part])
            to_grid(fine_recv.at[part], 2 * part, fore_high_f, fore_low_f, turn_xc_f[...], turn_xs_f[...])

    def fine_sweep():
        @pl.when(rank < 3)
        def _():
            prepare_fine()
            receive(news.at[pl.ds(0, 2)], news_got.at[0])
            receive(news.at[2], news_got.at[1])
            start_fine()
            send_fine()

        @pl.when(rank == 3)
        def _():
            take_fine()
            base_grid[...] = grid_buf[...]
            receive(news.at[pl.ds(0, 2)], news_got.at[0])
            receive(last_recv, back_got.at[2])
            tables = (keep_same_r, keep_cross_r, damp_r)
            finish_coarse(last_recv, news.at[1], parcel_send.at[2], news.at[2], *tables)
            for part in range(3):
                spread_change(part)
                pairs = (change_send.at[part], change_recv.at[part], change_sent.at[part], change_got.at[part])
                post_own(*pairs, RANK, rank, place)
            start_fine()

        correct_fine(STATE_TWO, old_two, right_two_f)
        give_back_coarse(news.at[1], 0)
        give_back_coarse(news.at[2], 192)
        @pl.when(rank < 3)
        def _():
            take_fine()

        @pl.when(rank == 3)
        def _():
            for part in range(3):
                receive(change_recv.at[part], change_got.at[part])
                change_to_grid(part, turn_xc_f[...], turn_xs_f[...])
            grid_buf[...] = grid_buf[...] + base_grid[...]

        for part in range(3):
            from_grid(cross_fine(part), fine_back_send.at[part], back_f, turn_xc_f[...], turn_xs_f[...])
            pairs = (fine_back_send.at[part], fine_back_recv.at[part])
            post_own(*pairs, fine_back_sent.at[part], fine_back_got.at[part], RANK, rank, place)
        for component in range(3):
            give_back(node_f, component, nodes_out, 0)
        for part in range(3):
            receive(fine_back_recv.at[part], fine_back_got.at[part])
            gather_fine(part)
        finish_fine()
        for component in range(3):
            give_back(right_one_f, component, term_out, 0)
            give_back(node_f, component, nodes_out, 768)

    @pl.when(rank == 3)
    def _():
        prepare_fine()
        set_node()
        send_fine()

    early = high_z * (1 - low_z)

    def phase(step, carry):
        fine_now = (step + early) % 2

        @pl.when(fine_now == 0)
        def _():
            coarse_sweep()

        @pl.when(fine_now == 1)
        def _():
            fine_sweep()

        return carry

    lax.fori_loop(0, 2, phase, 0)

    @pl.when(rank == 0)
    def _():
        drain_other(fore_send.at[0], fore_sent.at[0])

    drain(fore_send.at[1], fore_sent.at[1], GROUP - 1)
    drain(back_send.at[0], back_sent.at[0], GROUP - 1)
    for part in range(3):
        drain(fine_send.at[part], fine_sent.at[part], GROUP - 1)
        drain(fine_back_send.at[part], fine_back_sent.at[part], GROUP - 1)

    @pl.when(duty == 3)
    def _():
        drain_other(back_send.at[1], back_sent.at[1])

    @pl.when(duty < 3)
    def _():
        drain(back_send.at[1], back_sent.at[1], GROUP - 1)
        drain(fore_send.at[2], fore_sent.at[2], GROUP)
        receive(sweep.at[2], hand_sems.at[0])

    @pl.when(jnp.logical_not(alone))
    def _():
        receive(parcel_send, parcel_sems.at[0])
        receive(sweep.at[pl.ds(0, 2)], news_sent.at[0])

        @pl.when(duty < 3)
        def _():
            receive(sweep.at[2], news_sent.at[1])

    @pl.when(rank == 3)
    def _():
        for part in range(3):
            drain(change_send.at[part], change_sent.at[part], GROUP - 1)

    @pl.when(rank < 3)
    def _():
        receive(start_send, start_sems.at[0])


def shards(fine_state, fine_terms):
    matrices, turns = constant_tables()
    full, natural, wide = (ROWS, LANES), (768, LANES), (ROWS, 3 * LANES)
    dma = pltpu.SemaphoreType.DMA
    tiles = (3, ROWS, LANES)
    shapes = [(ROWS, 6 * LANES)]
    shapes += [(3, ROWS, 2 * LANES), (2, ROWS, 2 * LANES), (2, ROWS, LANES), (2, ROWS, LANES), full, full]
    shapes += [tiles] * 4 + [(3, ROWS, 2 * LANES)] * 2 + [tiles] * 2
    shapes += [natural] * 6 + [full] * (9 + 9) + [wide] * 3
    shapes += [(ROWS, 6 * LANES), tiles, tiles, full, (2304, LANES), (2304, LANES)]
    scratch = [pltpu.VMEM((2 * ROWS, 6 * LANES), BF16)] * 2 + [pltpu.VMEM(shape, F32) for shape in shapes]
    scratch += [pltpu.VMEM(matrices.shape, BF16), pltpu.VMEM(turns.shape, F32)]
    scratch += [dma((count,)) for count in (3, 2, 2, 3, 2, 2, 2, 2, 3, 3, 3, 3, 2, 7, 3, 3)]
    scratch += [pltpu.SemaphoreType.REGULAR]
    outs = pl.pallas_call(
        iterate,
        out_shape=(
            jax.ShapeDtypeStruct((1536, LANES), F32),
            jax.ShapeDtypeStruct((768, LANES), F32),
            jax.ShapeDtypeStruct((384, LANES), F32),
        ),
        in_specs=[pl.BlockSpec(memory_space=pltpu.HBM)] * 4,
        out_specs=[pl.BlockSpec(memory_space=pltpu.VMEM)] * 3,
        scratch_shapes=scratch,
        compiler_params=pltpu.CompilerParams(
            collective_id=0, has_side_effects=True, vmem_limit_bytes=52 * 1024 * 1024
        ),
        name="iterate",
    )(fine_state.reshape(2304, LANES), fine_terms.reshape(2304, LANES), jnp.asarray(matrices), jnp.asarray(turns))
    return (
        outs[0].reshape(1, 2, 2, 16, 1, 3, 1, 1024),
        outs[1].reshape(1, 2, 16, 1, 3, 1, 1024),
        outs[2].reshape(1, 2, 2, 8, 1, 3, 1, 512),
    )


def solution(mesh):
    split_over = P("tm", None, None, None, ("py", "pz"), None, None, None)
    return jax.shard_map(
        shards,
        mesh=mesh,
        in_specs=(split_over, split_over),
        out_specs=(
            split_over,
            P("tm", None, None, ("py", "pz"), None, None, None),
            split_over,
        ),
        check_vma=False,
    )
```

```python
import math

import jax
import jax.numpy as jnp
import ml_dtypes
import numpy as np
from jax import lax
from jax.experimental import pallas as pl
from jax.experimental.pallas import tpu as pltpu
from jax.sharding import PartitionSpec as P

EDGE = 1024
VISCOSITY = 0.5
TIME_STEP = 0.2
HALF_STEP = 0.5 * TIME_STEP
WEIGHTS = ((5.0 / 24.0, 1.0 / 3.0, -1.0 / 24.0), (-1.0 / 24.0, 1.0 / 3.0, 5.0 / 24.0))
UNIT = 2.0 * math.pi / EDGE
GROUP = 32
ROWS = 256
LANES = 128
F32 = jnp.float32
BF16 = jnp.bfloat16
MESH = pl.DeviceIdType.MESH
TERM_ONE = [TIME_STEP * w for w in WEIGHTS[0]]
TERM_ONE[0] -= HALF_STEP
TERM_TWO = [TIME_STEP * w for w in WEIGHTS[1]]
TERM_TWO[1] -= HALF_STEP
STATE_ONE = [-TIME_STEP * w for w in WEIGHTS[0]]
STATE_ONE[1] += HALF_STEP
STATE_TWO = [-TIME_STEP * w for w in WEIGHTS[1]]
STATE_TWO[2] += HALF_STEP


HOPS = (0, 1, 2, 1)
DUTY, RANK = (
    sorted(
        ((y, z, x) for y in range(4) for z in range(2) for x in range(4)),
        key=lambda step: -(HOPS[step[0]] + apart * step[1] + HOPS[step[2]]),
    )
    for apart in (1, 2)
)


def halves(table):
    high = table.astype(ml_dtypes.bfloat16)
    low = (table - high.astype(np.float64)).astype(ml_dtypes.bfloat16)
    return high, low


def lane_circle(extent):
    inner = extent // GROUP
    modes = inner // 2
    pairs = 64 // modes
    fore = np.zeros((2, pairs, modes, 2, pairs, inner))
    back = np.zeros((2, pairs, inner, 2, pairs, modes))
    phase = 2.0 * math.pi * np.outer(np.arange(modes), np.arange(inner)) / inner
    kept = (np.arange(modes) * GROUP <= extent // 3)[None, :]
    for pair in range(pairs):
        cosine, sine = 2.0 / extent * np.cos(phase), 2.0 / extent * np.sin(phase)
        fore[0, pair, :, 0, pair] = cosine
        fore[1, pair, :, 0, pair] = -sine
        fore[0, pair, :, 1, pair] = sine
        fore[1, pair, :, 1, pair] = cosine
        target = pair
        sources = [(pair, pair)]
        if extent < EDGE:
            slot, rest = divmod(pair, 2)
            sources = [(((1, 2, 0, 1)[slot]) * 2 + rest, pair)]
        for source, target in sources:
            cosine = 1.0 / extent * np.cos(phase).T * kept
            sine = 1.0 / extent * np.sin(phase).T * kept
            back[0, source, :, 0, target] = cosine
            back[1, source, :, 0, target] = sine
            back[0, source, :, 1, target] = -sine
            back[1, source, :, 1, target] = cosine
    fore = fore.reshape(128, 256)
    back = back.reshape(256, 128)
    return fore, back


def real_form(table):
    return np.block([[table.real, table.imag], [-table.imag, table.real]])


def doubled(table):
    return np.concatenate([table, table], axis=0)


def lane_maps():
    sign = np.array([[1.0, 1.0], [1.0, -1.0]])
    curl_y, curl_x, partner = np.zeros((4, 4)), np.zeros((4, 4)), np.zeros((4, 4))
    curl_y[2, 0] = curl_y[2, 3] = 1.0
    curl_y[0, 2] = -1.0
    curl_x[2, 1] = -1.0
    curl_x[1, 2] = 1.0
    partner[1, 0] = partner[1, 3] = partner[0, 1] = 1.0

    def coarse(slots):
        table = np.kron(np.kron(slots, sign), np.eye(8)).astype(complex)
        return real_form(table), real_form(1j * table)

    same = coarse(np.eye(4))
    spread_c = doubled(np.concatenate(same, axis=1))
    curl_c = np.concatenate([np.concatenate(coarse(slots), axis=1) for slots in (curl_y, curl_x)], axis=0)
    finish_c = doubled(np.concatenate([same[0], coarse(partner)[0]], axis=1))
    quarters, powers = np.arange(4), np.array([0, 2, 1, 3])
    table = np.kron(1j ** (np.outer(quarters, powers) % 4), np.eye(16))
    spread_f = doubled(np.concatenate([real_form(table), real_form(1j * table)], axis=1))
    finish_f = doubled(real_form(np.conj(table).T))
    place = np.zeros((3, 4, 2, 8, 4, 16))
    for component in range(3):
        for a in range(8):
            place[component, component, 0, a, 0, a] = 1.0
            place[component, component, 1, a, 3, a] = 1.0
    place_f = doubled(np.concatenate([real_form(table.reshape(64, 64).astype(complex)) for table in place], axis=1))
    return [
        np.concatenate(pair, axis=1).astype(ml_dtypes.bfloat16)
        for pair in ((spread_c, curl_c), (finish_c, spread_f), (place_f, finish_f))
    ]


def constant_tables():
    index = np.arange(ROWS)
    phase = 2.0 * math.pi * np.outer(np.arange(ROWS // 2) + 0.5, index) / ROWS
    along_y = np.concatenate([np.cos(phase), np.sin(phase)], axis=1)
    back_y = np.concatenate([np.cos(phase).T, np.sin(phase).T], axis=1)
    small = 2.0 * math.pi * np.outer(np.arange(GROUP) + 0.5, np.arange(GROUP)) / GROUP
    along_x = np.concatenate([np.cos(small), -np.sin(small)], axis=1).reshape(GROUP, 2, GROUP)
    half = GROUP // 2
    order = np.stack([np.arange(half), GROUP - 1 - np.arange(half)], axis=1).reshape(-1)
    back_x = np.kron(along_x[order].transpose(1, 2, 0).reshape(2 * GROUP, GROUP), np.eye(8))
    along_x = np.kron(along_x[:half].reshape(half, 2 * GROUP), np.eye(8))
    maps = lane_maps()
    matrices = list(halves(along_y)) + [np.concatenate(halves(back_y), axis=1), maps[0]]
    matrices += list(halves(along_x)) + [np.concatenate(halves(back_x), axis=1)]
    lane = np.arange(LANES)
    turns, inner_parts = [], []
    for extent in (EDGE // 2, EDGE):
        fore, back = lane_circle(extent)
        fore_high, fore_low = halves(fore)
        back_high, back_low = halves(back)
        inner_parts.append(
            np.concatenate([fore_high, fore_high, fore_low, np.concatenate([back_high, back_low], axis=1)], axis=0)
        )
        inner = extent // GROUP
        turn = 2.0 * math.pi * np.outer(index // 8, lane % inner / extent - 0.5 / GROUP)
        turns += [np.cos(turn), np.sin(turn)]
        if extent < EDGE:
            offset = (lane % 16) // 8
        else:
            offset = np.array([0, 2, 1, 3])[(lane % 64) // 16]
        turn = 2.0 * math.pi * np.outer(index, offset / extent - 0.5 / ROWS)
        turns += [np.cos(turn), np.sin(turn)]
    matrices.append(np.concatenate(inner_parts, axis=1))
    matrices += maps[1:]
    return np.concatenate(matrices, axis=0), np.concatenate(turns, axis=0).astype(np.float32)


def split(value):
    high = value.astype(BF16)
    return high, (value - high.astype(F32)).astype(BF16)


def dot(left, right):
    return jnp.dot(left, right, preferred_element_type=F32)


def roll(value, shift):
    return pltpu.roll(value, shift % LANES, axis=1)


def lanes_like(value):
    return lax.broadcasted_iota(jnp.int32, value.shape, 1)


def turned(value):
    other = roll(value, 64)
    return jnp.where(lanes_like(value) < 64, -other, other)


def tile(index):
    return pl.ds(index * LANES, LANES)


def chunks(size):
    return [pl.ds(start, size) for start in range(0, ROWS, size)]


def iterate(
    state_hbm, terms_hbm, matrices_hbm, turns_hbm,
    nodes_out, term_out, coarse_out,
    rhs_high, rhs_low, grid_buf,
    fore_send, fore_recv, back_send, back_recv, last_recv, hand_recv,
    parcel_send, parcel_recv, sweep, news,
    fine_send, fine_recv, fine_back_send, fine_back_recv, start_send, start_recv,
    right_one, right_two, mix_one, mix_two,
    curl_y, keep_same, keep_cross, damp_c, keep_same_r, keep_cross_r, damp_r, old_one, old_two,
    ky_f, damp_f, stiff_f, cos_f, sin_f, same_x, same_y, cross_f, mask_f,
    right_one_f, right_two_f, node_f,
    state_ref, terms_ref, matrices, turns,
    fore_sent, fore_got, back_sent, back_got, hand_sems, parcel_sems, news_sent, news_got,
    fine_sent, fine_got, fine_back_sent, fine_back_got, start_sems, load_sems,
    ready,
):
    loads = []
    for source, target, start, size in (
        (state_hbm, state_ref, 0, 768),
        (matrices_hbm, matrices, 0, 768),
        (turns_hbm, turns, 0, 1024),
        (state_hbm, state_ref, 768, 1536),
        (terms_hbm, terms_ref, 0, 2304),
        (matrices_hbm, matrices, 768, 1920),
        (turns_hbm, turns, 1024, 1024),
    ):
        rows = pl.ds(start, size)
        loads.append(pltpu.make_async_copy(source.at[rows], target.at[rows], load_sems.at[len(loads)]))
    for load in loads[:3]:
        load.start()

    def matrix(start, size, first=0, width=512):
        return matrices.at[pl.ds(start, size), pl.ds(first, width)]

    y_halves = (matrix(0, 256, 0, 256), matrix(0, 256, 256, 256))
    yt_high, yt_low = matrix(256, 256, 0, 256), matrix(256, 256, 256, 256)
    spread_map, curl_map = matrix(512, 256, 0, 256), matrix(512, 256, 256, 256)
    x_halves = (matrix(768, 256, 0, 256), matrix(768, 256, 256, 256))
    xt_high, xt_low = matrix(1024, 512, 0, 256), matrix(1024, 512, 256, 256)
    fore_high_c, fore_low_c, back_c = (matrix(*rows, 0, 256) for rows in ((1536, 256), (1792, 128), (1920, 256)))
    fore_high_f, fore_low_f, back_f = (matrix(*rows, 256, 256) for rows in ((1536, 256), (1792, 128), (1920, 256)))
    finish_map, spread_map_f = matrix(2176, 256, 0, 256), matrix(2176, 256, 256, 256)
    place_map, finish_map_f = matrix(2432, 256, 0, 384), matrix(2432, 256, 384, 128)
    turn_xc_c, turn_xs_c, turn_yc_c, turn_ys_c, turn_xc_f, turn_xs_f, turn_yc_f, turn_ys_f = (
        turns.at[pl.ds(start, ROWS), :] for start in range(0, 8 * ROWS, ROWS)
    )
    rank = lax.axis_index("tm")
    at_y, at_pz = lax.axis_index("py"), lax.axis_index("pz")
    low_z, core, high_z, at_x = rank // 2, rank % 2, at_pz // 4, at_pz % 4
    place = at_y * 8 + at_pz
    duty = high_z * 2 + core
    spot = at_y * 8 + low_z * 4 + at_x
    alone = high_z == low_z
    partner = (duty, at_y, low_z * 4 + at_x)

    barrier = pltpu.get_barrier_semaphore()
    number = rank * GROUP + place
    near = (core == 0) & (high_z + low_z < 2)

    def signal(semaphore, other):
        target = (other // GROUP, (other // 8) % 4, other % 8)
        pl.semaphore_signal(semaphore, inc=1, device_id=target, device_id_type=MESH)

    def greet_first(step, carry):
        signal(barrier, (place + step) % GROUP)
        return carry

    @pl.when(near)
    def _():
        @pl.when(rank > 0)
        def _():
            signal(barrier, place)

        lax.fori_loop(1, GROUP, greet_first, 0)

    def greet(step, carry):
        signal(barrier, GROUP + (number + 2 * GROUP + step) % (3 * GROUP))
        return carry

    @pl.when(rank == 0)
    def _():
        greet(0, 0)

    lax.fori_loop(1, 3 * GROUP, greet, 0)

    def block(position):
        return pl.ds(pl.multiple_of(position * 8, 8), 8)

    spots_y = [(at_y + step) % 4 for step in range(4)]
    spots_x = [(at_x + step) % 4 for step in range(4)]
    duty_z = [(low_z + step) % 2 for step in range(2)]
    rank_z = [(high_z + step) % 2 for step in range(2)]

    def spot_of(steps, step):
        spot_y, spot_x = spots_y[step[0]], spots_x[step[2]]
        if steps is DUTY:
            spot_z = duty_z[step[1]]
            address = lambda group: (spot_z * 2 + group % 2, spot_y, (group // 2) * 4 + spot_x)
        else:
            spot_z = rank_z[step[1]]
            address = lambda group: (group, spot_y, spot_z * 4 + spot_x)
        return spot_y * 8 + spot_z * 4 + spot_x, address

    def post(source, target, sent, got, steps, group, mine, count):
        for step in steps[:count]:
            index, address = spot_of(steps, step)
            pltpu.make_async_remote_copy(
                src_ref=source.at[block(index)],
                dst_ref=target.at[block(mine)],
                send_sem=sent,
                recv_sem=got,
                device_id=address(group),
                device_id_type=MESH,
            ).start()

    def post_own(source, target, sent, got, steps, group, mine):
        post(source, target, sent, got, steps, group, mine, GROUP - 1)
        pltpu.make_async_copy(source.at[block(mine)], target.at[block(mine)], got).start()

    def post_other(source, target, sent, got, steps, group, mine):
        post(source, target, sent, got, steps, group, mine, GROUP - 1)
        index, address = spot_of(steps, steps[-1])

        @pl.when(alone)
        def _():
            pltpu.make_async_copy(source.at[block(index)], target.at[block(mine)], got).start()

        @pl.when(jnp.logical_not(alone))
        def _():
            pltpu.make_async_remote_copy(
                src_ref=source.at[block(index)],
                dst_ref=target.at[block(mine)],
                send_sem=sent,
                recv_sem=got,
                device_id=address(group),
                device_id_type=MESH,
            ).start()

    def send_one(source, target, sent, got, address):
        return pltpu.make_async_remote_copy(
            src_ref=source, dst_ref=target, send_sem=sent, recv_sem=got, device_id=address, device_id_type=MESH
        )

    def to_partner(source, target, sent, got):
        @pl.when(alone)
        def _():
            pltpu.make_async_copy(source, target, got).start()

        @pl.when(jnp.logical_not(alone))
        def _():
            send_one(source, target, sent, got, partner).start()

    def receive(target, got):
        pltpu.make_async_copy(target, target, got).wait()

    def drain(source, sent, count):
        part = source.at[pl.ds(0, count * 8)]
        pltpu.make_async_copy(part, part, sent).wait()

    def drain_other(source, sent):
        @pl.when(alone)
        def _():
            drain(source, sent, GROUP - 1)

        @pl.when(jnp.logical_not(alone))
        def _():
            drain(source, sent, GROUP)

    place_f32, spot_f32 = place.astype(F32), spot.astype(F32)
    row = lax.broadcasted_iota(jnp.int32, (ROWS, LANES), 0)
    lane = lax.broadcasted_iota(jnp.int32, (ROWS, LANES), 1)

    def wave_tables(extent, mode_x, mode_y):
        wave_x, wave_y = UNIT * mode_x, UNIT * mode_y
        wave_sq = wave_x * wave_x + wave_y * wave_y
        anchor = (mode_x == 0) & (mode_y == 0)
        kept = (mode_x <= extent // 3) & (jnp.abs(mode_y) <= extent // 3) & ~anchor
        mask = jnp.where(kept, 1.0, 0.0).astype(F32)
        inverse = mask / jnp.where(anchor, 1.0, wave_sq)
        damp = 1.0 / (1.0 + HALF_STEP * VISCOSITY * wave_sq)
        return wave_x, wave_y, wave_sq, mask, inverse, damp

    def coarse_tables(position, same_ref, cross_ref, damp_ref):
        slot = (lane % 64) // 16
        mode_x = (lane % 8).astype(F32) * GROUP + position
        mode_y = (row - 256 * ((lane % 16) // 8)).astype(F32)
        wave_x, wave_y, wave_sq, mask, inverse, damp = wave_tables(EDGE // 2, mode_x, mode_y)
        same = jnp.where(slot == 2, mask, jnp.where(slot == 1, wave_x * wave_x, wave_y * wave_y) * inverse)
        same_ref[...] = same * (HALF_STEP * damp)
        cross_ref[...] = jnp.where(slot == 2, 0.0, -wave_x * wave_y * inverse) * (HALF_STEP * damp)
        damp_ref[...] = damp

    curl_y[...] = UNIT * (row - 256 * ((lane % 16) // 8)).astype(F32)

    def coarse_tile(ref, base, scale, target):
        for half in range(2):
            pieces = []
            for part in range(2):
                for component in (0, 1, 2, 0):
                    for quarter in (0, 3):
                        start = base + part * 384 + component * 8 + 2 * quarter + half
                        pieces.append(ref[pl.ds(start, 8, stride=24), :])
            target[pl.ds(half * 128, 128), :] = scale * jnp.concatenate(pieces, axis=0).T

    def fine_tile(ref, component, target):
        for half in range(2):
            pieces = []
            for part in range(2):
                for quarter in range(4):
                    start = part * 384 + component * 8 + 2 * quarter + half
                    pieces.append(ref[pl.ds(start, 16, stride=24), :])
            target[pl.ds(half * 128, 128), tile(component)] = jnp.concatenate(pieces, axis=0).T

    def half_products(matrices_two, first, count, target):
        part = pl.ds(first * LANES, count * LANES)
        halves_two = []
        for index, both_parts in enumerate(matrices_two):
            rows = pl.ds(index * ROWS, ROWS)
            both = dot(both_parts[...], rhs_high[rows, part])
            rest = dot(both_parts[pl.ds(0, 128), :], rhs_low[rows, part])
            halves_two.append(both[:128] + both[128:] + rest)
        even, odd = halves_two
        total, difference = even + odd, even - odd
        for step in range(16):
            lines = slice(step * 8, step * 8 + 8)
            target[pl.ds(step * 16, 8), :] = total[lines]
            target[pl.ds(step * 16 + 8, 8), :] = difference[lines]

    def y_back(first, count):
        part = pl.ds(first * LANES, count * LANES)
        high, low = rhs_high[pl.ds(0, ROWS), part], rhs_low[pl.ds(0, ROWS), part]
        grid_buf[:, part] = dot(yt_high[...], high) + dot(yt_high[...], low) + dot(yt_low[...], high)

    def folded(value):
        mirrored = value.reshape(16, 2, 8, LANES)
        first, second = mirrored[:, 0].reshape(128, LANES), mirrored[:, 1].reshape(128, LANES)
        return first + second, first - second

    def stack_back(index, upper, lower):
        for start, value in ((0, upper), (128, lower)):
            high, low = split(value)
            rhs_high[pl.ds(start, 128), tile(index)] = high
            rhs_low[pl.ds(start, 128), tile(index)] = low

    def pair(high, low):
        return jnp.concatenate([high, low], axis=1)

    def twisted(rows, index, value, value_turned, cosine, sine):
        stack(rows, index, value * cosine + value_turned * sine, value_turned * cosine - value * sine)

    def stack(rows, index, first, second):
        high, low = split(first)
        rhs_high[rows, tile(index)] = high
        rhs_low[rows, tile(index)] = low
        high, low = split(second)
        lower = pl.ds(rows.start + ROWS, rows.size)
        rhs_high[lower, tile(index)] = high
        rhs_low[lower, tile(index)] = low

    def spread_coarse(source, target, position):
        lanes = lax.broadcasted_iota(jnp.int32, (1, LANES), 1) % 8
        mode_x = lanes.astype(F32) * GROUP + position
        weight = jnp.where(mode_x == 0, 0.5, 1.0)
        for rows in chunks(128):
            velocity = source[rows, :] * weight
            high_y, low_y = split(velocity * curl_y[rows, :])
            high_x, low_x = split(velocity * (UNIT * mode_x))
            mixed = dot(pair(*split(velocity)), spread_map[...])
            curled = dot(pair(high_y, high_x), curl_map[...]) + dot(pair(low_y, low_x), curl_map[...])
            cosine, sine = turn_yc_c[rows, :], turn_ys_c[rows, :]
            twisted(rows, 0, mixed[:, :LANES], mixed[:, LANES:], cosine, sine)
            twisted(rows, 1, curled[:, LANES:], -curled[:, :LANES], cosine, sine)
        half_products(y_halves, 0, 2, target)

    def to_grid(source, first, fore_high, fore_low, cosine, sine):
        every = pl.ds(0, ROWS)
        for index in range(2):
            high, low = split(source[:, tile(index)])
            inner = dot(pair(high, low), fore_high[...]) + dot(high, fore_low[...])
            real, imag = inner[:, :LANES], inner[:, LANES:]
            stack(every, first + index, real * cosine - imag * sine, real * sine + imag * cosine)
        part = pl.ds(first * LANES, 2 * LANES)
        half_products(x_halves, first, 2, grid_buf.at[:, part])

    def from_grid(value, target, back, cosine, sine):
        high, low = split(value)
        both = dot(xt_high[...], pair(high, low))
        outer = both[:, :LANES] + both[:, LANES:] + dot(xt_low[...], high)
        real, imag = outer[:ROWS], outer[ROWS:]
        high, low = split(pair(real * cosine + imag * sine, imag * cosine - real * sine))
        both = dot(high, back[...])
        target[...] = both[:, :LANES] + both[:, LANES:] + dot(low, back[:, :LANES])

    def grid_coarse(source, target):
        cosine, sine = turn_xc_c[...], turn_xs_c[...]
        to_grid(source, 0, fore_high_c, fore_low_c, cosine, sine)
        speed, spin = grid_buf[:, tile(0)], grid_buf[:, tile(1)]
        crossed = speed * roll(spin, -32) - roll(speed, -32) * spin
        from_grid(crossed, target, back_c, cosine, sine)

    def finish_coarse(source, start_ref, right_ref, target, same_ref, cross_ref, damp_ref):
        even, odd = folded(source[...])
        stack_back(0, even, -turned(odd))
        stack_back(1, turned(even), odd)
        y_back(0, 2)
        for rows in chunks(128):
            value = grid_buf[rows, tile(0)] * turn_yc_c[rows, :] - grid_buf[rows, tile(1)] * turn_ys_c[rows, :]
            modes = dot(pair(*split(value)), finish_map[...])
            term = same_ref[rows, :] * modes[:, :LANES] + cross_ref[rows, :] * modes[:, LANES:]
            target[rows, :] = damp_ref[rows, :] * (start_ref[rows, :] + right_ref[rows, :]) + term

    loads[0].wait()
    coarse_tile(state_ref, 0, 0.5, parcel_send.at[0])
    loads[1].wait()
    loads[2].wait()
    for load in loads[3:]:
        load.start()

    @pl.when(rank == 0)
    def _():
        spread_coarse(parcel_send.at[0], fore_send.at[0], place_f32)

    @pl.when(rank > 0)
    def _():
        pl.semaphore_wait(barrier, 4 * GROUP - 1)

    def greet_last(step, carry):
        signal(ready, (place + step) % GROUP)
        return carry

    @pl.when(jnp.logical_not(near))
    def _():
        lax.fori_loop(0, GROUP, greet_last, 0)

    @pl.when(rank == 0)
    def _():
        pl.semaphore_wait(barrier, 3 * GROUP // 2 - 1)
        post_other(fore_send.at[0], fore_recv.at[0], fore_sent.at[0], fore_got.at[0], DUTY, 0, place)

    def combine(a, carry):
        wave_x = UNIT * (a.astype(F32) * GROUP + place_f32)
        sub = lax.broadcasted_iota(jnp.int32, (8, LANES), 0)
        mode = sub * 128 + lax.broadcasted_iota(jnp.int32, (8, LANES), 1)
        wave_y = UNIT * jnp.where(mode < EDGE // 2, mode, mode - EDGE).astype(F32)
        stiff = VISCOSITY * (wave_x * wave_x + wave_y * wave_y)
        for part in range(2):
            for component in range(3):
                base = pl.multiple_of(a * 24 + (part * 384 + component * 8), 8)
                rows = pl.ds(base, 8)
                states = [state_ref[pl.ds(base + node * 768, 8), :] for node in range(3)]
                terms = [terms_ref[pl.ds(base + node * 768, 8), :] for node in range(3)]
                one = sum(w * s for w, s in zip(STATE_ONE, states))
                two = sum(w * s for w, s in zip(STATE_TWO, states))
                mix_one[rows, :] = one
                mix_two[rows, :] = two
                right_one[rows, :] = sum(w * t for w, t in zip(TERM_ONE, terms)) + stiff * one
                right_two[rows, :] = sum(w * t for w, t in zip(TERM_TWO, terms)) + stiff * two
                start_send[rows, :] = states[2] + HALF_STEP * terms[2]
        return carry

    for index in (3, 4, 5, 6):
        loads[index].wait()
    lax.fori_loop(0, 16, combine, 0, unroll=2)

    following = (rank + 1, at_y, at_pz)

    @pl.when(rank == 0)
    def _():
        pl.semaphore_wait(ready, 5 * GROUP // 2)

    @pl.when(rank < 3)
    def _():
        send_one(start_send, start_recv, start_sems.at[0], start_sems.at[1], following).start()

    coarse_tile(right_one, 0, 0.5, parcel_send.at[1])
    coarse_tile(right_two, 0, 0.5, parcel_send.at[2])
    to_partner(parcel_send, parcel_recv, parcel_sems.at[0], parcel_sems.at[1])
    coarse_tables(spot_f32, keep_same, keep_cross, damp_c)

    def coarse_sweep():
        receive(fore_recv.at[0], fore_got.at[0])
        grid_coarse(fore_recv.at[0], back_send.at[0])
        post_own(back_send.at[0], back_recv.at[0], back_sent.at[0], back_got.at[0], DUTY, duty, spot)
        receive(parcel_recv, parcel_sems.at[1])

        @pl.when(duty == 0)
        def _():
            sweep[0] = parcel_recv[0]

        @pl.when(duty > 0)
        def _():
            receive(hand_recv, hand_sems.at[1])
            sweep[0] = hand_recv[...]

        receive(back_recv.at[0], back_got.at[0])
        tables = (keep_same, keep_cross, damp_c)
        finish_coarse(back_recv.at[0], sweep.at[0], parcel_recv.at[1], sweep.at[1], *tables)
        spread_coarse(sweep.at[1], fore_send.at[1], spot_f32)
        post_own(fore_send.at[1], fore_recv.at[1], fore_sent.at[1], fore_got.at[1], DUTY, duty, spot)
        to_partner(sweep.at[pl.ds(0, 2)], news.at[pl.ds(0, 2)], news_sent.at[0], news_got.at[0])
        receive(fore_recv.at[1], fore_got.at[1])
        grid_coarse(fore_recv.at[1], back_send.at[1])

        @pl.when(duty == 3)
        def _():
            post_other(back_send.at[1], last_recv, back_sent.at[1], back_got.at[2], RANK, 3, spot)

        @pl.when(duty < 3)
        def _():
            post_own(back_send.at[1], back_recv.at[1], back_sent.at[1], back_got.at[1], DUTY, duty, spot)
            receive(back_recv.at[1], back_got.at[1])
            finish_coarse(back_recv.at[1], sweep.at[1], parcel_recv.at[2], sweep.at[2], *tables)
            spread_coarse(sweep.at[2], fore_send.at[2], spot_f32)
            after = duty + 1
            post(fore_send.at[2], fore_recv.at[0], fore_sent.at[2], fore_got.at[0], DUTY, after, spot, GROUP)
            address = (low_z * 2 + after % 2, at_y, (after // 2) * 4 + at_x)
            send_one(sweep.at[2], hand_recv, hand_sems.at[0], hand_sems.at[1], address).start()
            to_partner(sweep.at[2], news.at[2], news_sent.at[1], news_got.at[1])

    coarse_tile(mix_one, 0, 0.5, old_one)
    coarse_tile(mix_two, 0, 0.5, old_two)
    quarter = (lane % 64) // 16
    mode_x = (lane % 16).astype(F32) * GROUP + place_f32
    mode_y = (row + 256 * quarter - jnp.where(quarter >= 2, EDGE, 0)).astype(F32)
    wave_x, wave_y, wave_sq, mask, inverse, damp = wave_tables(EDGE, mode_x, mode_y)
    ky_f[...] = wave_y
    damp_f[...] = damp
    stiff_f[...] = (2.0 * VISCOSITY) * wave_sq
    same_x[...] = wave_y * wave_y * inverse
    same_y[...] = wave_x * wave_x * inverse
    cross_f[...] = -wave_x * wave_y * inverse
    mask_f[...] = mask
    weight = jnp.where(mode_x == 0, 0.5, 1.0)
    cos_f[...] = turn_yc_f[...] * weight
    sin_f[...] = turn_ys_f[...] * weight

    @pl.when(rank == 3)
    def _():
        coarse_tables(place_f32, keep_same_r, keep_cross_r, damp_r)

    def correct_fine(weights, old_ref, target):
        for rows in chunks(128):
            nodes = [news[node, rows, :] for node in range(3)]
            change = sum(w * n for w, n in zip(weights, nodes)) - old_ref[rows, :]
            placed = dot(pair(*split(change)), place_map[...])
            stiff = stiff_f[rows, :]
            for component in range(3):
                part = tile(component)
                lanes = slice(component * LANES, (component + 1) * LANES)
                target[rows, part] = target[rows, part] + stiff * placed[:, lanes]

    def start_fine():
        correct_fine(STATE_ONE, old_one, right_one_f)
        for component in range(3):
            node_f[:, tile(component)] = right_one_f[:, tile(component)] * damp_f[...]

    def fine_field(index, rows):
        x, y, z = (node_f.at[rows, tile(component)] for component in range(3))
        if index < 3:
            return (x, y, z)[index][...]
        ky = ky_f[rows, :]
        kx = UNIT * ((lanes_like(ky) % 16).astype(F32) * GROUP + place_f32)
        if index == 3:
            return ky * z[...]
        if index == 4:
            return -kx * z[...]
        return kx * y[...] - ky * x[...]

    def spread_fine(first):
        for rows in chunks(128):
            cosine, sine = cos_f[rows, :], sin_f[rows, :]
            for index in (first, first + 1):
                mixed = dot(pair(*split(fine_field(index, rows))), spread_map_f[...])
                if index < 3:
                    twisted(rows, index, mixed[:, :LANES], mixed[:, LANES:], cosine, sine)
                else:
                    twisted(rows, index, mixed[:, LANES:], -mixed[:, :LANES], cosine, sine)
        half_products(y_halves, first, 2, fine_send.at[first // 2])

    def give_back(source, component, target, base):
        for half in range(2):
            block_t = source[pl.ds(half * 128, 128), tile(component)].T
            for part in range(2):
                for quarter in range(4):
                    start = base + part * 384 + component * 8 + 2 * quarter + half
                    first = (part * 4 + quarter) * 16
                    target[pl.ds(start, 16, stride=24), :] = block_t[first : first + 16]

    def give_back_coarse(source, base):
        for half in range(2):
            block_t = source[pl.ds(half * 128, 128), :].T
            for part in range(2):
                for component in range(3):
                    for quarter in range(2):
                        start = base + part * 96 + component * 4 + 2 * quarter + half
                        first = part * 64 + component * 16 + quarter * 8
                        coarse_out[pl.ds(start, 8, stride=12), :] = block_t[first : first + 8]

    def cross_fine(component):
        second, third = (component + 1) % 3, (component + 2) % 3
        fields = [grid_buf[:, tile(index)] for index in (second, third, second + 3, third + 3)]
        return fields[0] * fields[3] - fields[1] * fields[2]

    def gather_fine(component):
        even, odd = folded(fine_back_recv[component])
        stack_back(component, even, -turned(odd))
        y_back(component, 1)
        for rows in chunks(128):
            value = grid_buf[rows, tile(component)]
            value = value * turn_yc_f[rows, :] - turned(value) * turn_ys_f[rows, :]
            right_one_f[rows, tile(component)] = dot(pair(*split(value)), finish_map_f[...])

    def finish_fine():
        for rows in chunks(64):
            modes = [right_one_f[rows, tile(component)] for component in range(3)]
            cross = cross_f[rows, :]
            results = [
                same_x[rows, :] * modes[0] + cross * modes[1],
                same_y[rows, :] * modes[1] + cross * modes[0],
                mask_f[rows, :] * modes[2],
            ]
            for component, value in enumerate(results):
                part = tile(component)
                right_one_f[rows, part] = value
                total = node_f[rows, part] + HALF_STEP * value + right_two_f[rows, part]
                node_f[rows, part] = total * damp_f[rows, :]

    def fine_sweep():
        @pl.when(rank == 0)
        def _():
            first = pl.ds(0, 768)
            right_one[...] = right_one[...] + state_ref[first, :] + HALF_STEP * terms_ref[first, :]

        @pl.when(rank > 0)
        def _():
            receive(start_recv, start_sems.at[1])
            right_one[...] = right_one[...] + start_recv[...]

        for component in range(3):
            fine_tile(right_one, component, right_one_f)
            fine_tile(right_two, component, right_two_f)
        receive(news.at[pl.ds(0, 2)], news_got.at[0])

        @pl.when(rank < 3)
        def _():
            receive(news.at[2], news_got.at[1])

        @pl.when(rank == 3)
        def _():
            receive(last_recv, back_got.at[2])
            tables = (keep_same_r, keep_cross_r, damp_r)
            finish_coarse(last_recv, news.at[1], parcel_send.at[2], news.at[2], *tables)

        start_fine()
        for part in range(3):
            spread_fine(2 * part)
            pairs = (fine_send.at[part], fine_recv.at[part], fine_sent.at[part], fine_got.at[part])
            post_own(*pairs, RANK, rank, place)
        correct_fine(STATE_TWO, old_two, right_two_f)
        give_back_coarse(news.at[1], 0)
        give_back_coarse(news.at[2], 192)
        for part in range(3):
            receive(fine_recv.at[part], fine_got.at[part])
            to_grid(fine_recv.at[part], 2 * part, fore_high_f, fore_low_f, turn_xc_f[...], turn_xs_f[...])
        for part in range(3):
            from_grid(cross_fine(part), fine_back_send.at[part], back_f, turn_xc_f[...], turn_xs_f[...])
            pairs = (fine_back_send.at[part], fine_back_recv.at[part])
            post_own(*pairs, fine_back_sent.at[part], fine_back_got.at[part], RANK, rank, place)
        for component in range(3):
            give_back(node_f, component, nodes_out, 0)
        for part in range(3):
            receive(fine_back_recv.at[part], fine_back_got.at[part])
            gather_fine(part)
        finish_fine()
        for component in range(3):
            give_back(right_one_f, component, term_out, 0)
            give_back(node_f, component, nodes_out, 768)

    early = high_z * (1 - low_z)

    def phase(step, carry):
        fine_now = (step + early) % 2

        @pl.when(fine_now == 0)
        def _():
            coarse_sweep()

        @pl.when(fine_now == 1)
        def _():
            fine_sweep()

        return carry

    lax.fori_loop(0, 2, phase, 0)

    @pl.when(rank == 0)
    def _():
        drain_other(fore_send.at[0], fore_sent.at[0])

    drain(fore_send.at[1], fore_sent.at[1], GROUP - 1)
    drain(back_send.at[0], back_sent.at[0], GROUP - 1)
    for part in range(3):
        drain(fine_send.at[part], fine_sent.at[part], GROUP - 1)
        drain(fine_back_send.at[part], fine_back_sent.at[part], GROUP - 1)

    @pl.when(duty == 3)
    def _():
        drain_other(back_send.at[1], back_sent.at[1])

    @pl.when(duty < 3)
    def _():
        drain(back_send.at[1], back_sent.at[1], GROUP - 1)
        drain(fore_send.at[2], fore_sent.at[2], GROUP)
        receive(sweep.at[2], hand_sems.at[0])

    @pl.when(jnp.logical_not(alone))
    def _():
        receive(parcel_send, parcel_sems.at[0])
        receive(sweep.at[pl.ds(0, 2)], news_sent.at[0])

        @pl.when(duty < 3)
        def _():
            receive(sweep.at[2], news_sent.at[1])

    @pl.when(rank < 3)
    def _():
        receive(start_send, start_sems.at[0])


def shards(fine_state, fine_terms):
    matrices, turns = constant_tables()
    full, natural, wide = (ROWS, LANES), (768, LANES), (ROWS, 3 * LANES)
    dma = pltpu.SemaphoreType.DMA
    tiles = (3, ROWS, LANES)
    shapes = [(ROWS, 6 * LANES)]
    shapes += [(3, ROWS, 2 * LANES), (2, ROWS, 2 * LANES), (2, ROWS, LANES), (2, ROWS, LANES), full, full]
    shapes += [tiles] * 4 + [(3, ROWS, 2 * LANES)] * 2 + [tiles] * 2
    shapes += [natural] * 6 + [full] * (9 + 9) + [wide] * 3 + [(2304, LANES)] * 2
    scratch = [pltpu.VMEM((2 * ROWS, 6 * LANES), BF16)] * 2 + [pltpu.VMEM(shape, F32) for shape in shapes]
    scratch += [pltpu.VMEM(matrices.shape, BF16), pltpu.VMEM(turns.shape, F32)]
    scratch += [dma((count,)) for count in (3, 2, 2, 3, 2, 2, 2, 2, 3, 3, 3, 3, 2, 7)]
    scratch += [pltpu.SemaphoreType.REGULAR]
    outs = pl.pallas_call(
        iterate,
        out_shape=(
            jax.ShapeDtypeStruct((1536, LANES), F32),
            jax.ShapeDtypeStruct((768, LANES), F32),
            jax.ShapeDtypeStruct((384, LANES), F32),
        ),
        in_specs=[pl.BlockSpec(memory_space=pltpu.HBM)] * 4,
        out_specs=[pl.BlockSpec(memory_space=pltpu.VMEM)] * 3,
        scratch_shapes=scratch,
        compiler_params=pltpu.CompilerParams(
            collective_id=0, has_side_effects=True, vmem_limit_bytes=52 * 1024 * 1024
        ),
        name="iterate",
    )(fine_state.reshape(2304, LANES), fine_terms.reshape(2304, LANES), jnp.asarray(matrices), jnp.asarray(turns))
    return (
        outs[0].reshape(1, 2, 2, 16, 1, 3, 1, 1024),
        outs[1].reshape(1, 2, 16, 1, 3, 1, 1024),
        outs[2].reshape(1, 2, 2, 8, 1, 3, 1, 512),
    )


def solution(mesh):
    split_over = P("tm", None, None, None, ("py", "pz"), None, None, None)
    return jax.shard_map(
        shards,
        mesh=mesh,
        in_specs=(split_over, split_over),
        out_specs=(
            split_over,
            P("tm", None, None, ("py", "pz"), None, None, None),
            split_over,
        ),
        check_vma=False,
    )
```
